32 devices in a mesh: row: 16 (over z, y, x), col: 2 (over core).
Axes of the slice: x: 2, y: 2, z: 4, core: 2. Of those that a mesh axis runs over, the one named last changes fastest.
Arguments:
- tokens: bfloat16 [8192, 768], P(('row', 'col')), may hold values from -6 to 6
- seg_ids: int32 [32, 256], P(('row', 'col')), may hold values from 0 to 15, never falling along the last dimension, each value on 1 to 128 neighbouring positions
- live_mask: int32 [32, 256], P(('row', 'col')), may hold values from 0 to 1, as said below
- ret_rows: int32 [8192, 16], P(('row', 'col')), may hold values from 0 to 65535, as said below
- enc_store: bfloat16 [65536, 768], P(('row', 'col')), may hold values from -6 to 6
- attn_in: bfloat16 [6, 768, 768], P(None, 'row', 'col'), may hold values from -0.21875 to 0.21875
- attn_out: bfloat16 [2, 768, 768], P(None, 'row', 'col'), may hold values from -0.625 to 0.625
- ff_in: bfloat16 [768, 3072], P('row', 'col'), may hold values from -0.21875 to 0.21875
- ff_out: bfloat16 [3072, 768], P('row', 'col'), may hold values from -0.109375 to 0.109375
- biases: bfloat16 [7, 768], P(None, 'row'), may hold values from -3 to 3
- ln_gain: bfloat16 [3, 768], P(None, 'row'), may hold values from 0.25 to 1.75
- ln_shift: bfloat16 [3, 768], P(None, 'row'), may hold values from -2 to 2
- ff_bias: bfloat16 [3072], P('row'), may hold values from -3 to 3
- cotangent: bfloat16 [8192, 768], P(('row', 'col')), may hold values from -6 to 6
Outputs:
- output: bfloat16 [8192, 768], P(('row', 'col'))
- grad_tokens: float32 [8192, 768], P(('row', 'col'))
- grad_store: float32 [65536, 768], P(('row', 'col'))
- grad_attn_in: float32 [6, 768, 768], P(None, 'row', 'col')
- grad_attn_out: float32 [2, 768, 768], P(None, 'row', 'col')
- grad_ff_in: float32 [768, 3072], P('row', 'col')
- grad_ff_out: float32 [3072, 768], P('row', 'col')
- grad_biases: float32 [7, 768], P(None, 'row')
- grad_ln_gain: float32 [3, 768], P(None, 'row')
- grad_ln_shift: float32 [3, 768], P(None, 'row')
- grad_ff_bias: float32 [3072], P('row')
The draws below stay inside these ranges and needn't reach their ends.
Inputs may be any that keep to these rules, and one draw needn't show every extreme that they name: Shard k is the store rows k * 2048 to (k + 1) * 2048 - 1, and sequence p's rows of ret_rows are its tokens' rows. Of the 4096 entries of one sequence, at most 192 lie in any one shard; exactly 192 lie in each of the same half of the shards for every sequence. `live_mask`: the padding of a sequence, if any, is its last tokens, at most 32 of them.
All inputs are finite; a program needn't handle non-finite values.
Results may differ from the reference program's by a relative error of at most 0.025.
Values may be sent and summed in bfloat16 or wider, within the bound.
No kernel may reach another device: no remote copies, remote signals or barrier semaphores. Data moves between devices by JAX's collectives and lax.ppermute only.
A program may use at most 256 MiB of HBM per device.

```python
import math
import jax
import jax.numpy as jnp
import numpy as np
from jax import lax

D = 768
H = 12
HD = 64
FF = 3072
T_DEV = 256
RET = 16
STORE_DEV = 2048
PACKS = 32
TOKENS = 8192
STORE_ROWS = 65536
CAP = 192
N_ROW = 16
N_COL = 2


def draw_live_mask(key, part):
    pads = jax.random.randint(key, (N_ROW * N_COL, 1), 0, T_DEV // 8 + 1)
    return (jnp.arange(T_DEV, dtype=jnp.int32)[None, :] < T_DEV - pads).astype(jnp.int32)


def draw_ret_rows(key, part):
    peers = N_ROW * N_COL
    per_seq = T_DEV * RET
    mean_load = per_seq // peers
    key_hot, key_rest = jax.random.split(jax.random.fold_in(key, 17))
    hot_rank = jax.random.permutation(key_hot, peers)
    is_hot = hot_rank < peers // 2
    cold_rank = jnp.cumsum(jnp.where(is_hot, 0, 1).astype(jnp.int32)) - 1

    def one_seq(seq_key):
        key_pair, key_shift, key_perm, key_rows = jax.random.split(seq_key, 4)
        cold_perm = jax.random.permutation(key_pair, peers // 2)
        paired = cold_perm[jnp.clip(cold_rank, 0, peers // 2 - 1)]
        shifts = jax.random.randint(key_shift, (peers // 4,), 0, mean_load // 2 + 1)
        signed = jnp.where(paired % 2 == 0, shifts[paired // 2], -shifts[paired // 2])
        loads = jnp.where(is_hot, CAP, mean_load // 2 + signed).astype(jnp.int32)
        ends = jnp.cumsum(loads)
        sorted_owner = jnp.searchsorted(ends, jnp.arange(per_seq, dtype=jnp.int32), side='right').astype(jnp.int32)
        owners = sorted_owner[jax.random.permutation(key_perm, per_seq)]
        inner = jax.random.randint(key_rows, (per_seq,), 0, STORE_DEV)
        return owners * STORE_DEV + inner
    every = jax.vmap(one_seq)(jax.random.split(key_rest, peers))
    return every.reshape(TOKENS, RET).astype(jnp.int32)


def spiked(values, key, source, target, blocks, factor):
    def block_of(dim):
        return (jnp.arange(values.shape[dim]) // (values.shape[dim] // blocks)).reshape((-1,) + (1,) * (values.ndim - 1 - dim))

    one_side = jax.random.permutation(key, blocks)[block_of(target)]
    other_side = (block_of(target) + blocks // 2) % blocks
    return jnp.where((block_of(source) == one_side) | (block_of(source) == other_side), factor * values, values)


def levels(key, dims, cuts, low, high):
    def one(axis_at, blocks):
        steps = jax.random.uniform(jax.random.fold_in(jax.random.fold_in(key, 6), axis_at), (blocks,), jnp.float32, low / len(cuts), high / len(cuts))
        return jnp.repeat(jnp.exp(steps), dims[axis_at] // blocks).reshape((-1,) + (1,) * (len(dims) - axis_at - 1))

    level = one(*cuts[0])
    for cut in cuts[1:]:
        level = level * one(*cut)
    return level


def profile(number_of, total, most, skew):
    weights = [(1 << 20) // math.isqrt(grade ** skew) + 1 for grade in range(2, number_of + 1)]
    surplus, holding = total - most - (number_of - 1), [1] * (number_of - 1)
    while surplus > 0:
        candidates = [i for i in range(number_of - 1) if holding[i] < most]
        mass, remaining = sum([weights[i] for i in candidates]), surplus
        for i in candidates:
            addition = min(most - holding[i], max(1, remaining * weights[i] // mass), surplus)
            holding[i] = holding[i] + addition
            surplus = surplus - addition
    return np.array([most] + holding)


def uneven_parts(rng, amount, total, most, slope):
    if amount == 2:
        one = jax.random.randint(rng, (), max(1, total - most), min(most, total - 1) + 1)
        return jnp.stack([one, total - one])
    tallies = jnp.asarray(profile(amount, total, most, slope), jnp.int32)
    twos = (amount - 1) // 2
    giver, receiver = tallies[1:1 + 2 * twos:2], tallies[2:2 + 2 * twos:2]
    margin = jnp.minimum(giver - 1, most - receiver)
    moved = jax.random.randint(jax.random.fold_in(rng, 1), (twos,), 0, 1 << 20) % (margin + 1)
    tallies = tallies.at[1:1 + 2 * twos:2].set(giver - moved).at[2:2 + 2 * twos:2].set(receiver + moved)
    return tallies[jax.random.permutation(jax.random.fold_in(rng, 2), amount)]


def gaussian(key, dims, width, bound, cuts=(), held_as=jnp.bfloat16):
    values = width * jax.random.normal(key, dims, jnp.float32)
    if cuts:
        values = values * levels(key, dims, cuts, -0.22, 0.18)
    return jnp.clip(values, -bound, bound).astype(held_as)


def noise_with(key, extent, scale, bound, cuts, heavy, held_as=jnp.bfloat16):
    values = scale * jax.random.normal(key, extent, jnp.float32)
    if cuts:
        values = values * levels(key, extent, cuts, -0.22, 0.18)
    return jnp.clip(spiked(values, jax.random.fold_in(key, 3), *heavy), -bound, bound).astype(held_as)


def setup_inputs(seed: int = 0) -> dict:
    key_list = jax.random.split(jax.random.key(seed), 15)
    tokens = noise_with(key_list[0], (TOKENS, D), 1.0, 6.0, ((0, 32),), (0, 1, 32, 2.75))
    seg_ids = jax.vmap(lambda own: jnp.searchsorted(jnp.cumsum(uneven_parts(own, T_DEV // 16, T_DEV, T_DEV // 2, 2)), jnp.arange(T_DEV), side="right"))(jax.random.split(key_list[1], PACKS)).reshape((PACKS, T_DEV)).astype(jnp.int32)
    live_mask = draw_live_mask(jax.random.fold_in(key_list[14], 71), 0)
    ret_rows = draw_ret_rows(jax.random.fold_in(key_list[14], 71), 0)
    enc_store = gaussian(key_list[4], (STORE_ROWS, D), 1.0, 6.0, ((0, 32),))
    attn_in = gaussian(key_list[5], (6, D, D), D ** -0.5, 0.21875, ((1, 16), (2, 2)))
    attn_out = gaussian(key_list[6], (2, D, D), (D // 8) ** -0.5, 0.625, ((1, 16), (2, 2)))
    ff_in = gaussian(key_list[7], (D, FF), D ** -0.5, 0.21875, ((0, 16), (1, 2)))
    ff_out = gaussian(key_list[8], (FF, D), FF ** -0.5, 0.109375, ((0, 16), (1, 2)))
    biases = gaussian(key_list[9], (7, D), 0.5, 3.0, ((1, 16),))
    ln_gain = jnp.clip(1.0 + 0.15 * jax.random.normal(key_list[10], (3, D), jnp.float32), 0.25, 1.75).astype(jnp.bfloat16)
    ln_shift = gaussian(key_list[11], (3, D), 0.3, 2.0, ((1, 16),))
    ff_bias = gaussian(key_list[12], (FF,), 0.5, 3.0, ((0, 16),))
    cotangent = gaussian(key_list[13], (TOKENS, D), 1.0, 6.0, ((0, 32),))
    return {"tokens": tokens, "seg_ids": seg_ids, "live_mask": live_mask, "ret_rows": ret_rows, "enc_store": enc_store, "attn_in": attn_in, "attn_out": attn_out, "ff_in": ff_in, "ff_out": ff_out, "biases": biases, "ln_gain": ln_gain, "ln_shift": ln_shift, "ff_bias": ff_bias, "cotangent": cotangent}


@jax.custom_vjp
def low(v):
    return lax.optimization_barrier(v.astype(jnp.bfloat16)).astype(jnp.float32)

@jax.custom_vjp
def low_back(v):
    return v

def low_keep(v):
    return (low(v), None)

def low_pass(kept, grad):
    return (grad,)

def back_keep(v):
    return (v, None)

def back_low(kept, grad):
    return (low(grad),)
low.defvjp(low_keep, low_pass)
low_back.defvjp(back_keep, back_low)

def round_both(value):
    return low_back(low(value))

def matmul(left, right):
    return jnp.dot(left, right, precision=lax.Precision.HIGHEST)

def norm_layer(resid, gain, shift):
    row_mean = lax.optimization_barrier(jnp.mean(resid, axis=-1, keepdims=True))
    centered = resid - row_mean
    row_var = lax.optimization_barrier(jnp.mean(centered * centered, axis=-1, keepdims=True))
    return centered * lax.rsqrt(row_var + 1e-05) * gain + shift

def self_attention(queries, key_rows, values, seg_row, live_row):
    total = queries.shape[0]
    block_rows = min(512, total)
    key_pos = jnp.arange(total, dtype=jnp.int32)

    def one_block(row_start):
        query_blk = lax.dynamic_slice_in_dim(queries, row_start, block_rows, 0)
        query_pos = row_start + jnp.arange(block_rows, dtype=jnp.int32)
        seg_query = lax.dynamic_slice_in_dim(seg_row, row_start, block_rows, 0)
        visible = (key_pos[None, :] <= query_pos[:, None]) & (seg_query[:, None] == seg_row[None, :]) & ((live_row[None, :] == 1) | (key_pos[None, :] == query_pos[:, None]))
        scores = low_back(jnp.einsum('qhd,khd->hqk', query_blk, key_rows, precision=lax.Precision.HIGHEST) * 0.125)
        scores = jnp.where(visible[None], scores, -1e+30)
        probs = low(jax.nn.softmax(scores, axis=-1))
        return jnp.einsum('hqk,khd->qhd', probs, values, precision=lax.Precision.HIGHEST)
    starts = jnp.arange(total // block_rows, dtype=jnp.int32) * block_rows
    blocks = lax.map(jax.checkpoint(one_block), starts)
    return blocks.reshape(total, H * HD)

def decoder_layer(seq_in, enc_store, attn_in, attn_out, ff_in, ff_out, biases, ln_gain, ln_shift, ff_bias, seg_row, live_row, rows_ret):
    total = seq_in.shape[0]
    queries = round_both(matmul(seq_in, attn_in[0]) + biases[0]).reshape(total, H, HD)
    key_rows = round_both(matmul(seq_in, attn_in[1])).reshape(total, H, HD)
    values = round_both(matmul(seq_in, attn_in[2]) + biases[1]).reshape(total, H, HD)
    mixed = round_both(self_attention(queries, key_rows, values, seg_row, live_row))
    branch = low_back(matmul(mixed, attn_out[0]) + biases[2])
    first = norm_layer(seq_in + branch, ln_gain[0], ln_shift[0])
    cross_q = round_both(matmul(low(first), attn_in[3]) + biases[3]).reshape(total, H, HD)
    query_keys = round_both(jnp.einsum('the,dhe->thd', cross_q, attn_in[4].reshape(D, H, HD), precision=lax.Precision.HIGHEST))
    fetched = enc_store[rows_ret.reshape(-1)].reshape(total, RET, D)
    cross_s = low_back(jnp.einsum('thd,trd->thr', query_keys, fetched, precision=lax.Precision.HIGHEST) * 0.125)
    cross_p = low(jax.nn.softmax(cross_s, axis=-1))
    state_mix = round_both(jnp.einsum('thr,trd->thd', cross_p, fetched, precision=lax.Precision.HIGHEST))
    cross_heads = jnp.einsum('thd,dhe->the', state_mix, attn_in[5].reshape(D, H, HD), precision=lax.Precision.HIGHEST) + biases[4].reshape(H, HD)
    cross_mix = round_both(cross_heads.reshape(total, D))
    branch_two = low_back(matmul(cross_mix, attn_out[1]) + biases[5])
    second = norm_layer(first + branch_two, ln_gain[1], ln_shift[1])
    hidden_pre = low_back(matmul(low(second), ff_in) + ff_bias)
    hidden = low(jax.nn.gelu(hidden_pre, approximate=False))
    branch_ffn = low_back(matmul(hidden, ff_out) + biases[6])
    return norm_layer(second + branch_ffn, ln_gain[2], ln_shift[2])

def reference(tokens, seg_ids, live_mask, ret_rows, enc_store, attn_in, attn_out, ff_in, ff_out, biases, ln_gain, ln_shift, ff_bias, cotangent):
    packs = N_ROW * N_COL
    params = tuple((array.astype(jnp.float32) for array in (enc_store, attn_in, attn_out, ff_in, ff_out, biases, ln_gain, ln_shift, ff_bias)))
    inputs = (tokens.astype(jnp.float32).reshape(packs, T_DEV, D), cotangent.astype(jnp.float32).reshape(packs, T_DEV, D), seg_ids, live_mask, ret_rows.reshape(packs, T_DEV, RET))

    def scan_step(totals, pack_in):
        seq_tokens, seq_cot, seg_row, live_row, rows_ret = pack_in

        def forward(seq_in, *weights):
            return decoder_layer(seq_in, *weights, seg_row, live_row, rows_ret)
        result, pull_back = jax.vjp(forward, seq_tokens, *params)
        grad_list = pull_back(seq_cot)
        totals = tuple((acc_sum + new_sum for acc_sum, new_sum in zip(totals, grad_list[1:])))
        return (totals, (result.astype(jnp.bfloat16), grad_list[0]))
    zero_sums = tuple((jnp.zeros_like(param) for param in params))
    totals, (outputs, grad_tokens) = lax.scan(scan_step, zero_sums, inputs)
    return (outputs.reshape(TOKENS, D), grad_tokens.reshape(TOKENS, D), totals[0], totals[1], totals[2], totals[3], totals[4], totals[5], totals[6], totals[7], totals[8])
```

```python
import functools

import jax
import jax.numpy as jnp
import numpy as np
from jax import lax
from jax.experimental import pallas as pl
from jax.experimental.pallas import tpu as pltpu
from jax.sharding import PartitionSpec as P

H = 12
HD = 64
RANKS = ("row", "col")
BF = jnp.bfloat16
F32 = jnp.float32
VMEM_LIMIT = 60 * 1024 * 1024


def mm(a, b):
    return jnp.dot(a, b, preferred_element_type=F32)


def mm_nt(a, b):
    return lax.dot_general(a, b, (((1,), (1,)), ((), ())), preferred_element_type=F32)


def mm_tn(a, b):
    return lax.dot_general(a, b, (((0,), (0,)), ((), ())), preferred_element_type=F32)


def norm_fwd(resid, gain, shift):
    row_mean = jnp.mean(resid, axis=-1, keepdims=True)
    centered = resid - row_mean
    inv_std = lax.rsqrt(jnp.mean(centered * centered, axis=-1, keepdims=True) + 1e-05)
    normed = centered * inv_std
    return (normed * gain + shift, normed, inv_std)


def norm_back(grad_in, normed, inv_std, gain):
    scaled = grad_in * gain
    return inv_std * (
        scaled
        - jnp.mean(scaled, axis=-1, keepdims=True)
        - normed * jnp.mean(scaled * normed, axis=-1, keepdims=True)
    )


def gelu_parts(pre_act):
    cdf_part = 0.5 * (1.0 + lax.erf(pre_act * 0.7071067811865476))
    density = jnp.exp(-0.5 * pre_act * pre_act) * 0.3989422804014327
    return (pre_act * cdf_part, cdf_part + pre_act * density)


def visible_mask(seg_row, live_row):
    pos = jnp.arange(seg_row.shape[0], dtype=jnp.int32)
    return (
        (pos[None, :] <= pos[:, None])
        & (seg_row[:, None] == seg_row[None, :])
        & ((live_row[None, :] == 1) | (pos[None, :] == pos[:, None]))
    )


def column_sum(array):
    return jnp.sum(array.astype(F32), axis=0)


def bit_orders(n_rows, n_cols):
    row_bits = [("row", 1 << b) for b in reversed(range(n_rows.bit_length() - 1))]
    col_bits = [("col", 1 << b) for b in reversed(range(n_cols.bit_length() - 1))]
    swapped = row_bits[:-2] + row_bits[-1:] + row_bits[-2:-1]
    return row_bits + col_bits, swapped + col_bits


def swap_bit(array, axis, bit):
    pairs = [(i, i ^ bit) for i in range(lax.axis_size(axis))]
    return lax.ppermute(array, axis, pairs)


def gather_bits(blocks, order):
    for axis, bit in order:
        blocks = jnp.concatenate([blocks, swap_bit(blocks, axis, bit)], axis=0)
    return blocks


def scatter_bits(blocks, order):
    for axis, bit in order:
        half = blocks.shape[0] // 2
        blocks = blocks[:half] + swap_bit(blocks[half:], axis, bit)
    return blocks[0]


def offsets(order, first_is_low):
    count = len(order)
    rows = np.zeros(1 << count, np.int32)
    cols = np.zeros(1 << count, np.int32)
    for k, (axis, bit) in enumerate(order):
        place = k if first_is_low else count - 1 - k
        has = (np.arange(1 << count) >> place) & 1
        (rows if axis == "row" else cols)[has == 1] ^= bit
    return rows, cols


def block_of_device(order, n_rows, n_cols):
    rows, cols = offsets(order, True)
    table = np.zeros((n_rows, n_cols), np.int32)
    table[rows, cols] = np.arange(n_rows * n_cols)
    at_row = lax.axis_index("row") ^ jnp.arange(n_rows, dtype=jnp.int32)
    at_col = lax.axis_index("col") ^ jnp.arange(n_cols, dtype=jnp.int32)
    return jnp.asarray(table)[at_row[:, None], at_col[None, :]].reshape(-1)


def device_of_block(order, n_cols):
    rows, cols = offsets(order, False)
    to_row = lax.axis_index("row") ^ jnp.asarray(rows)
    to_col = lax.axis_index("col") ^ jnp.asarray(cols)
    return to_row * n_cols + to_col


def flip_by_position(blocks, stages):
    for k, (axis, bit) in enumerate(stages):
        here = (lax.axis_index(axis) & bit) != 0
        blocks = jnp.where(here, jnp.flip(blocks, axis=k), blocks)
    return blocks


def by_device(blocks, order):
    stages = order[::-1]
    shape = blocks.shape[1:]
    blocks = flip_by_position(blocks.reshape((2,) * len(stages) + shape), stages)
    rank = sorted(range(len(stages)), key=lambda k: (stages[k][0] == "col", -stages[k][1]))
    rest = list(range(len(stages), blocks.ndim))
    return blocks.transpose(rank + rest).reshape((-1,) + shape)


def by_stage(blocks, stages):
    shape = blocks.shape[1:]
    rank = sorted(range(len(stages)), key=lambda k: (stages[k][0] == "col", -stages[k][1]))
    rest = list(range(len(stages), len(stages) + len(shape)))
    back = [rank.index(k) for k in range(len(stages))]
    blocks = blocks.reshape((2,) * len(stages) + shape).transpose(back + rest)
    return flip_by_position(blocks, stages).reshape((-1,) + shape)


def split_cols(array, pieces):
    width = array.shape[1] // pieces
    return jnp.concatenate([array[:, i * width : (i + 1) * width] for i in range(pieces)], axis=0)


def unpack_attn_kernel(perm, blk, w_in, w_out, small, *, rb):
    for k in range(6):
        w_in[k] = blk[0, k * rb : (k + 1) * rb]
    for k in range(2):
        w_out[k] = blk[0, (6 + k) * rb : (7 + k) * rb]
    small[0] = blk[0, 8 * rb :]


def unpack_ff_kernel(perm, blk, ff_in, ff_out, *, rb, cb):
    for k in range(4):
        ff_in[:, k * cb : (k + 1) * cb] = blk[0, k * rb : (k + 1) * rb]
    ff_out[...] = blk[0, 4 * rb :]


def pack_attn_kernel(dest, *refs, rb):
    parts, small, blk = refs[:8], refs[8], refs[9]
    for k in range(8):
        blk[0, k * rb : (k + 1) * rb] = parts[k][...]
    blk[0, 8 * rb :] = small[0]


def pack_ff_kernel(dest, ff_in, ff_out, blk, *, rb, cb):
    for k in range(4):
        blk[0, k * rb : (k + 1) * rb] = ff_in[:, k * cb : (k + 1) * cb]
    blk[0, 4 * rb :] = ff_out[...]


def unpack(attn_blocks, ff_blocks, order_a, order_b, n_rows, n_cols, rb, cb):
    dim, wide = rb * n_rows, 4 * rb * n_rows
    extra = attn_blocks.shape[1] - 8 * rb
    shapes_a = (
        jax.ShapeDtypeStruct((6, dim, dim), BF),
        jax.ShapeDtypeStruct((2, dim, dim), BF),
        jax.ShapeDtypeStruct((n_rows * n_cols, extra, cb), BF),
    )
    shapes_b = (jax.ShapeDtypeStruct((dim, wide), BF), jax.ShapeDtypeStruct((wide, dim), BF))
    if rb % 16 or cb % 128:
        got = by_device(attn_blocks, order_a).reshape(n_rows, n_cols, -1, cb)
        mats = got[:, :, : 8 * rb].reshape(n_rows, n_cols, 8, rb, cb)
        mats = mats.transpose(2, 0, 3, 1, 4).reshape(8, dim, dim)
        small = got[:, :, 8 * rb :].reshape(n_rows * n_cols, extra, cb)
        got = by_device(ff_blocks, order_b).reshape(n_rows, n_cols, 8, rb, cb)
        ff_in = got[:, :, :4].transpose(0, 3, 1, 2, 4).reshape(dim, wide)
        ff_out = got[:, :, 4:].transpose(0, 2, 3, 1, 4).reshape(wide, dim)
        return mats[:6], mats[6:], small, ff_in, ff_out
    at = lambda g, perm: (0, g // n_cols, g % n_cols)
    w_in, w_out, small = pl.pallas_call(
        functools.partial(unpack_attn_kernel, rb=rb),
        grid_spec=pltpu.PrefetchScalarGridSpec(
            num_scalar_prefetch=1,
            grid=(n_rows * n_cols,),
            in_specs=[pl.BlockSpec((1, 8 * rb + extra, cb), lambda g, perm: (perm[g], 0, 0))],
            out_specs=[
                pl.BlockSpec((6, rb, cb), at),
                pl.BlockSpec((2, rb, cb), at),
                pl.BlockSpec((1, extra, cb), lambda g, perm: (g, 0, 0)),
            ],
        ),
        out_shape=shapes_a,
        name="unpack_attn",
    )(block_of_device(order_a, n_rows, n_cols), attn_blocks)
    at = lambda g, perm: (g // n_cols, g % n_cols)
    ff_in, ff_out = pl.pallas_call(
        functools.partial(unpack_ff_kernel, rb=rb, cb=cb),
        grid_spec=pltpu.PrefetchScalarGridSpec(
            num_scalar_prefetch=1,
            grid=(n_rows * n_cols,),
            in_specs=[pl.BlockSpec((1, 8 * rb, cb), lambda g, perm: (perm[g], 0, 0))],
            out_specs=[pl.BlockSpec((rb, 4 * cb), at), pl.BlockSpec((4 * rb, cb), at)],
        ),
        out_shape=shapes_b,
        name="unpack_ff",
    )(block_of_device(order_b, n_rows, n_cols), ff_blocks)
    return w_in, w_out, small, ff_in, ff_out


def pack_attn(mats, small, order, n_rows, n_cols, rb, cb):
    peers, extra = n_rows * n_cols, small.shape[1]
    if rb % 16 or cb % 128:
        got = jnp.stack(mats).reshape(8, n_rows, rb, n_cols, cb).transpose(1, 3, 0, 2, 4)
        got = got.reshape(n_rows, n_cols, 8 * rb, cb)
        low = jnp.broadcast_to(small[:, None], (n_rows, n_cols, extra, cb))
        got = jnp.concatenate([got, low], axis=2).reshape(peers, 8 * rb + extra, cb)
        return by_stage(got, order)
    at = lambda g, dest: (dest[g] // n_cols, dest[g] % n_cols)
    return pl.pallas_call(
        functools.partial(pack_attn_kernel, rb=rb),
        grid_spec=pltpu.PrefetchScalarGridSpec(
            num_scalar_prefetch=1,
            grid=(peers,),
            in_specs=[pl.BlockSpec((rb, cb), at)] * 8
            + [pl.BlockSpec((1, extra, cb), lambda g, dest: (dest[g] // n_cols, 0, 0))],
            out_specs=pl.BlockSpec((1, 8 * rb + extra, cb), lambda g, dest: (g, 0, 0)),
        ),
        out_shape=jax.ShapeDtypeStruct((peers, 8 * rb + extra, cb), BF),
        name="pack_attn",
    )(device_of_block(order, n_cols), *mats, small)


def pack_ff(ff_in, ff_out, order, n_rows, n_cols, rb, cb):
    peers = n_rows * n_cols
    if rb % 16 or cb % 128:
        first = ff_in.reshape(n_rows, rb, n_cols, 4, cb).transpose(0, 2, 3, 1, 4)
        second = ff_out.reshape(n_rows, 4, rb, n_cols, cb).transpose(0, 3, 1, 2, 4)
        got = jnp.concatenate([first, second], axis=2)
        return by_stage(got.reshape(peers, 8 * rb, cb), order)
    at = lambda g, dest: (dest[g] // n_cols, dest[g] % n_cols)
    return pl.pallas_call(
        functools.partial(pack_ff_kernel, rb=rb, cb=cb),
        grid_spec=pltpu.PrefetchScalarGridSpec(
            num_scalar_prefetch=1,
            grid=(peers,),
            in_specs=[pl.BlockSpec((rb, 4 * cb), at), pl.BlockSpec((4 * rb, cb), at)],
            out_specs=pl.BlockSpec((1, 8 * rb, cb), lambda g, dest: (g, 0, 0)),
        ),
        out_shape=jax.ShapeDtypeStruct((peers, 8 * rb, cb), BF),
        name="pack_ff",
    )(device_of_block(order, n_cols), ff_in, ff_out)


def plan_requests(ret_rows, shard_rows, peers, slots):
    flat = ret_rows.reshape(-1)
    count = flat.shape[0]
    owner = flat // shard_rows
    local_row = flat - owner * shard_rows
    mine = owner[:, None] == jnp.arange(peers, dtype=jnp.int32)[None, :]
    run = 256
    runs = count // run
    ones = mine.astype(BF).reshape(runs, run, peers)
    lower = jnp.tril(jnp.ones((run, run), BF))
    within = jnp.einsum("ij,bjo->bio", lower, ones, preferred_element_type=F32)
    totals = within[:, -1, :]
    before = jnp.cumsum(totals, axis=0) - totals
    upto = (within + before[:, None, :]).reshape(count, peers)
    rank = jnp.sum(jnp.where(mine, upto, 0.0), axis=1).astype(jnp.int32) - 1
    place = owner * slots + rank
    row_code = local_row + 1
    entry_code = jnp.arange(count, dtype=jnp.int32)
    digits = jnp.stack([row_code // 64, row_code % 64, entry_code // 64, entry_code % 64])
    left = jnp.where(mine.T[None], digits[:, None, :], 0).astype(BF)
    at_rank = (rank[:, None] == jnp.arange(slots, dtype=jnp.int32)[None, :]).astype(BF)
    codes = mm(left.reshape(4 * peers, count), at_rank).astype(jnp.int32).reshape(4, peers, slots)
    return place, codes[0] * 64 + codes[1], codes[2] * 64 + codes[3]


def own_rows(tokens, ret, heads):
    shape = (heads * tokens, tokens * ret)
    row_tok = lax.broadcasted_iota(jnp.int32, shape, 0) % tokens
    col_tok = lax.broadcasted_iota(jnp.int32, shape, 1) // ret
    return row_tok == col_tok


def cross_fwd_kernel(qk, fetched, mix, probs, *, ret):
    heads, tokens, dim = qk.shape
    own = own_rows(tokens, ret, heads)
    query = qk[...].reshape(heads * tokens, dim)
    rows = fetched[...]
    scores = jnp.where(own, mm_nt(query, rows) * 0.125, -1e30)
    expo = jnp.exp(scores - jnp.max(scores, axis=-1, keepdims=True))
    prob = expo / jnp.sum(expo, axis=-1, keepdims=True)
    probs[0] = prob
    mix[...] = mm(prob.astype(BF), rows).astype(BF).reshape(heads, tokens, dim)


def cross_bwd_kernel(qk, gmix, fetched, probs, grad_rows, grad_s, *, ret):
    heads, tokens, dim = qk.shape
    query = qk[...].reshape(heads * tokens, dim)
    grad_mix = gmix[...].reshape(heads * tokens, dim)
    prob = probs[0]
    grad_p = mm_nt(grad_mix, fetched[...])
    g_s = (prob * (grad_p - jnp.sum(prob * grad_p, axis=-1, keepdims=True))).astype(BF)
    grad_s[0] = g_s
    grad_rows[...] = (
        mm_tn(prob.astype(BF), grad_mix) + mm_tn(g_s, query) * 0.125
    ).astype(BF)


def cross_back_q_kernel(grad_s, fetched, grad_qk):
    heads, tokens, dim = grad_qk.shape
    got = mm(grad_s[0], fetched[...]) * 0.125
    grad_qk[...] = got.astype(BF).reshape(heads, tokens, dim)


def cross_calls(tok_count, ret, dim):
    tb = 16
    blocks = tok_count // tb
    by_head = pl.BlockSpec((H, tb, dim), lambda g: (0, g, 0))
    rows = pl.BlockSpec((tb * ret, dim), lambda g: (g, 0))
    square = pl.BlockSpec((1, H * tb, tb * ret), lambda g: (g, 0, 0))
    heads_shape = jax.ShapeDtypeStruct((H, tok_count, dim), BF)
    square_f32 = jax.ShapeDtypeStruct((blocks, H * tb, tb * ret), F32)
    square_bf = jax.ShapeDtypeStruct((blocks, H * tb, tb * ret), BF)
    params = pltpu.CompilerParams(vmem_limit_bytes=VMEM_LIMIT)
    fwd = pl.pallas_call(
        functools.partial(cross_fwd_kernel, ret=ret),
        grid=(blocks,),
        in_specs=[by_head, rows],
        out_specs=[by_head, square],
        out_shape=(heads_shape, square_f32),
        compiler_params=params,
        name="cross_fwd",
    )
    bwd = pl.pallas_call(
        functools.partial(cross_bwd_kernel, ret=ret),
        grid=(blocks,),
        in_specs=[by_head, by_head, rows, square],
        out_specs=[rows, square],
        out_shape=(jax.ShapeDtypeStruct((tok_count * ret, dim), BF), square_bf),
        compiler_params=params,
        name="cross_bwd",
    )
    back_q = pl.pallas_call(
        cross_back_q_kernel,
        grid=(blocks,),
        in_specs=[square, rows],
        out_specs=by_head,
        out_shape=heads_shape,
        compiler_params=params,
        name="cross_back_q",
    )
    return fwd, bwd, back_q


def store_sum_kernel(asked, returned, total, *, block):
    first = pl.program_id(0) * block + 1
    shape = (block, asked.shape[1])
    hit = lax.broadcasted_iota(jnp.int32, shape, 0) + first == asked[...]
    total[...] = mm(hit.astype(BF), returned[...])


def store_sum(asked, returned, shard_rows):
    count, dim = returned.shape
    block = 256
    return pl.pallas_call(
        functools.partial(store_sum_kernel, block=block),
        grid=(shard_rows // block,),
        in_specs=[
            pl.BlockSpec((1, count), lambda g: (0, 0)),
            pl.BlockSpec((count, dim), lambda g: (0, 0)),
        ],
        out_specs=pl.BlockSpec((block, dim), lambda g: (g, 0)),
        out_shape=jax.ShapeDtypeStruct((shard_rows, dim), F32),
        compiler_params=pltpu.CompilerParams(vmem_limit_bytes=VMEM_LIMIT),
        name="store_sum",
    )(asked.reshape(1, count), returned)


def all_to_all(array):
    return lax.all_to_all(array, RANKS, split_axis=0, concat_axis=0, tiled=True)


def on_device(
    tokens,
    seg_ids,
    live_mask,
    ret_rows,
    enc_store,
    attn_in,
    attn_out,
    ff_in,
    ff_out,
    biases,
    ln_gain,
    ln_shift,
    ff_bias,
    cotangent,
):
    n_rows = lax.axis_size("row")
    n_cols = lax.axis_size("col")
    peers = n_rows * n_cols
    tok_count, dim = tokens.shape
    shard_rows = enc_store.shape[0]
    ret = ret_rows.shape[1]
    slots = 3 * ret_rows.size // (2 * peers)
    rb, cb = attn_in.shape[1], attn_in.shape[2]
    order_a, order_b = bit_orders(n_rows, n_cols)
    far = n_rows.bit_length() - 3

    small_parts = (biases, ln_gain, ln_shift, ff_bias)
    small = jnp.concatenate([part.reshape(-1) for part in small_parts])
    small_rows = -(-small.size // (16 * cb)) * 16
    small = jnp.pad(small, (0, small_rows * cb - small.size)).reshape(small_rows, cb)
    pack_a = jnp.concatenate([attn_in.reshape(-1, cb), attn_out.reshape(-1, cb), small], axis=0)
    pack_b = jnp.concatenate([split_cols(ff_in, 4), ff_out], axis=0)
    part_a = gather_bits(pack_a[None], order_a[:far])
    part_b = gather_bits(pack_b[None], order_b[:far])

    place, wanted, entry = plan_requests(ret_rows, shard_rows, peers, slots)
    asked = all_to_all(wanted)
    answer = enc_store[jnp.maximum(asked - 1, 0)]
    answer, part_a, part_b = lax.optimization_barrier((answer, part_a, part_b))
    arrived = all_to_all(answer)
    part_a = gather_bits(part_a, order_a[far:])
    part_b = gather_bits(part_b, order_b[far:])
    w_in, w_out, small_all, w_ff1, w_ff2 = unpack(
        part_a,
        part_b,
        order_a,
        order_b,
        n_rows,
        n_cols,
        rb,
        cb,
    )
    small_all = small_all.reshape(n_rows, n_cols, -1)[:, 0, : sum(p.size for p in small_parts)]
    small_all = small_all.astype(F32)
    row_block = dim // n_rows
    vectors = small_all[:, : 13 * row_block].reshape(n_rows, 13, row_block)
    vectors = vectors.transpose(1, 0, 2).reshape(13, dim)
    bias_all, gain_all, shift_all = vectors[:7], vectors[7:10], vectors[10:]
    bias_ff = small_all[:, 13 * row_block :].reshape(-1)

    def heads(array):
        return array.reshape(tok_count, H, HD)

    queries = heads((mm(tokens, w_in[0]) + bias_all[0]).astype(BF))
    key_rows = heads(mm(tokens, w_in[1]).astype(BF))
    values = heads((mm(tokens, w_in[2]) + bias_all[1]).astype(BF))
    visible = visible_mask(seg_ids[0], live_mask[0])
    scores = jnp.einsum("qhd,khd->hqk", queries, key_rows, preferred_element_type=F32) * 0.125
    probs = jax.nn.softmax(jnp.where(visible[None], scores, -1e30), axis=-1)
    probs_low = probs.astype(BF)
    mixed = jnp.einsum("hqk,khd->qhd", probs_low, values, preferred_element_type=F32)
    mixed = mixed.reshape(tok_count, dim).astype(BF)
    branch = mm(mixed, w_out[0]) + bias_all[2]
    first, first_norm, first_scale = norm_fwd(
        tokens.astype(F32) + branch, gain_all[0], shift_all[0]
    )
    first_low = first.astype(BF)
    cross_q = (mm(first_low, w_in[3]) + bias_all[3]).astype(BF)

    key_heads = w_in[4].reshape(dim, H, HD)
    val_heads = w_in[5].reshape(dim, H, HD)
    query_keys = jnp.einsum(
        "the,dhe->htd", heads(cross_q), key_heads, preferred_element_type=F32
    ).astype(BF)
    cross_fwd, cross_bwd, cross_back_q = cross_calls(tok_count, ret, dim)
    fetched = arrived.reshape(peers * slots, dim)[place]
    state_mix, cross_p = cross_fwd(query_keys, fetched)
    cross_mix = jnp.einsum("htd,dhe->the", state_mix, val_heads, preferred_element_type=F32)
    cross_low = (cross_mix.reshape(tok_count, dim) + bias_all[4]).astype(BF)
    branch_two = mm(cross_low, w_out[1]) + bias_all[5]
    second, second_norm, second_scale = norm_fwd(first + branch_two, gain_all[1], shift_all[1])
    second_low = second.astype(BF)

    hidden_act, hidden_slope = gelu_parts(mm(second_low, w_ff1) + bias_ff)
    hidden_low = hidden_act.astype(BF)
    branch_ffn = mm(hidden_low, w_ff2) + bias_all[6]
    final, final_norm, final_scale = norm_fwd(second + branch_ffn, gain_all[2], shift_all[2])
    output = final.astype(BF)
    cot = cotangent.astype(F32)
    grad_three = norm_back(cot, final_norm, final_scale, gain_all[2])
    grad_y = grad_three.astype(BF)
    grad_pre = (mm_nt(grad_y, w_ff2) * hidden_slope).astype(BF)
    grad_second = grad_three + mm_nt(grad_pre, w_ff1)
    grad_two = norm_back(grad_second, second_norm, second_scale, gain_all[1])
    grad_o2 = grad_two.astype(BF)
    grad_cmix = mm_nt(grad_o2, w_out[1]).astype(BF)
    grad_smix = jnp.einsum(
        "the,dhe->htd", heads(grad_cmix), val_heads, preferred_element_type=F32
    ).astype(BF)
    grad_rows, grad_cs = cross_bwd(query_keys, grad_smix, fetched, cross_p)
    send_back = grad_rows[entry]
    returned = all_to_all(send_back)

    send_back, hidden_low, grad_cs, second_low, cross_low, state_mix = lax.optimization_barrier(
        (send_back, hidden_low, grad_cs, second_low, cross_low, state_mix)
    )
    grad_w_ff2 = mm_tn(hidden_low, grad_y).astype(BF)
    grad_w_ff1 = mm_tn(second_low, grad_pre).astype(BF)
    blocks_b = pack_ff(
        grad_w_ff1, grad_w_ff2, order_b[::-1], n_rows, n_cols, rb, cb
    )
    sum_b = scatter_bits(blocks_b, order_b[::-1])

    grad_qk = cross_back_q(grad_cs, fetched)
    grad_cq = jnp.einsum("htd,dhe->the", grad_qk, key_heads, preferred_element_type=F32)
    grad_cq = grad_cq.reshape(tok_count, dim).astype(BF)
    grad_first = grad_two + mm_nt(grad_cq, w_in[3])
    grad_one = norm_back(grad_first, first_norm, first_scale, gain_all[0])
    grad_o = grad_one.astype(BF)
    grad_mix = heads(mm_nt(grad_o, w_out[0]).astype(BF))
    grad_probs = jnp.einsum("qhd,khd->hqk", grad_mix, values, preferred_element_type=F32)
    grad_v = jnp.einsum("hqk,qhd->khd", probs_low, grad_mix, preferred_element_type=F32)
    grad_scores = (
        probs * (grad_probs - jnp.sum(probs * grad_probs, axis=-1, keepdims=True))
    ).astype(BF)
    grad_q = jnp.einsum("hqk,khd->qhd", grad_scores, key_rows, preferred_element_type=F32) * 0.125
    grad_k = jnp.einsum("hqk,qhd->khd", grad_scores, queries, preferred_element_type=F32) * 0.125
    grad_q, grad_k, grad_v = (
        part.reshape(tok_count, dim).astype(BF) for part in (grad_q, grad_k, grad_v)
    )
    grad_tokens = (
        grad_one + mm_nt(grad_q, w_in[0]) + mm_nt(grad_k, w_in[1]) + mm_nt(grad_v, w_in[2])
    )

    def by_head(left, right):
        return jnp.einsum("htd,the->dhe", left, heads(right), preferred_element_type=F32)

    mats = (
        mm_tn(tokens, grad_q).astype(BF),
        mm_tn(tokens, grad_k).astype(BF),
        mm_tn(tokens, grad_v).astype(BF),
        mm_tn(first_low, grad_cq).astype(BF),
        by_head(grad_qk, cross_q).reshape(dim, dim).astype(BF),
        by_head(state_mix, grad_cmix).reshape(dim, dim).astype(BF),
        mm_tn(mixed, grad_o).astype(BF),
        mm_tn(cross_low, grad_o2).astype(BF),
    )
    grad_vectors = jnp.stack(
        [
            column_sum(grad_q),
            column_sum(grad_v),
            column_sum(grad_o),
            column_sum(grad_cq),
            column_sum(grad_cmix),
            column_sum(grad_o2),
            column_sum(grad_y),
            jnp.sum(grad_first * first_norm, axis=0),
            jnp.sum(grad_second * second_norm, axis=0),
            jnp.sum(cot * final_norm, axis=0),
            jnp.sum(grad_first, axis=0),
            jnp.sum(grad_second, axis=0),
            jnp.sum(cot, axis=0),
        ]
    )
    grad_small = jnp.concatenate(
        [
            grad_vectors.reshape(13, n_rows, row_block)
            .transpose(1, 0, 2)
            .reshape(n_rows, 13 * row_block),
            column_sum(grad_pre).reshape(n_rows, -1),
        ],
        axis=1,
    ).astype(BF)
    grad_small = jnp.pad(grad_small, ((0, 0), (0, small_rows * cb - grad_small.shape[1])))
    blocks_a = pack_attn(
        mats,
        grad_small.reshape(n_rows, small_rows, cb),
        order_a[::-1],
        n_rows,
        n_cols,
        rb,
        cb,
    )
    sum_a = scatter_bits(blocks_a, order_a[::-1])

    grad_store = store_sum(asked, returned.reshape(peers * slots, dim), shard_rows)

    sum_a = sum_a.astype(F32)
    sum_b = sum_b.astype(F32)
    sum_small = sum_a[8 * rb :].reshape(-1)
    sum_vec = sum_small[: 13 * row_block].reshape(13, row_block)
    return (
        output,
        grad_tokens,
        grad_store,
        sum_a[: 6 * rb].reshape(6, rb, cb),
        sum_a[6 * rb : 8 * rb].reshape(2, rb, cb),
        jnp.concatenate([sum_b[k * rb : (k + 1) * rb] for k in range(4)], axis=1),
        sum_b[4 * rb :],
        sum_vec[:7],
        sum_vec[7:10],
        sum_vec[10:],
        sum_small[13 * row_block : 13 * row_block + ff_bias.size],
    )


def solution(mesh):
    both = ("row", "col")
    return jax.shard_map(
        on_device,
        mesh=mesh,
        in_specs=(
            P(both, None),
            P(both, None),
            P(both, None),
            P(both, None),
            P(both, None),
            P(None, "row", "col"),
            P(None, "row", "col"),
            P("row", "col"),
            P("row", "col"),
            P(None, "row"),
            P(None, "row"),
            P(None, "row"),
            P("row"),
            P(both, None),
        ),
        out_specs=(
            P(both, None),
            P(both, None),
            P(both, None),
            P(None, "row", "col"),
            P(None, "row", "col"),
            P("row", "col"),
            P("row", "col"),
            P(None, "row"),
            P(None, "row"),
            P(None, "row"),
            P("row"),
        ),
        check_vma=False,
    )
```

```python
import functools

import jax
import jax.numpy as jnp
import numpy as np
from jax import lax
from jax.experimental import pallas as pl
from jax.experimental.pallas import tpu as pltpu
from jax.sharding import PartitionSpec as P

H = 12
HD = 64
RANKS = ("row", "col")
BF = jnp.bfloat16
F32 = jnp.float32
VMEM_LIMIT = 60 * 1024 * 1024


def mm(a, b):
    return jnp.dot(a, b, preferred_element_type=F32)


def mm_nt(a, b):
    return lax.dot_general(a, b, (((1,), (1,)), ((), ())), preferred_element_type=F32)


def mm_tn(a, b):
    return lax.dot_general(a, b, (((0,), (0,)), ((), ())), preferred_element_type=F32)


def norm_fwd(resid, gain, shift):
    row_mean = jnp.mean(resid, axis=-1, keepdims=True)
    centered = resid - row_mean
    inv_std = lax.rsqrt(jnp.mean(centered * centered, axis=-1, keepdims=True) + 1e-05)
    normed = centered * inv_std
    return (normed * gain + shift, normed, inv_std)


def norm_back(grad_in, normed, inv_std, gain):
    scaled = grad_in * gain
    return inv_std * (
        scaled
        - jnp.mean(scaled, axis=-1, keepdims=True)
        - normed * jnp.mean(scaled * normed, axis=-1, keepdims=True)
    )


def gelu_parts(pre_act):
    cdf_part = 0.5 * (1.0 + lax.erf(pre_act * 0.7071067811865476))
    density = jnp.exp(-0.5 * pre_act * pre_act) * 0.3989422804014327
    return (pre_act * cdf_part, cdf_part + pre_act * density)


def visible_mask(seg_row, live_row):
    pos = jnp.arange(seg_row.shape[0], dtype=jnp.int32)
    return (
        (pos[None, :] <= pos[:, None])
        & (seg_row[:, None] == seg_row[None, :])
        & ((live_row[None, :] == 1) | (pos[None, :] == pos[:, None]))
    )


def column_sum(array):
    return jnp.sum(array.astype(F32), axis=0)


def bit_orders(n_rows, n_cols):
    row_bits = [("row", 1 << b) for b in reversed(range(n_rows.bit_length() - 1))]
    col_bits = [("col", 1 << b) for b in reversed(range(n_cols.bit_length() - 1))]
    swapped = row_bits[:-2] + row_bits[-1:] + row_bits[-2:-1]
    return row_bits + col_bits, swapped + col_bits


def swap_bit(array, axis, bit):
    pairs = [(i, i ^ bit) for i in range(lax.axis_size(axis))]
    return lax.ppermute(array, axis, pairs)


def gather_bits(blocks, order):
    for axis, bit in order:
        blocks = jnp.concatenate([blocks, swap_bit(blocks, axis, bit)], axis=0)
    return blocks


def scatter_bits(keep, send, order):
    for axis, bit in order:
        got = swap_bit(send, axis, bit)
        half = keep.shape[0] // 2
        keep, send = keep[:half] + got[:half], keep[half:] + got[half:]
    return keep, send


def block_of_row(order, n_rows):
    apart = np.zeros(n_rows, np.int32)
    for k, (_, bit) in enumerate(order[: n_rows.bit_length() - 1]):
        apart[(np.arange(n_rows) >> k) & 1 == 1] ^= bit
    table = np.zeros(n_rows, np.int32)
    table[apart] = np.arange(n_rows)
    return jnp.asarray(table)[lax.axis_index("row") ^ jnp.arange(n_rows, dtype=jnp.int32)]


def flip_by_position(blocks, stages):
    for k, (axis, bit) in enumerate(stages):
        here = (lax.axis_index(axis) & bit) != 0
        blocks = jnp.where(here, jnp.flip(blocks, axis=k), blocks)
    return blocks


def by_device(blocks, order):
    stages = order[::-1]
    shape = blocks.shape[1:]
    blocks = flip_by_position(blocks.reshape((2,) * len(stages) + shape), stages)
    rank = sorted(range(len(stages)), key=lambda k: (stages[k][0] == "col", -stages[k][1]))
    rest = list(range(len(stages), blocks.ndim))
    return blocks.transpose(rank + rest).reshape((-1,) + shape)


def by_stage(blocks, stages):
    shape = blocks.shape[1:]
    rank = sorted(range(len(stages)), key=lambda k: (stages[k][0] == "col", -stages[k][1]))
    rest = list(range(len(stages), len(stages) + len(shape)))
    back = [rank.index(k) for k in range(len(stages))]
    blocks = blocks.reshape((2,) * len(stages) + shape).transpose(back + rest)
    return flip_by_position(blocks, stages).reshape((-1,) + shape)


WAIT = pl.BlockSpec(memory_space=pl.ANY)


def tie_kernel(*refs):
    refs[-1][...] = refs[0][...]


def tie(array, after):
    return pl.pallas_call(
        tie_kernel,
        in_specs=[pl.BlockSpec(memory_space=pltpu.VMEM)] + [WAIT] * len(after),
        out_shape=jax.ShapeDtypeStruct(array.shape, array.dtype),
        name="tie",
    )(array, *after)


def hold_kernel(*refs):
    del refs


def hold(array, after):
    return pl.pallas_call(
        hold_kernel,
        in_specs=[WAIT] * (1 + len(after)),
        out_specs=WAIT,
        out_shape=jax.ShapeDtypeStruct(array.shape, array.dtype),
        input_output_aliases={0: 0},
        name="hold",
    )(array, *after)


def tile_of(buf, k, r, c, shape):
    rows, cols = shape
    return buf.at[
        k, pl.ds(pl.multiple_of(r * rows, rows), rows), pl.ds(pl.multiple_of(c * cols, cols), cols)
    ]


def unpack_kernel(place, own, other, *refs, count, shape, first, beside, extra):
    outs, (buf, *more) = refs[: 1 + bool(extra)], refs[1 + bool(extra) :]
    sems = more[-1]
    n_rows, col, rows = own.shape[0], place[own.shape[0]], shape[0]

    def fill(r, carry):
        j = place[r]
        for src, c, sem in ((own, col, 0), (other, 1 - col, 1)):
            for k in range(count):
                part = src.at[j, pl.ds(first + k * rows, rows)]
                to = (0, r, c * count + k) if beside else (k, r, c)
                pltpu.make_async_copy(part, tile_of(buf, *to, shape), sems.at[sem]).start()
        if extra:
            tail = own.at[j, pl.ds(first + count * rows, extra)]
            pltpu.make_async_copy(tail, more[0].at[r], sems.at[2]).start()
        return carry

    lax.fori_loop(0, n_rows, fill, 0)
    body = own.at[:, pl.ds(first, count * rows)]
    for sem in range(2):
        pltpu.make_async_copy(body, body, sems.at[sem]).wait()
    out = pltpu.make_async_copy(buf, outs[0], sems.at[3])
    out.start()
    if extra:
        pltpu.make_async_copy(more[0], more[0], sems.at[2]).wait()
        tails = pltpu.make_async_copy(more[0], outs[1], sems.at[4])
        tails.start()
        tails.wait()
    out.wait()


def unpack(own, other, place, count, shape, first=0, beside=False, extra=0):
    n_rows = own.shape[0]
    rows, cols = shape
    many, wide = (1, count) if beside else (count, 1)
    whole = jax.ShapeDtypeStruct((many, n_rows * rows, 2 * wide * cols), BF)
    tails = jax.ShapeDtypeStruct((n_rows, extra, cols), BF)
    shapes = [whole] + [tails] * bool(extra)
    got = pl.pallas_call(
        functools.partial(
            unpack_kernel, count=count, shape=shape, first=first, beside=beside, extra=extra
        ),
        in_specs=[pl.BlockSpec(memory_space=pltpu.SMEM)] + [pl.BlockSpec(memory_space=pl.ANY)] * 2,
        out_specs=[pl.BlockSpec(memory_space=pl.ANY)] * len(shapes),
        out_shape=shapes,
        scratch_shapes=[pltpu.VMEM(x.shape, BF) for x in shapes] + [pltpu.SemaphoreType.DMA((5,))],
        compiler_params=pltpu.CompilerParams(vmem_limit_bytes=32 * 1024 * 1024),
        cost_estimate=pl.CostEstimate(
            flops=0, bytes_accessed=4 * whole.size * 2, transcendentals=0
        ),
        name="unpack",
    )(place, own, other)
    return got if extra else got[0]


def split_cols(array, pieces):
    width = array.shape[1] // pieces
    return jnp.concatenate([array[:, i * width : (i + 1) * width] for i in range(pieces)], axis=0)


def join_kernel(attn_in, attn_out, small, ff_in, ff_out, side_a, side_b, *, rb, cb):
    at = 0
    for array in (attn_in, attn_out):
        for k in range(array.shape[0]):
            side_a[0, at : at + rb] = array[k]
            at += rb
    side_a[0, at:] = small[...]
    for k in range(4):
        side_b[0, k * rb : (k + 1) * rb] = ff_in[:, k * cb : (k + 1) * cb]
    side_b[0, 4 * rb :] = ff_out[...]


def join(attn_in, attn_out, small, ff_in, ff_out):
    rb, cb = attn_in.shape[1:]
    if rb % 16 or cb % 128:
        side_a = [attn_in.reshape(-1, cb), attn_out.reshape(-1, cb), small]
        side_b = [split_cols(ff_in, 4), ff_out]
        return tuple(jnp.concatenate(side, axis=0)[None] for side in (side_a, side_b))
    return pl.pallas_call(
        functools.partial(join_kernel, rb=rb, cb=cb),
        out_shape=(
            jax.ShapeDtypeStruct((1, 8 * rb + small.shape[0], cb), BF),
            jax.ShapeDtypeStruct((1, 8 * rb, cb), BF),
        ),
        name="join",
    )(attn_in, attn_out, small, ff_in, ff_out)


def pack_kernel(place, *refs, mats, rows, extra, waits):
    n_ops = 1 + max(max(mat[0]) for mat in mats)
    ops, refs = refs[:n_ops], refs[n_ops:]
    small, refs = refs[: bool(extra)], refs[bool(extra) + waits :]
    keep, send, *bufs, sems = refs
    n_rows, col = keep.shape[0], place[keep.shape[0]]
    loads = {}
    for k, (at, _, _) in enumerate(mats):
        if len(at) == 1:
            loads[k] = pltpu.make_async_copy(ops[at[0]], bufs[k].at[0], sems.at[2 + k])
            loads[k].start()
    for k, (at, _, _) in enumerate(mats):
        if len(at) == 2:
            left, right = ops[at[0]], ops[at[1]]
            _, tall, wide = bufs[k].shape
            tile = min(tall, wide)
            for i in range(0, tall, tile):
                for j in range(0, wide, tile):
                    got = mm_tn(left[:, i : i + tile], right[:, j : j + tile])
                    bufs[k][0, i : i + tile, j : j + tile] = got.astype(BF)
    for load in loads.values():
        load.wait()

    def spread(r, carry):
        j = place[r]
        for dst, c, sem in ((keep, col, 0), (send, 1 - col, 1)):
            first = 0
            for buf, (_, shape, beside) in zip(bufs, mats):
                for k in range(beside):
                    part = dst.at[j, pl.ds(first, shape[0])]
                    tile = tile_of(buf, 0, r, c * beside + k, shape)
                    pltpu.make_async_copy(tile, part, sems.at[sem]).start()
                    first += shape[0]
            if extra:
                tail = dst.at[j, pl.ds(first, extra)]
                pltpu.make_async_copy(small[0].at[r], tail, sems.at[sem]).start()
        return carry

    lax.fori_loop(0, n_rows, spread, 0)
    for dst, sem in ((keep, 0), (send, 1)):
        pltpu.make_async_copy(dst, dst, sems.at[sem]).wait()


def pack(mats, place, small=None, after=()):
    ops, parts, specs, bufs, flops, total = [], [], [], [], 0, 0
    for mat, shape, beside in mats:
        mat = mat if isinstance(mat, tuple) else (mat,)
        parts.append((tuple(range(len(ops), len(ops) + len(mat))), shape, beside))
        ops += mat
        specs += [pl.BlockSpec(memory_space=pltpu.VMEM if len(mat) == 2 else pl.ANY)] * len(mat)
        whole = (mat[0].shape[1], mat[1].shape[1]) if len(mat) == 2 else mat[0].shape
        bufs.append(pltpu.VMEM((1,) + tuple(whole), BF))
        flops += 2 * mat[0].shape[0] * whole[0] * whole[1] if len(mat) == 2 else 0
        total += beside * shape[0]
        n_rows = whole[0] // shape[0]
    extra = 0 if small is None else small.shape[1]
    block = jax.ShapeDtypeStruct((n_rows, total + extra, shape[1]), BF)
    if extra:
        ops.append(small)
        specs.append(pl.BlockSpec(memory_space=pltpu.VMEM))
    return pl.pallas_call(
        functools.partial(
            pack_kernel, mats=tuple(parts), rows=total, extra=extra, waits=len(after)
        ),
        in_specs=[pl.BlockSpec(memory_space=pltpu.SMEM)] + specs + [WAIT] * len(after),
        out_specs=[pl.BlockSpec(memory_space=pl.ANY)] * 2,
        out_shape=[block, block],
        scratch_shapes=bufs + [pltpu.SemaphoreType.DMA((2 + len(mats),))],
        compiler_params=pltpu.CompilerParams(vmem_limit_bytes=48 * 1024 * 1024),
        cost_estimate=pl.CostEstimate(
            flops=flops, bytes_accessed=8 * block.size, transcendentals=0
        ),
        name="pack",
    )(place, *ops, *after)


def unpack_any(blocks, order, n_rows, n_cols, rb):
    cols = blocks.shape[2]
    got = by_device(blocks, order).reshape(n_rows, n_cols, -1, cols)
    return got[:, :, : 8 * rb].reshape(n_rows, n_cols, 8, rb, cols), got[:, 0, 8 * rb :]


def pack_any(mats, order, small, n_rows, n_cols):
    got = []
    for mat, (rows, cols), beside in mats:
        mat = mm_tn(*mat).astype(BF) if isinstance(mat, tuple) else mat
        mat = mat.reshape(n_rows, rows, n_cols, beside, cols).transpose(0, 2, 3, 1, 4)
        got.append(mat.reshape(n_rows, n_cols, beside * rows, cols))
    if small is not None:
        got.append(jnp.broadcast_to(small[:, None], (n_rows, n_cols) + small.shape[1:]))
    got = jnp.concatenate(got, axis=2)
    got = by_stage(got.reshape((-1,) + got.shape[2:]), order)
    half = got.shape[0] // 2
    return got[:half], got[half:]


def plan_requests(ret_rows, shard_rows, peers, slots):
    flat = ret_rows.reshape(-1)
    count = flat.shape[0]
    owner = flat // shard_rows
    local_row = flat - owner * shard_rows
    mine = owner[:, None] == jnp.arange(peers, dtype=jnp.int32)[None, :]
    run = 256
    runs = count // run
    ones = mine.astype(BF).reshape(runs, run, peers)
    lower = jnp.tril(jnp.ones((run, run), BF))
    within = jnp.einsum("ij,bjo->bio", lower, ones, preferred_element_type=F32)
    totals = within[:, -1, :]
    before = jnp.cumsum(totals, axis=0) - totals
    upto = (within + before[:, None, :]).reshape(count, peers)
    rank = jnp.sum(jnp.where(mine, upto, 0.0), axis=1).astype(jnp.int32) - 1
    place = owner * slots + rank
    row_code = local_row + 1
    entry_code = jnp.arange(count, dtype=jnp.int32)
    digits = jnp.stack([row_code // 64, row_code % 64, entry_code // 64, entry_code % 64])
    left = jnp.where(mine.T[None], digits[:, None, :], 0).astype(BF)
    at_rank = (rank[:, None] == jnp.arange(slots, dtype=jnp.int32)[None, :]).astype(BF)
    codes = mm(left.reshape(4 * peers, count), at_rank).astype(jnp.int32).reshape(4, peers, slots)
    return place, codes[0] * 64 + codes[1], codes[2] * 64 + codes[3]


def own_rows(tokens, ret, heads):
    shape = (heads * tokens, tokens * ret)
    row_tok = lax.broadcasted_iota(jnp.int32, shape, 0) % tokens
    col_tok = lax.broadcasted_iota(jnp.int32, shape, 1) // ret
    return row_tok == col_tok


def cross_fwd_kernel(qk, fetched, mix, probs, *, ret):
    heads, tokens, dim = qk.shape
    own = own_rows(tokens, ret, heads)
    query = qk[...].reshape(heads * tokens, dim)
    rows = fetched[...]
    scores = jnp.where(own, mm_nt(query, rows) * 0.125, -1e30)
    expo = jnp.exp(scores - jnp.max(scores, axis=-1, keepdims=True))
    prob = expo / jnp.sum(expo, axis=-1, keepdims=True)
    probs[0] = prob
    mix[...] = mm(prob.astype(BF), rows).astype(BF).reshape(heads, tokens, dim)


def cross_bwd_kernel(qk, gmix, fetched, probs, grad_rows, grad_s, *, ret):
    heads, tokens, dim = qk.shape
    query = qk[...].reshape(heads * tokens, dim)
    grad_mix = gmix[...].reshape(heads * tokens, dim)
    prob = probs[0]
    grad_p = mm_nt(grad_mix, fetched[...])
    g_s = (prob * (grad_p - jnp.sum(prob * grad_p, axis=-1, keepdims=True))).astype(BF)
    grad_s[0] = g_s
    grad_rows[...] = (
        mm_tn(prob.astype(BF), grad_mix) + mm_tn(g_s, query) * 0.125
    ).astype(BF)


def cross_back_q_kernel(grad_s, fetched, grad_qk):
    heads, tokens, dim = grad_qk.shape
    got = mm(grad_s[0], fetched[...]) * 0.125
    grad_qk[...] = got.astype(BF).reshape(heads, tokens, dim)


def cross_calls(tok_count, ret, dim):
    tb = 16
    blocks = tok_count // tb
    by_head = pl.BlockSpec((H, tb, dim), lambda g: (0, g, 0))
    rows = pl.BlockSpec((tb * ret, dim), lambda g: (g, 0))
    square = pl.BlockSpec((1, H * tb, tb * ret), lambda g: (g, 0, 0))
    heads_shape = jax.ShapeDtypeStruct((H, tok_count, dim), BF)
    square_f32 = jax.ShapeDtypeStruct((blocks, H * tb, tb * ret), F32)
    square_bf = jax.ShapeDtypeStruct((blocks, H * tb, tb * ret), BF)
    params = pltpu.CompilerParams(vmem_limit_bytes=VMEM_LIMIT)
    fwd = pl.pallas_call(
        functools.partial(cross_fwd_kernel, ret=ret),
        grid=(blocks,),
        in_specs=[by_head, rows],
        out_specs=[by_head, square],
        out_shape=(heads_shape, square_f32),
        compiler_params=params,
        name="cross_fwd",
    )
    bwd = pl.pallas_call(
        functools.partial(cross_bwd_kernel, ret=ret),
        grid=(blocks,),
        in_specs=[by_head, by_head, rows, square],
        out_specs=[rows, square],
        out_shape=(jax.ShapeDtypeStruct((tok_count * ret, dim), BF), square_bf),
        compiler_params=params,
        name="cross_bwd",
    )
    back_q = pl.pallas_call(
        cross_back_q_kernel,
        grid=(blocks,),
        in_specs=[square, rows],
        out_specs=by_head,
        out_shape=heads_shape,
        compiler_params=params,
        name="cross_back_q",
    )
    return fwd, bwd, back_q


GROUP = 8
LANES = 128
PITCH = LANES // GROUP


def plan_kernel(rows, wanted, token, at_rank, owner, *, shard_rows):
    peers, slots = wanted.shape
    ret, toks = rows.shape
    shape = (toks, toks)
    upper = (
        lax.broadcasted_iota(jnp.int32, shape, 0) <= lax.broadcasted_iota(jnp.int32, shape, 1)
    ).astype(BF)
    peer = lax.broadcasted_iota(jnp.int32, (peers, toks), 0)
    tok_code = (lax.broadcasted_iota(jnp.int32, (peers, toks), 1) + 1).astype(F32)
    k_rows = lax.broadcasted_iota(jnp.int32, (at_rank.shape[0], toks), 0)
    shift = shard_rows.bit_length() - 1
    before = jnp.zeros((peers, 1), F32)
    codes = jnp.zeros((3 * peers, at_rank.shape[0]), F32)
    for r in range(ret):
        row = rows[r : r + 1, :]
        own = lax.shift_right_logical(row, shift)
        code = lax.bitwise_and(row, shard_rows - 1) + 1
        mine = own == peer
        upto = mm(mine.astype(BF), upper) + before
        before = upto[:, toks - 1 :]
        rank = jnp.sum(jnp.where(mine, upto, 0.0), axis=0, keepdims=True).astype(jnp.int32) - 1
        at = (k_rows == rank).astype(BF)
        at_rank[:, r * toks : (r + 1) * toks] = at
        owner[r : r + 1, :] = own
        high = lax.shift_right_logical(code, 6).astype(F32)
        low = lax.bitwise_and(code, 63).astype(F32)
        left = jnp.concatenate(
            [
                jnp.where(mine, high, 0.0).astype(BF),
                jnp.where(mine, low, 0.0).astype(BF),
                jnp.where(mine, tok_code, 0.0).astype(BF),
            ],
            axis=0,
        )
        codes = codes + mm_nt(left, at)
    codes = codes[:, :slots].astype(jnp.int32)
    wanted[...] = codes[:peers] * 64 + codes[peers : 2 * peers]
    token[...] = codes[2 * peers :]


def plan_slots(rows, shard_rows, peers, slots):
    ret, toks = rows.shape
    tall = -(-slots // LANES) * LANES
    return pl.pallas_call(
        functools.partial(plan_kernel, shard_rows=shard_rows),
        out_shape=(
            jax.ShapeDtypeStruct((peers, slots), jnp.int32),
            jax.ShapeDtypeStruct((peers, slots), jnp.int32),
            jax.ShapeDtypeStruct((tall, ret * toks), BF),
            jax.ShapeDtypeStruct((ret, toks), jnp.int32),
        ),
        name="plan",
    )(rows)


def head_sum(dim):
    shape = (dim, LANES)
    head = lax.broadcasted_iota(jnp.int32, shape, 0) // HD
    return (head == lax.broadcasted_iota(jnp.int32, shape, 1)).astype(BF)


def head_spread(dim):
    shape = (LANES, dim)
    head = lax.broadcasted_iota(jnp.int32, shape, 1) // HD
    return (head == lax.broadcasted_iota(jnp.int32, shape, 0)).astype(BF)


def to_lanes(by_peer, k):
    total = by_peer[:k]
    for q in range(1, GROUP):
        total = total + pltpu.roll(by_peer[q * k : (q + 1) * k], PITCH * q, 1)
    return total


def from_lanes(lanes):
    parts = [lanes] + [pltpu.roll(lanes, LANES - PITCH * q, 1) for q in range(1, GROUP)]
    return jnp.concatenate([part.astype(BF) for part in parts], axis=0)


def to_entries(slot_vals, at_rank, owner):
    k, wide = slot_vals.shape
    tall, toks = at_rank.shape[0], owner.shape[1]
    peers = wide // PITCH
    full = jnp.concatenate([slot_vals, jnp.zeros((tall - k, wide), F32)], axis=0).T
    high = full.astype(BF)
    low = (full - high.astype(F32)).astype(BF)
    peer = lax.broadcasted_iota(jnp.int32, (wide, toks), 0) // PITCH
    out = []
    for r in range(owner.shape[0]):
        at = at_rank[:, r * toks : (r + 1) * toks]
        got = mm(high, at) + mm(low, at)
        got = jnp.where(peer == owner[r : r + 1, :], got, 0.0)
        out.append(jnp.sum(got.reshape(peers, PITCH, toks), axis=0))
    return out


def to_slots(entry_vals, at_rank, owner, peers, slots):
    toks = owner.shape[1]
    wide = peers * PITCH
    peer = lax.broadcasted_iota(jnp.int32, (wide, toks), 0) // PITCH
    total = jnp.zeros((at_rank.shape[0], wide), F32)
    for r, vals in enumerate(entry_vals):
        tiled = jnp.concatenate([vals] * peers, axis=0)
        mine = jnp.where(peer == owner[r : r + 1, :], tiled, 0.0).astype(BF)
        total = total + mm_nt(at_rank[:, r * toks : (r + 1) * toks], mine)
    return total[:slots]


def rows_in_kernel(arrived, query, w_k, w_v, keys, vals, scores):
    group, k, dim = arrived.shape
    rows = arrived[...].reshape(group * k, dim)
    key = mm(rows, w_k[...])
    keys[...] = key.astype(BF).reshape(group, k, dim)
    prod = (key * query[...].reshape(group * k, dim).astype(F32)).astype(BF)
    scores[...] = to_lanes(mm(prod, head_sum(dim)), k) * 0.125
    vals[...] = mm(rows, w_v[...]).astype(BF).reshape(group, k, dim)


def attend_kernel(*refs, chunks):
    scores, vals, token_t = refs[:chunks], refs[chunks : 2 * chunks], refs[2 * chunks : 3 * chunks]
    at_rank, owner, bias, prob_tok, prob_slot, mixed, total = refs[3 * chunks :]
    step, steps = pl.program_id(0), pl.num_programs(0)
    k, dim = vals[0].shape[1:]

    @pl.when(step == 0)
    def _():
        entry = to_entries(
            jnp.concatenate([part[...] for part in scores], axis=0), at_rank, owner
        )
        top = functools.reduce(jnp.maximum, entry)
        expo = [jnp.exp(part - top) for part in entry]
        norm = functools.reduce(jnp.add, expo)
        probs = [part / norm for part in expo]
        for r, part in enumerate(probs):
            prob_tok[r * PITCH : (r + 1) * PITCH, :] = part
        peers = scores[0].shape[1] // PITCH
        prob_slot[...] = to_slots(probs, at_rank, owner, peers, chunks * k)
        total[...] = jnp.zeros_like(total)

    spread = head_spread(dim)
    lanes = pl.ds(pl.multiple_of(step * LANES, LANES), LANES)
    acc = total[...]
    for c in range(chunks):
        prob = mm(from_lanes(prob_slot[c * k : (c + 1) * k, lanes]), spread)
        prod = (prob * vals[c][...].reshape(-1, dim).astype(F32)).astype(BF)
        acc = acc + mm(token_t[c][...], prod)
    total[...] = acc

    @pl.when(step == steps - 1)
    def _():
        mixed[...] = (total[...] + bias[...]).astype(BF)


def attend_back_kernel(*refs, chunks):
    vals, token = refs[:chunks], refs[chunks : 2 * chunks]
    grad, prob_tok, at_rank, owner = refs[2 * chunks : 2 * chunks + 4]
    grads, (grad_slot, slot_p) = refs[2 * chunks + 4 : -2], refs[-2:]
    step, steps = pl.program_id(0), pl.num_programs(0)
    k, dim = vals[0].shape[1:]
    lanes = pl.ds(pl.multiple_of(step * LANES, LANES), LANES)
    add_up = head_sum(dim)
    for c in range(chunks):
        wide = mm(token[c][...], grad[...])
        grads[c][...] = wide.astype(BF).reshape(vals[c].shape)
        prod = (wide * vals[c][...].reshape(-1, dim).astype(F32)).astype(BF)
        slot_p[c * k : (c + 1) * k, lanes] = to_lanes(mm(prod, add_up), k)

    @pl.when(step == steps - 1)
    def _():
        entry = to_entries(slot_p[...], at_rank, owner)
        probs = [prob_tok[r * PITCH : (r + 1) * PITCH, :] for r in range(len(entry))]
        dots = functools.reduce(jnp.add, [p * g for p, g in zip(probs, entry)])
        scores = [(p * (g - dots)).astype(BF).astype(F32) for p, g in zip(probs, entry)]
        peers = slot_p.shape[1] // PITCH
        grad_slot[...] = to_slots(scores, at_rank, owner, peers, chunks * k)


def rows_out_kernel(prob_slot, grad_slot, grad, query, w_k, w_v, *refs):
    out, by_prob, by_score = refs[-3:]
    group, k, dim = grad.shape
    spread = head_spread(dim)
    prob = mm(from_lanes(prob_slot[...]), spread)
    mix = (prob * grad[...].reshape(-1, dim).astype(F32)).astype(BF)
    score = mm(from_lanes(grad_slot[...]), spread) * 0.125
    ask = (score * query[...].reshape(-1, dim).astype(F32)).astype(BF)
    out[...] = (mm_nt(mix, w_v[...]) + mm_nt(ask, w_k[...])).astype(BF).reshape(grad.shape)
    by_prob[...] = mix.reshape(grad.shape)
    by_score[...] = ask.reshape(grad.shape)


def query_back_kernel(*refs, chunks):
    keys, token_t = refs[:chunks], refs[chunks : 2 * chunks]
    grad_slot, (out, total) = refs[2 * chunks], refs[-2:]
    step, steps = pl.program_id(0), pl.num_programs(0)
    k, dim = keys[0].shape[1:]

    @pl.when(step == 0)
    def _():
        total[...] = jnp.zeros_like(total)

    spread = head_spread(dim)
    lanes = pl.ds(pl.multiple_of(step * LANES, LANES), LANES)
    acc = total[...]
    for c in range(chunks):
        score = mm(from_lanes(grad_slot[c * k : (c + 1) * k, lanes]), spread) * 0.125
        prod = (score * keys[c][...].reshape(-1, dim).astype(F32)).astype(BF)
        acc = acc + mm(token_t[c][...], prod)
    total[...] = acc

    @pl.when(step == steps - 1)
    def _():
        out[...] = total[...].astype(BF)


def vector_sums_kernel(*refs, plain, pairs):
    ops, (wide, out, out_wide) = refs[: plain + 2 * pairs], refs[plain + 2 * pairs :]
    rows = [ops[i][...].astype(F32) for i in range(plain)]
    lefts = [ops[plain + 2 * i][...].astype(F32) for i in range(pairs)]
    rows += [lefts[i] * ops[plain + 2 * i + 1][...] for i in range(pairs)]
    rows += lefts
    sums = [jnp.sum(row, axis=0, keepdims=True) for row in rows]
    sums.append(jnp.zeros((out.shape[0] - len(sums), out.shape[1]), F32))
    out[...] = jnp.concatenate(sums, axis=0)
    out_wide[...] = jnp.sum(wide[...].astype(F32), axis=0, keepdims=True)


def vector_sums(plain, pairs, wide):
    ops = list(plain) + [x for pair in pairs for x in pair] + [wide]
    dim = plain[0].shape[1]
    return pl.pallas_call(
        functools.partial(vector_sums_kernel, plain=len(plain), pairs=len(pairs)),
        out_shape=(
            jax.ShapeDtypeStruct((16, dim), F32),
            jax.ShapeDtypeStruct((1, wide.shape[1]), F32),
        ),
        compiler_params=pltpu.CompilerParams(vmem_limit_bytes=24 * 1024 * 1024),
        name="vector_sums",
    )(*ops)


class SlotAttention:
    def __init__(self, ret_rows, shard_rows, peers, slots, dim, parts):
        self.toks, self.ret = ret_rows.shape
        chunks = parts
        self.peers, self.slots, self.dim, self.chunks = peers, slots, dim, chunks
        self.k = slots // chunks
        self.sent = []
        self.wanted, token, self.at_rank, self.owner = plan_slots(
            ret_rows.T, shard_rows, peers, slots
        )
        self.codes = [self.part(token, c).reshape(-1) for c in range(chunks)]
        self.heads = jax.ShapeDtypeStruct((slots, peers * PITCH), F32)

    def part(self, array, c):
        return array[:, c * self.k : (c + 1) * self.k]

    def specs(self):
        k, dim, toks = self.k, self.dim, self.toks
        rows = pl.BlockSpec((GROUP, k, dim), lambda g: (g, 0, 0))
        whole = lambda *shape: pl.BlockSpec(shape, lambda g: (0,) * len(shape))
        token = pl.BlockSpec((GROUP * k, toks), lambda g: (g, 0))
        token_t = pl.BlockSpec((toks, GROUP * k), lambda g: (0, g))
        lanes = lambda c: pl.BlockSpec((k, LANES), lambda g: (c, g))
        return rows, whole, token, token_t, lanes

    def call(self, kernel, name, in_specs, out_specs, out_shape, scratch=(), mib=28):
        return pl.pallas_call(
            kernel,
            grid=(self.peers // GROUP,),
            in_specs=in_specs,
            out_specs=out_specs,
            out_shape=out_shape,
            scratch_shapes=list(scratch),
            compiler_params=pltpu.CompilerParams(vmem_limit_bytes=mib * 1024 * 1024),
            name=name,
        )

    def prepare(self, cross_q):
        toks = self.toks
        ids = jnp.arange(1, toks + 1, dtype=jnp.int32)
        self.token = [(code[:, None] == ids[None, :]).astype(BF) for code in self.codes]
        self.token_t = [(ids[:, None] == code[None, :]).astype(BF) for code in self.codes]
        shape = (self.peers, self.k, self.dim)
        self.query = [mm(token, cross_q).astype(BF).reshape(shape) for token in self.token]

    def forward(self, arrived, w_k, w_v, bias):
        rows, whole, token, token_t, lanes = self.specs()
        shape = jax.ShapeDtypeStruct((self.peers, self.k, self.dim), BF)
        dim, toks, chunks = self.dim, self.toks, self.chunks
        self.arrived, self.w_k, self.w_v = arrived, w_k, w_v
        wide = self.peers * PITCH
        first = self.call(
            rows_in_kernel,
            "rows_in",
            [rows, rows, whole(dim, dim), whole(dim, dim)],
            [rows, rows, lanes(0)],
            (shape, shape, jax.ShapeDtypeStruct((self.k, wide), F32)),
        )
        got = [first(part, query, w_k, w_v) for part, query in zip(arrived, self.query)]
        self.keys, self.vals, scores = zip(*got)
        self.prob_tok, self.prob_slot, mixed = self.call(
            functools.partial(attend_kernel, chunks=chunks),
            "attend",
            [whole(self.k, wide)] * chunks
            + [rows] * chunks
            + [token_t] * chunks
            + [whole(*self.at_rank.shape), whole(*self.owner.shape), whole(1, dim)],
            [whole(self.ret * PITCH, toks), whole(self.slots, wide), whole(toks, dim)],
            (
                jax.ShapeDtypeStruct((self.ret * PITCH, toks), F32),
                self.heads,
                jax.ShapeDtypeStruct((toks, dim), BF),
            ),
            [pltpu.VMEM((toks, dim), F32)],
        )(*scores, *self.vals, *self.token_t, self.at_rank, self.owner, bias.reshape(1, dim))
        return mixed

    def backward(self, grad):
        rows, whole, token, token_t, lanes = self.specs()
        shape = jax.ShapeDtypeStruct((self.peers, self.k, self.dim), BF)
        dim, toks, chunks = self.dim, self.toks, self.chunks
        wide = self.peers * PITCH
        *grads, self.grad_slot = self.call(
            functools.partial(attend_back_kernel, chunks=chunks),
            "attend_back",
            [rows] * chunks
            + [token] * chunks
            + [whole(toks, dim), whole(self.ret * PITCH, toks)]
            + [whole(*self.at_rank.shape), whole(*self.owner.shape)],
            [rows] * chunks + [whole(self.slots, wide)],
            [shape] * chunks + [self.heads],
            [pltpu.VMEM((self.slots, wide), F32)],
        )(*self.vals, *self.token, grad, self.prob_tok, self.at_rank, self.owner)
        self.grads = grads

    def send(self, c, after=()):
        rows, whole, _, _, lanes = self.specs()
        shape = jax.ShapeDtypeStruct((self.peers, self.k, self.dim), BF)
        dim = self.dim
        got = self.call(
            rows_out_kernel,
            "rows_out",
            [lanes(c), lanes(c), rows, rows, whole(dim, dim), whole(dim, dim)]
            + [WAIT] * len(after),
            [rows, rows, rows],
            (shape, shape, shape),
        )(
            self.prob_slot,
            self.grad_slot,
            self.grads[c],
            self.query[c],
            self.w_k,
            self.w_v,
            *after,
        )
        self.sent.append(got)
        return got[0]

    def finish(self):
        rows, whole, token, token_t, lanes = self.specs()
        dim, toks, chunks = self.dim, self.toks, self.chunks
        grad_q = self.call(
            functools.partial(query_back_kernel, chunks=chunks),
            "query_back",
            [rows] * chunks
            + [token_t] * chunks
            + [whole(self.slots, self.peers * PITCH), WAIT],
            whole(toks, dim),
            jax.ShapeDtypeStruct((toks, dim), BF),
            [pltpu.VMEM((toks, dim), F32)],
        )(*self.keys, *self.token_t, self.grad_slot, self.sent[0][0])

        def product(parts):
            flat = lambda x: x.reshape(-1, dim)
            both = [mm_tn(flat(a), flat(b)) for a, b in zip(self.arrived, parts)]
            return functools.reduce(jnp.add, both).astype(BF)

        _, by_prob, by_score = zip(*self.sent)
        return grad_q, product(by_score), product(by_prob)


class GatheredAttention:
    def __init__(self, ret_rows, shard_rows, peers, slots, dim, parts):
        self.toks, self.ret = ret_rows.shape
        self.dim, self.slots = dim, slots
        self.place, self.wanted, self.entry = plan_requests(ret_rows, shard_rows, peers, slots)
        self.fwd, self.bwd, self.back_q = cross_calls(self.toks, self.ret, dim)

    def part(self, array, c):
        return array

    def prepare(self, cross_q):
        self.cross_q = cross_q

    def forward(self, arrived, w_k, w_v, bias):
        toks, dim = self.toks, self.dim
        self.key_heads, self.val_heads = w_k.reshape(dim, H, HD), w_v.reshape(dim, H, HD)
        query = self.cross_q.reshape(toks, H, HD)
        self.query_keys = jnp.einsum(
            "the,dhe->htd", query, self.key_heads, preferred_element_type=F32
        ).astype(BF)
        self.fetched = arrived[0].reshape(-1, dim)[self.place]
        self.state_mix, self.cross_p = self.fwd(self.query_keys, self.fetched)
        mixed = jnp.einsum(
            "htd,dhe->the", self.state_mix, self.val_heads, preferred_element_type=F32
        )
        return (mixed.reshape(toks, dim) + bias).astype(BF)

    def backward(self, grad):
        self.grad = grad.reshape(self.toks, H, HD)
        grad_mix = jnp.einsum(
            "the,dhe->htd", self.grad, self.val_heads, preferred_element_type=F32
        ).astype(BF)
        self.rows, self.grad_s = self.bwd(self.query_keys, grad_mix, self.fetched, self.cross_p)

    def send(self, c, after=()):
        return self.rows[self.entry]

    def finish(self):
        toks, dim = self.toks, self.dim
        grad_qk = self.back_q(self.grad_s, self.fetched)
        grad_q = jnp.einsum("htd,dhe->the", grad_qk, self.key_heads, preferred_element_type=F32)

        def product(left, right):
            got = jnp.einsum("htd,the->dhe", left, right, preferred_element_type=F32)
            return got.reshape(dim, dim).astype(BF)

        grad_k = product(grad_qk, self.cross_q.reshape(toks, H, HD))
        return grad_q.reshape(toks, dim).astype(BF), grad_k, product(self.state_mix, self.grad)


def store_sum_kernel(asked, returned, *refs, block, added):
    first = pl.program_id(0) * block + 1
    shape = (block, asked.shape[1])
    hit = lax.broadcasted_iota(jnp.int32, shape, 0) + first == asked[...]
    total = mm(hit.astype(BF), returned[...])
    refs[-1][...] = total + refs[0][...] if added else total


def store_sum(asked, returned, shard_rows, so_far, after=()):
    count, dim = returned.shape
    block = 256
    out = pl.BlockSpec((block, dim), lambda g: (g, 0))
    before = [] if so_far is None else [so_far]
    return pl.pallas_call(
        functools.partial(store_sum_kernel, block=block, added=so_far is not None),
        grid=(shard_rows // block,),
        in_specs=[
            pl.BlockSpec((1, count), lambda g: (0, 0)),
            pl.BlockSpec((count, dim), lambda g: (0, 0)),
        ]
        + [out] * len(before)
        + [WAIT] * len(after),
        out_specs=out,
        out_shape=jax.ShapeDtypeStruct((shard_rows, dim), F32),
        input_output_aliases={2: 0} if before else {},
        compiler_params=pltpu.CompilerParams(vmem_limit_bytes=VMEM_LIMIT),
        name="store_sum",
    )(asked.reshape(1, count), returned, *before, *after)


def all_to_all(array):
    return lax.all_to_all(array, RANKS, split_axis=0, concat_axis=0, tiled=True)


def on_device(
    tokens,
    seg_ids,
    live_mask,
    ret_rows,
    enc_store,
    attn_in,
    attn_out,
    ff_in,
    ff_out,
    biases,
    ln_gain,
    ln_shift,
    ff_bias,
    cotangent,
):
    n_rows = lax.axis_size("row")
    n_cols = lax.axis_size("col")
    peers = n_rows * n_cols
    tok_count, dim = tokens.shape
    shard_rows = enc_store.shape[0]
    ret = ret_rows.shape[1]
    slots = 3 * ret_rows.size // (2 * peers)
    rb, cb = attn_in.shape[1], attn_in.shape[2]
    order_a, order_b = bit_orders(n_rows, n_cols)
    n_row_bits = n_rows.bit_length() - 1
    n_far = n_row_bits - 2
    by_rows = n_cols == 2 and rb % 16 == 0 and cb % 128 == 0
    if by_rows:
        col = lax.axis_index("col").astype(jnp.int32)[None]
        place_a = jnp.concatenate([block_of_row(order_a, n_rows), col])
        place_b = jnp.concatenate([block_of_row(order_b, n_rows), col])

    parts = 2
    in_slots = (
        slots % (16 * parts) == 0
        and peers % GROUP == 0
        and tok_count % LANES == 0
        and tok_count <= 256
        and shard_rows & (shard_rows - 1) == 0
        and H <= PITCH
    )
    parts = parts if in_slots else 1
    attention = (SlotAttention if in_slots else GatheredAttention)(
        ret_rows, shard_rows, peers, slots, dim, parts
    )
    def vector_rows(parts):
        parts = [jnp.pad(part, ((0, 0), (0, cb - part.shape[1]))) for part in parts]
        return jnp.pad(jnp.concatenate(parts, axis=0), ((0, 2), (0, 0)))

    small = vector_rows([biases, ln_gain, ln_shift, ff_bias.reshape(1, -1)])
    cut = 8 * rb + small.shape[0]
    side_a, side_b = join(attn_in, attn_out, small, ff_in, ff_out)
    side_a, side_b = gather_bits(side_a, order_a[:n_far]), gather_bits(side_b, order_b[:n_far])
    asked = all_to_all(attention.wanted)

    answers = [
        enc_store[jnp.maximum(attention.part(asked, c) - 1, 0)] for c in range(parts)
    ]
    if by_rows:
        answers[0] = hold(answers[0], [side_a, side_b])
    side_a = gather_bits(side_a, order_a[n_far : n_far + 1])
    side_b = gather_bits(side_b, order_b[n_far : n_far + 1])
    arrived = [all_to_all(answers[0])]
    for c in range(1, parts):
        if by_rows:
            side_a = hold(side_a, [answers[c]])
            side_b = hold(side_b, [answers[c]])
            answers[c] = hold(answers[c], arrived[-1:])
        arrived.append(all_to_all(answers[c]))
    if by_rows:
        side_a = gather_bits(side_a, order_a[n_far + 1 : n_row_bits])
        side_b = gather_bits(side_b, order_b[n_far + 1 : n_row_bits])
        other_a, other_b = swap_bit(side_a, "col", 1), swap_bit(side_b, "col", 1)
        tile = (rb, cb)
        mats, small_all = unpack(side_a, other_a, place_a, 8, tile, extra=small.shape[0])
        w_ff1 = unpack(side_b, other_b, place_b, 4, tile, beside=True)[0]
        w_ff2 = unpack(side_b, other_b, place_b, 1, (4 * rb, cb), first=4 * rb)[0]
    else:
        side_a = gather_bits(side_a, order_a[n_far + 1 :])
        side_b = gather_bits(side_b, order_b[n_far + 1 :])
        mats, small_all = unpack_any(side_a, order_a, n_rows, n_cols, rb)
        mats = mats.transpose(2, 0, 3, 1, 4).reshape(8, dim, dim)
        ff_blocks, _ = unpack_any(side_b, order_b, n_rows, n_cols, rb)
        w_ff1 = ff_blocks[:, :, :4].transpose(0, 3, 1, 2, 4).reshape(dim, 4 * dim)
        w_ff2 = ff_blocks[:, :, 4:].transpose(0, 2, 3, 1, 4).reshape(4 * dim, dim)
    w_q, w_k, w_v, w_cq, w_ck, w_cv, w_o, w_co = (mats[i] for i in range(8))
    small_all = small_all.astype(F32)
    vectors = small_all[:, :13, :rb].transpose(1, 0, 2).reshape(13, dim)
    bias_all, gain_all, shift_all = vectors[:7], vectors[7:10], vectors[10:]
    bias_ff = small_all[:, 13, : ff_bias.size].reshape(-1)

    def heads(array):
        return array.reshape(tok_count, H, HD)

    queries = heads((mm(tokens, w_q) + bias_all[0]).astype(BF))
    key_rows = heads(mm(tokens, w_k).astype(BF))
    values = heads((mm(tokens, w_v) + bias_all[1]).astype(BF))
    visible = visible_mask(seg_ids[0], live_mask[0])
    scores = jnp.einsum("qhd,khd->hqk", queries, key_rows, preferred_element_type=F32) * 0.125
    probs = jax.nn.softmax(jnp.where(visible[None], scores, -1e30), axis=-1)
    probs_low = probs.astype(BF)
    mixed = jnp.einsum("hqk,khd->qhd", probs_low, values, preferred_element_type=F32)
    mixed = mixed.reshape(tok_count, dim).astype(BF)
    branch = mm(mixed, w_o) + bias_all[2]
    first, first_norm, first_scale = norm_fwd(
        tokens.astype(F32) + branch, gain_all[0], shift_all[0]
    )
    first_low = first.astype(BF)
    cross_q = (mm(first_low, w_cq) + bias_all[3]).astype(BF)

    attention.prepare(cross_q)
    cross_low = attention.forward(arrived, w_ck, w_cv, bias_all[4])
    branch_two = mm(cross_low, w_co) + bias_all[5]
    second, second_norm, second_scale = norm_fwd(first + branch_two, gain_all[1], shift_all[1])
    second_low = second.astype(BF)

    hidden_act, hidden_slope = gelu_parts(mm(second_low, w_ff1) + bias_ff)
    hidden_low = hidden_act.astype(BF)
    branch_ffn = mm(hidden_low, w_ff2) + bias_all[6]
    final, final_norm, final_scale = norm_fwd(second + branch_ffn, gain_all[2], shift_all[2])
    output = final.astype(BF)
    cot = cotangent.astype(F32)
    grad_three = norm_back(cot, final_norm, final_scale, gain_all[2])
    grad_y = grad_three.astype(BF)
    grad_pre = (mm_nt(grad_y, w_ff2) * hidden_slope).astype(BF)
    grad_second = grad_three + mm_nt(grad_pre, w_ff1)
    grad_two = norm_back(grad_second, second_norm, second_scale, gain_all[1])
    grad_o2 = grad_two.astype(BF)
    grad_cmix = mm_nt(grad_o2, w_co).astype(BF)
    attention.backward(grad_cmix)
    send_back = [attention.send(0)]

    def packed(order, place, mats, small=None, after=()):
        if by_rows:
            return pack(mats, place, small, after)
        return pack_any(mats, order[::-1], small, n_rows, n_cols)

    tile = (rb, cb)
    near = len(order_a) - n_far
    back_a, back_b = order_a[::-1], order_b[::-1]
    at_a, at_b = (place_a, place_b) if by_rows else (None, None)
    send_back += [attention.send(c, send_back) for c in range(1, parts)]
    grad_cq, grad_wk, grad_wv = attention.finish()
    ff = [
        (order_a, at_a, [((second_low, grad_pre), tile, 4)]),
        (order_b, at_b, [((hidden_low, grad_y), (4 * rb, cb), 1)]),
    ]
    ff = [packed(*part, None, [grad_cq]) for part in ff]
    grad_first = grad_two + mm_nt(grad_cq, w_cq)
    grad_one = norm_back(grad_first, first_norm, first_scale, gain_all[0])
    grad_o = grad_one.astype(BF)
    grad_mix = heads(mm_nt(grad_o, w_o).astype(BF))
    grad_probs = jnp.einsum("qhd,khd->hqk", grad_mix, values, preferred_element_type=F32)
    grad_v = jnp.einsum("hqk,qhd->khd", probs_low, grad_mix, preferred_element_type=F32)
    grad_scores = (
        probs * (grad_probs - jnp.sum(probs * grad_probs, axis=-1, keepdims=True))
    ).astype(BF)
    grad_q = jnp.einsum("hqk,khd->qhd", grad_scores, key_rows, preferred_element_type=F32) * 0.125
    grad_k = jnp.einsum("hqk,qhd->khd", grad_scores, queries, preferred_element_type=F32) * 0.125
    grad_q, grad_k, grad_v = (
        part.reshape(tok_count, dim).astype(BF) for part in (grad_q, grad_k, grad_v)
    )
    grad_tokens = (
        grad_one + mm_nt(grad_q, w_q) + mm_nt(grad_k, w_k) + mm_nt(grad_v, w_v)
    )

    vectors, wide = vector_sums(
        [grad_q, grad_v, grad_o, grad_cq, grad_cmix, grad_o2, grad_y],
        [(grad_first, first_norm), (grad_second, second_norm), (cotangent, final_norm)],
        grad_pre,
    )
    vectors = vectors[:13].reshape(13, n_rows, rb).transpose(1, 0, 2)
    wide = wide.reshape(n_rows, 1, -1)
    grad_small = [
        jnp.pad(vectors, ((0, 0), (0, 0), (0, cb - rb))),
        jnp.pad(wide, ((0, 0), (0, 2), (0, cb - ff_bias.size))),
    ]
    grad_small = jnp.concatenate(grad_small, axis=1).astype(BF)
    attn_one = packed(
        order_a,
        at_a,
        [
            ((tokens, grad_q), tile, 1),
            ((tokens, grad_k), tile, 1),
            ((tokens, grad_v), tile, 1),
            ((first_low, grad_cq), tile, 1),
        ],
    )
    attn_two = packed(
        order_b,
        at_b,
        [
            (grad_wk, tile, 1),
            (grad_wv, tile, 1),
            ((mixed, grad_o), tile, 1),
            ((cross_low, grad_o2), tile, 1),
        ],
        grad_small,
    )
    if by_rows:
        send_back[1:] = [hold(part, [*attn_one, *attn_two]) for part in send_back[1:]]
    returned = [all_to_all(part) for part in send_back]

    def stored(c, so_far, after):
        rows = returned[c].reshape(-1, dim)
        return store_sum(attention.part(asked, c), rows, shard_rows, so_far, after)

    def join_pairs(one, two):
        return tuple(jnp.concatenate(both, axis=1) for both in zip(one, two))

    ff = [scatter_bits(*part, back[:near]) for part, back in zip(ff, (back_a, back_b))]
    ff = join_pairs(*ff)
    def behind(pair, array):
        return (hold(pair[0], [array]), pair[1]) if by_rows else pair

    attn = [
        scatter_bits(*part, back[: near - 2])
        for part, back in zip((attn_one, attn_two), (back_a, back_b))
    ]
    grad_store = None
    for c in range(parts - 1):
        grad_store = stored(c, grad_store, ())
        attn = [behind(pair, grad_store) for pair in attn]
    attn = [
        scatter_bits(*part, back[near - 2 : near]) for part, back in zip(attn, (back_a, back_b))
    ]
    grad_store = stored(parts - 1, grad_store, ())
    attn = behind(join_pairs(*attn), grad_store)
    total_a, total_b = (
        (keep + swap_bit(send, *order_a[0]))[0].astype(F32)
        for keep, send in (scatter_bits(*pair, back_a[near:-1]) for pair in (attn, ff))
    )

    sum_small = total_a[8 * rb :]
    return (
        output,
        grad_tokens,
        grad_store,
        total_a[: 6 * rb].reshape(6, rb, cb),
        total_a[6 * rb : 8 * rb].reshape(2, rb, cb),
        jnp.concatenate([total_b[k * rb : (k + 1) * rb] for k in range(4)], axis=1),
        total_b[4 * rb :],
        sum_small[:7, :rb],
        sum_small[7:10, :rb],
        sum_small[10:13, :rb],
        sum_small[13, : ff_bias.size],
    )


def solution(mesh):
    both = ("row", "col")
    return jax.shard_map(
        on_device,
        mesh=mesh,
        in_specs=(
            P(both, None),
            P(both, None),
            P(both, None),
            P(both, None),
            P(both, None),
            P(None, "row", "col"),
            P(None, "row", "col"),
            P("row", "col"),
            P("row", "col"),
            P(None, "row"),
            P(None, "row"),
            P(None, "row"),
            P("row"),
            P(both, None),
        ),
        out_specs=(
            P(both, None),
            P(both, None),
            P(both, None),
            P(None, "row", "col"),
            P(None, "row", "col"),
            P("row", "col"),
            P("row", "col"),
            P(None, "row"),
            P(None, "row"),
            P(None, "row"),
            P("row"),
        ),
        check_vma=False,
    )
```

```python
import functools

import jax
import jax.numpy as jnp
import numpy as np
from jax import lax
from jax.experimental import pallas as pl
from jax.experimental.pallas import tpu as pltpu
from jax.sharding import PartitionSpec as P

H = 12
HD = 64
RANKS = ("row", "col")
BF = jnp.bfloat16
F32 = jnp.float32
VMEM_LIMIT = 60 * 1024 * 1024


def mm(a, b):
    return jnp.dot(a, b, preferred_element_type=F32)


def mm_nt(a, b):
    return lax.dot_general(a, b, (((1,), (1,)), ((), ())), preferred_element_type=F32)


def mm_tn(a, b):
    return lax.dot_general(a, b, (((0,), (0,)), ((), ())), preferred_element_type=F32)


def norm_fwd(resid, gain, shift):
    row_mean = jnp.mean(resid, axis=-1, keepdims=True)
    centered = resid - row_mean
    inv_std = lax.rsqrt(jnp.mean(centered * centered, axis=-1, keepdims=True) + 1e-05)
    normed = centered * inv_std
    return (normed * gain + shift, normed, inv_std)


def norm_back(grad_in, normed, inv_std, gain):
    scaled = grad_in * gain
    return inv_std * (
        scaled
        - jnp.mean(scaled, axis=-1, keepdims=True)
        - normed * jnp.mean(scaled * normed, axis=-1, keepdims=True)
    )


def gelu_parts(pre_act):
    cdf_part = 0.5 * (1.0 + lax.erf(pre_act * 0.7071067811865476))
    density = jnp.exp(-0.5 * pre_act * pre_act) * 0.3989422804014327
    return (pre_act * cdf_part, cdf_part + pre_act * density)


def column_sum(array):
    return jnp.sum(array.astype(F32), axis=0)


def bit_orders(n_rows, n_cols):
    row_bits = [("row", 1 << b) for b in reversed(range(n_rows.bit_length() - 1))]
    col_bits = [("col", 1 << b) for b in reversed(range(n_cols.bit_length() - 1))]
    swapped = row_bits[:-2] + row_bits[-1:] + row_bits[-2:-1]
    return row_bits + col_bits, swapped + col_bits


def swap_bit(array, axis, bit):
    pairs = [(i, i ^ bit) for i in range(lax.axis_size(axis))]
    return lax.ppermute(array, axis, pairs)


def gather_bits(blocks, order):
    for axis, bit in order:
        blocks = jnp.concatenate([blocks, swap_bit(blocks, axis, bit)], axis=0)
    return blocks


def scatter_bits(keep, send, order):
    for axis, bit in order:
        got = swap_bit(send, axis, bit)
        half = keep.shape[0] // 2
        keep, send = keep[:half] + got[:half], keep[half:] + got[half:]
    return keep, send


def block_of_row(order, n_rows):
    apart = np.zeros(n_rows, np.int32)
    for k, (_, bit) in enumerate(order[: n_rows.bit_length() - 1]):
        apart[(np.arange(n_rows) >> k) & 1 == 1] ^= bit
    table = np.zeros(n_rows, np.int32)
    table[apart] = np.arange(n_rows)
    return jnp.asarray(table)[lax.axis_index("row") ^ jnp.arange(n_rows, dtype=jnp.int32)]


def flip_by_position(blocks, stages):
    for k, (axis, bit) in enumerate(stages):
        here = (lax.axis_index(axis) & bit) != 0
        blocks = jnp.where(here, jnp.flip(blocks, axis=k), blocks)
    return blocks


def by_device(blocks, order):
    stages = order[::-1]
    shape = blocks.shape[1:]
    blocks = flip_by_position(blocks.reshape((2,) * len(stages) + shape), stages)
    rank = sorted(range(len(stages)), key=lambda k: (stages[k][0] == "col", -stages[k][1]))
    rest = list(range(len(stages), blocks.ndim))
    return blocks.transpose(rank + rest).reshape((-1,) + shape)


def by_stage(blocks, stages):
    shape = blocks.shape[1:]
    rank = sorted(range(len(stages)), key=lambda k: (stages[k][0] == "col", -stages[k][1]))
    rest = list(range(len(stages), len(stages) + len(shape)))
    back = [rank.index(k) for k in range(len(stages))]
    blocks = blocks.reshape((2,) * len(stages) + shape).transpose(back + rest)
    return flip_by_position(blocks, stages).reshape((-1,) + shape)


def cost(micros):
    return pl.CostEstimate(flops=int(micros * 1.1e9), bytes_accessed=0, transcendentals=0)


WAIT = pl.BlockSpec(memory_space=pltpu.HBM)


def in_hbm(shape, dtype):
    return pltpu.HBM(shape=shape, dtype=dtype)


def from_hbm(array):
    return pltpu.with_memory_space_constraint(array, pltpu.HBM)


def tie_kernel(*refs):
    refs[-1][...] = refs[0][...]


def tie(array, after):
    return pl.pallas_call(
        tie_kernel,
        in_specs=[pl.BlockSpec(memory_space=pltpu.VMEM)] + [WAIT] * len(after),
        out_shape=jax.ShapeDtypeStruct(array.shape, array.dtype),
        name="tie",
    )(array, *after)


def hold_kernel(*refs):
    del refs


def hold(array, after):
    return pl.pallas_call(
        hold_kernel,
        in_specs=[WAIT] * (1 + len(after)),
        out_specs=WAIT,
        out_shape=jax.ShapeDtypeStruct(array.shape, array.dtype),
        input_output_aliases={0: 0},
        name="hold",
    )(array, *after)


def tile_of(buf, k, r, c, shape):
    rows, cols = shape
    return buf.at[
        k, pl.ds(pl.multiple_of(r * rows, rows), rows), pl.ds(pl.multiple_of(c * cols, cols), cols)
    ]


def unpack_kernel(place, own, other, *refs, count, shape, extra):
    outs, (buf, *more) = refs[: 1 + bool(extra)], refs[1 + bool(extra) :]
    sems = more[-1]
    n_rows, col, rows = own.shape[0], place[own.shape[0]], shape[0]

    def fill(r, carry):
        j = place[r]
        for src, c, sem in ((own, col, 0), (other, 1 - col, 1)):
            for k in range(count):
                part = src.at[j, pl.ds(k * rows, rows)]
                pltpu.make_async_copy(part, tile_of(buf, k, r, c, shape), sems.at[sem]).start()
        if extra:
            tail = own.at[j, pl.ds(count * rows, extra)]
            pltpu.make_async_copy(tail, more[0].at[r], sems.at[2]).start()
        return carry

    lax.fori_loop(0, n_rows, fill, 0)
    body = own.at[:, pl.ds(0, count * rows)]
    for sem in range(2):
        pltpu.make_async_copy(body, body, sems.at[sem]).wait()
    out = pltpu.make_async_copy(buf, outs[0], sems.at[3])
    out.start()
    if extra:
        pltpu.make_async_copy(more[0], more[0], sems.at[2]).wait()
        tails = pltpu.make_async_copy(more[0], outs[1], sems.at[4])
        tails.start()
        tails.wait()
    out.wait()


def unpack(own, other, place, count, shape, extra=0):
    n_rows = own.shape[0]
    rows, cols = shape
    whole = jax.ShapeDtypeStruct((count, n_rows * rows, 2 * cols), BF)
    tails = jax.ShapeDtypeStruct((n_rows, extra, cols), BF)
    shapes = [whole] + [tails] * bool(extra)
    got = pl.pallas_call(
        functools.partial(unpack_kernel, count=count, shape=shape, extra=extra),
        in_specs=[pl.BlockSpec(memory_space=pltpu.SMEM)] + [pl.BlockSpec(memory_space=pl.ANY)] * 2,
        out_specs=[pl.BlockSpec(memory_space=pl.ANY)] * len(shapes),
        out_shape=shapes,
        scratch_shapes=[pltpu.VMEM(x.shape, BF) for x in shapes] + [pltpu.SemaphoreType.DMA((5,))],
        compiler_params=pltpu.CompilerParams(vmem_limit_bytes=32 * 1024 * 1024),
        cost_estimate=pl.CostEstimate(
            flops=0, bytes_accessed=4 * whole.size * 2, transcendentals=0
        ),
        name="unpack",
    )(place, own, other)
    return got if extra else got[0]


def join_kernel(attn_in, attn_out, small, waited, one, two, *, rb):
    del waited
    for k in range(4):
        one[0, k * rb : (k + 1) * rb] = attn_in[k]
    for k in range(2):
        two[0, k * rb : (k + 1) * rb] = attn_in[4 + k]
        two[0, (2 + k) * rb : (3 + k) * rb] = attn_out[k]
    two[0, 4 * rb :] = small[...]


def join(attn_in, attn_out, small, after):
    rb, cb = attn_in.shape[1:]
    if rb % 16 or cb % 128:
        two = [attn_in[4:].reshape(-1, cb), attn_out.reshape(-1, cb), small]
        return attn_in[:4].reshape(1, -1, cb), jnp.concatenate(two, axis=0)[None]
    return pl.pallas_call(
        functools.partial(join_kernel, rb=rb),
        in_specs=[pl.BlockSpec(memory_space=pltpu.VMEM)] * 3 + [WAIT],
        out_shape=(
            jax.ShapeDtypeStruct((1, 4 * rb, cb), BF),
            jax.ShapeDtypeStruct((1, 4 * rb + small.shape[0], cb), BF),
        ),
        name="join",
    )(attn_in, attn_out, small, after)


def pack_kernel(place, *refs, mats, rows, extra, waits):
    n_ops = 1 + max(max(mat[0]) for mat in mats)
    ops, refs = refs[:n_ops], refs[n_ops:]
    small, refs = refs[: bool(extra)], refs[bool(extra) + waits :]
    keep, send, *bufs, sems = refs
    n_rows, col = keep.shape[0], place[keep.shape[0]]
    loads = {}
    for k, (at, _, _) in enumerate(mats):
        if len(at) == 1:
            loads[k] = pltpu.make_async_copy(ops[at[0]], bufs[k].at[0], sems.at[2 + k])
            loads[k].start()
    for k, (at, _, _) in enumerate(mats):
        if len(at) == 2:
            left, right = ops[at[0]], ops[at[1]]
            _, tall, wide = bufs[k].shape
            tile = min(tall, wide)
            for i in range(0, tall, tile):
                for j in range(0, wide, tile):
                    got = mm_tn(left[:, i : i + tile], right[:, j : j + tile])
                    bufs[k][0, i : i + tile, j : j + tile] = got.astype(BF)
    for load in loads.values():
        load.wait()

    def spread(r, carry):
        j = place[r]
        for dst, c, sem in ((keep, col, 0), (send, 1 - col, 1)):
            first = 0
            for buf, (_, shape, beside) in zip(bufs, mats):
                for k in range(beside):
                    part = dst.at[j, pl.ds(first, shape[0])]
                    tile = tile_of(buf, 0, r, c * beside + k, shape)
                    pltpu.make_async_copy(tile, part, sems.at[sem]).start()
                    first += shape[0]
            if extra:
                tail = dst.at[j, pl.ds(first, extra)]
                pltpu.make_async_copy(small[0].at[r], tail, sems.at[sem]).start()
        return carry

    lax.fori_loop(0, n_rows, spread, 0)
    for dst, sem in ((keep, 0), (send, 1)):
        pltpu.make_async_copy(dst, dst, sems.at[sem]).wait()


def pack(mats, place, small=None, after=()):
    ops, parts, specs, bufs, flops, total = [], [], [], [], 0, 0
    for mat, shape, beside in mats:
        mat = mat if isinstance(mat, tuple) else (mat,)
        parts.append((tuple(range(len(ops), len(ops) + len(mat))), shape, beside))
        ops += mat
        specs += [pl.BlockSpec(memory_space=pltpu.VMEM if len(mat) == 2 else pl.ANY)] * len(mat)
        whole = (mat[0].shape[1], mat[1].shape[1]) if len(mat) == 2 else mat[0].shape
        bufs.append(pltpu.VMEM((1,) + tuple(whole), BF))
        flops += 2 * mat[0].shape[0] * whole[0] * whole[1] if len(mat) == 2 else 0
        total += beside * shape[0]
        n_rows = whole[0] // shape[0]
    extra = 0 if small is None else small.shape[1]
    block = in_hbm((n_rows, total + extra, shape[1]), BF)
    if extra:
        ops.append(small)
        specs.append(pl.BlockSpec(memory_space=pltpu.VMEM))
    return pl.pallas_call(
        functools.partial(
            pack_kernel, mats=tuple(parts), rows=total, extra=extra, waits=len(after)
        ),
        in_specs=[pl.BlockSpec(memory_space=pltpu.SMEM)] + specs + [WAIT] * len(after),
        out_specs=[pl.BlockSpec(memory_space=pl.ANY)] * 2,
        out_shape=[block, block],
        scratch_shapes=bufs + [pltpu.SemaphoreType.DMA((2 + len(mats),))],
        compiler_params=pltpu.CompilerParams(vmem_limit_bytes=48 * 1024 * 1024),
        cost_estimate=pl.CostEstimate(
            flops=flops, bytes_accessed=8 * n_rows * total * shape[1], transcendentals=0
        ),
        name="pack",
    )(place, *ops, *after)


def unpack_any(blocks, order, count, shape, extra, n_rows, n_cols):
    rows, cols = shape
    got = by_device(blocks, order).reshape(n_rows, n_cols, -1, cols)
    mats = got[:, :, : count * rows].reshape(n_rows, n_cols, count, rows, cols)
    mats = mats.transpose(2, 0, 3, 1, 4).reshape(count, n_rows * rows, n_cols * cols)
    return (mats, got[:, 0, count * rows :]) if extra else mats


def pack_any(mats, order, small, n_rows, n_cols):
    got = []
    for mat, (rows, cols), beside in mats:
        mat = mm_tn(*mat).astype(BF) if isinstance(mat, tuple) else mat
        mat = mat.reshape(n_rows, rows, n_cols, beside, cols).transpose(0, 2, 3, 1, 4)
        got.append(mat.reshape(n_rows, n_cols, beside * rows, cols))
    if small is not None:
        got.append(jnp.broadcast_to(small[:, None], (n_rows, n_cols) + small.shape[1:]))
    got = jnp.concatenate(got, axis=2)
    got = by_stage(got.reshape((-1,) + got.shape[2:]), order)
    half = got.shape[0] // 2
    return got[:half], got[half:]


def plan_requests(ret_rows, shard_rows, peers, slots):
    flat = ret_rows.reshape(-1)
    count = flat.shape[0]
    owner = flat // shard_rows
    local_row = flat - owner * shard_rows
    mine = owner[:, None] == jnp.arange(peers, dtype=jnp.int32)[None, :]
    run = 256
    runs = count // run
    ones = mine.astype(BF).reshape(runs, run, peers)
    lower = jnp.tril(jnp.ones((run, run), BF))
    within = jnp.einsum("ij,bjo->bio", lower, ones, preferred_element_type=F32)
    totals = within[:, -1, :]
    before = jnp.cumsum(totals, axis=0) - totals
    upto = (within + before[:, None, :]).reshape(count, peers)
    rank = jnp.sum(jnp.where(mine, upto, 0.0), axis=1).astype(jnp.int32) - 1
    place = owner * slots + rank
    row_code = local_row + 1
    entry_code = jnp.arange(count, dtype=jnp.int32)
    digits = jnp.stack([row_code // 64, row_code % 64, entry_code // 64, entry_code % 64])
    left = jnp.where(mine.T[None], digits[:, None, :], 0).astype(BF)
    at_rank = (rank[:, None] == jnp.arange(slots, dtype=jnp.int32)[None, :]).astype(BF)
    codes = mm(left.reshape(4 * peers, count), at_rank).astype(jnp.int32).reshape(4, peers, slots)
    return place, codes[0] * 64 + codes[1], codes[2] * 64 + codes[3]


def row_norm(resid):
    centered = resid - jnp.mean(resid, axis=-1, keepdims=True)
    scale = lax.rsqrt(jnp.mean(centered * centered, axis=-1, keepdims=True) + 1e-05)
    return centered * scale, scale


def head_masks():
    lane = lax.broadcasted_iota(jnp.int32, (1, 2 * HD), 1)
    return [(lane // HD == i).astype(F32).astype(BF) for i in range(2)]


def self_probs(query, key, visible):
    scores = jnp.where(visible, mm_nt(query, key) * (HD**-0.5), -1e30)
    expo = jnp.exp(scores - jnp.max(scores, axis=-1, keepdims=True))
    return expo / jnp.sum(expo, axis=-1, keepdims=True)


def visible_pairs(seg_col, seg_row, live_row):
    shape = (seg_col.shape[0], seg_row.shape[1])
    at_query = lax.broadcasted_iota(jnp.int32, shape, 0)
    at_key = lax.broadcasted_iota(jnp.int32, shape, 1)
    return (
        (at_key <= at_query)
        & (seg_col[...] == seg_row[...])
        & ((live_row[...] == 1) | (at_key == at_query))
    )


def self_fwd_kernel(*refs):
    tokens, seg_col, seg_row, live_row, w_qkvc, w_o, bias, gain, shift = refs[:9]
    queries, keys, values, mixed, first, normed, scale, cross_q = refs[9:]
    x = tokens[...]
    queries[...] = (mm(x, w_qkvc[0]) + bias[0:1]).astype(BF)
    keys[...] = mm(x, w_qkvc[1]).astype(BF)
    values[...] = (mm(x, w_qkvc[2]) + bias[1:2]).astype(BF)
    visible = visible_pairs(seg_col, seg_row, live_row)
    for pair in range(H // 2):
        lanes = slice(2 * HD * pair, 2 * HD * (pair + 1))
        total = 0.0
        for mask in head_masks():
            prob = self_probs(queries[:, lanes], keys[:, lanes] * mask, visible)
            total = total + mm(prob.astype(BF), values[:, lanes] * mask)
        mixed[:, lanes] = total.astype(BF)
    resid = x.astype(F32) + mm(mixed[...], w_o[...]) + bias[2:3]
    norm, inv = row_norm(resid)
    normed[...] = norm
    scale[...] = jnp.broadcast_to(inv, scale.shape)
    out = norm * gain[0:1] + shift[0:1]
    first[...] = out
    cross_q[...] = (mm(out.astype(BF), w_qkvc[3]) + bias[3:4]).astype(BF)


def self_fwd(tokens, seg, live, w_qkvc, w_o, bias, gain, shift):
    toks, dim = tokens.shape
    low = jax.ShapeDtypeStruct((toks, dim), BF)
    full = jax.ShapeDtypeStruct((toks, dim), F32)
    column = jax.ShapeDtypeStruct((toks, 128), F32)
    return pl.pallas_call(
        self_fwd_kernel,
        out_shape=(low, low, low, low, full, full, column, low),
        compiler_params=pltpu.CompilerParams(vmem_limit_bytes=28 * 1024 * 1024),
        cost_estimate=cost(5),
        name="self_fwd",
    )(tokens, seg.reshape(toks, 1), seg, live, w_qkvc, w_o, bias, gain, shift)


def self_bwd_kernel(*refs):
    grad_cq, grad_two, normed, scale, gain, queries, keys, values = refs[:8]
    seg_col, seg_row, live_row, w_qkvc, w_o = refs[8:13]
    grad_first, grad_one, grad_o, grad_q, grad_k, grad_v, grad_mix = refs[13:]
    incoming = grad_two[...] + mm_nt(grad_cq[...], w_qkvc[3])
    grad_first[...] = incoming
    one = norm_back(incoming, normed[...], scale[:, 0:1], gain[0:1])
    grad_one[...] = one
    low = one.astype(BF)
    grad_o[...] = low
    grad_mix[...] = mm_nt(low, w_o[...]).astype(BF)
    visible = visible_pairs(seg_col, seg_row, live_row)
    for pair in range(H // 2):
        lanes = slice(2 * HD * pair, 2 * HD * (pair + 1))
        by_query, by_key, by_value = 0.0, 0.0, 0.0
        for mask in head_masks():
            query, key = queries[:, lanes] * mask, keys[:, lanes] * mask
            grad = grad_mix[:, lanes] * mask
            prob = self_probs(query, key, visible)
            grad_p = mm_nt(grad, values[:, lanes])
            dot = jnp.sum(prob * grad_p, axis=-1, keepdims=True)
            grad_s = (prob * (grad_p - dot)).astype(BF)
            by_query = by_query + mm(grad_s, key)
            by_key = by_key + mm_tn(grad_s, query)
            by_value = by_value + mm_tn(prob.astype(BF), grad)
        grad_q[:, lanes] = (by_query * (HD**-0.5)).astype(BF)
        grad_k[:, lanes] = (by_key * (HD**-0.5)).astype(BF)
        grad_v[:, lanes] = by_value.astype(BF)


def self_bwd(grad_cq, grad_two, normed, scale, gain, qkv, seg, live, w_qkvc, w_o):
    toks, dim = grad_two.shape
    low = jax.ShapeDtypeStruct((toks, dim), BF)
    full = jax.ShapeDtypeStruct((toks, dim), F32)
    return pl.pallas_call(
        self_bwd_kernel,
        out_shape=(full, full, low, low, low, low),
        scratch_shapes=[pltpu.VMEM((toks, dim), BF)],
        compiler_params=pltpu.CompilerParams(vmem_limit_bytes=28 * 1024 * 1024),
        cost_estimate=cost(6),
        name="self_bwd",
    )(grad_cq, grad_two, normed, scale, gain, *qkv, seg.reshape(toks, 1), seg, live, w_qkvc, w_o)


def own_rows(tokens, ret, heads):
    shape = (heads * tokens, tokens * ret)
    row_tok = lax.broadcasted_iota(jnp.int32, shape, 0) % tokens
    col_tok = lax.broadcasted_iota(jnp.int32, shape, 1) // ret
    return row_tok == col_tok


def cross_fwd_kernel(qk, fetched, mix, probs, *, ret):
    heads, tokens, dim = qk.shape
    own = own_rows(tokens, ret, heads)
    query = qk[...].reshape(heads * tokens, dim)
    rows = fetched[...]
    scores = jnp.where(own, mm_nt(query, rows) * 0.125, -1e30)
    expo = jnp.exp(scores - jnp.max(scores, axis=-1, keepdims=True))
    prob = expo / jnp.sum(expo, axis=-1, keepdims=True)
    probs[0] = prob
    mix[...] = mm(prob.astype(BF), rows).astype(BF).reshape(heads, tokens, dim)


def cross_bwd_kernel(qk, gmix, fetched, probs, grad_rows, grad_s, *, ret):
    heads, tokens, dim = qk.shape
    query = qk[...].reshape(heads * tokens, dim)
    grad_mix = gmix[...].reshape(heads * tokens, dim)
    prob = probs[0]
    grad_p = mm_nt(grad_mix, fetched[...])
    g_s = (prob * (grad_p - jnp.sum(prob * grad_p, axis=-1, keepdims=True))).astype(BF)
    grad_s[0] = g_s
    grad_rows[...] = (
        mm_tn(prob.astype(BF), grad_mix) + mm_tn(g_s, query) * 0.125
    ).astype(BF)


def cross_back_q_kernel(grad_s, fetched, grad_qk):
    heads, tokens, dim = grad_qk.shape
    got = mm(grad_s[0], fetched[...]) * 0.125
    grad_qk[...] = got.astype(BF).reshape(heads, tokens, dim)


def cross_calls(tok_count, ret, dim):
    tb = 16
    blocks = tok_count // tb
    by_head = pl.BlockSpec((H, tb, dim), lambda g: (0, g, 0))
    rows = pl.BlockSpec((tb * ret, dim), lambda g: (g, 0))
    square = pl.BlockSpec((1, H * tb, tb * ret), lambda g: (g, 0, 0))
    heads_shape = jax.ShapeDtypeStruct((H, tok_count, dim), BF)
    square_f32 = jax.ShapeDtypeStruct((blocks, H * tb, tb * ret), F32)
    square_bf = jax.ShapeDtypeStruct((blocks, H * tb, tb * ret), BF)
    params = pltpu.CompilerParams(vmem_limit_bytes=VMEM_LIMIT)
    fwd = pl.pallas_call(
        functools.partial(cross_fwd_kernel, ret=ret),
        grid=(blocks,),
        in_specs=[by_head, rows],
        out_specs=[by_head, square],
        out_shape=(heads_shape, square_f32),
        compiler_params=params,
        name="cross_fwd",
    )
    bwd = pl.pallas_call(
        functools.partial(cross_bwd_kernel, ret=ret),
        grid=(blocks,),
        in_specs=[by_head, by_head, rows, square],
        out_specs=[rows, square],
        out_shape=(jax.ShapeDtypeStruct((tok_count * ret, dim), BF), square_bf),
        compiler_params=params,
        name="cross_bwd",
    )
    back_q = pl.pallas_call(
        cross_back_q_kernel,
        grid=(blocks,),
        in_specs=[square, rows],
        out_specs=by_head,
        out_shape=heads_shape,
        compiler_params=params,
        name="cross_back_q",
    )
    return fwd, bwd, back_q


GROUP = 8
LANES = 128
PITCH = LANES // GROUP


def plan_kernel(rows, wanted, token, at_rank, owner, *, shard_rows):
    peers, slots = wanted.shape
    ret, toks = rows.shape
    shape = (toks, toks)
    upper = (
        lax.broadcasted_iota(jnp.int32, shape, 0) <= lax.broadcasted_iota(jnp.int32, shape, 1)
    ).astype(BF)
    peer = lax.broadcasted_iota(jnp.int32, (peers, toks), 0)
    tok_code = (lax.broadcasted_iota(jnp.int32, (peers, toks), 1) + 1).astype(F32)
    k_rows = lax.broadcasted_iota(jnp.int32, (at_rank.shape[0], toks), 0)
    shift = shard_rows.bit_length() - 1
    before = jnp.zeros((peers, 1), F32)
    codes = jnp.zeros((3 * peers, at_rank.shape[0]), F32)
    for r in range(ret):
        row = rows[r : r + 1, :]
        own = lax.shift_right_logical(row, shift)
        code = lax.bitwise_and(row, shard_rows - 1) + 1
        mine = own == peer
        upto = mm(mine.astype(BF), upper) + before
        before = upto[:, toks - 1 :]
        rank = jnp.sum(jnp.where(mine, upto, 0.0), axis=0, keepdims=True).astype(jnp.int32) - 1
        at = (k_rows == rank).astype(BF)
        at_rank[:, r * toks : (r + 1) * toks] = at
        owner[r : r + 1, :] = own
        high = lax.shift_right_logical(code, 6).astype(F32)
        low = lax.bitwise_and(code, 63).astype(F32)
        left = jnp.concatenate(
            [
                jnp.where(mine, high, 0.0).astype(BF),
                jnp.where(mine, low, 0.0).astype(BF),
                jnp.where(mine, tok_code, 0.0).astype(BF),
            ],
            axis=0,
        )
        codes = codes + mm_nt(left, at)
    codes = codes[:, :slots].astype(jnp.int32)
    wanted[...] = codes[:peers] * 64 + codes[peers : 2 * peers]
    token[...] = codes[2 * peers :]


def plan_slots(rows, shard_rows, peers, slots):
    ret, toks = rows.shape
    tall = -(-slots // LANES) * LANES
    return pl.pallas_call(
        functools.partial(plan_kernel, shard_rows=shard_rows),
        out_shape=(
            jax.ShapeDtypeStruct((peers, slots), jnp.int32),
            jax.ShapeDtypeStruct((peers, slots), jnp.int32),
            jax.ShapeDtypeStruct((tall, ret * toks), BF),
            jax.ShapeDtypeStruct((ret, toks), jnp.int32),
        ),
        cost_estimate=cost(4),
        name="plan",
    )(rows)


def head_sum(dim):
    shape = (dim, LANES)
    head = lax.broadcasted_iota(jnp.int32, shape, 0) // HD
    return (head == lax.broadcasted_iota(jnp.int32, shape, 1)).astype(BF)


def head_spread(dim):
    shape = (LANES, dim)
    head = lax.broadcasted_iota(jnp.int32, shape, 1) // HD
    return (head == lax.broadcasted_iota(jnp.int32, shape, 0)).astype(BF)


def to_lanes(by_peer, k):
    total = by_peer[:k]
    for q in range(1, GROUP):
        total = total + pltpu.roll(by_peer[q * k : (q + 1) * k], PITCH * q, 1)
    return total


def from_lanes(lanes):
    parts = [lanes] + [pltpu.roll(lanes, LANES - PITCH * q, 1) for q in range(1, GROUP)]
    return jnp.concatenate([part.astype(BF) for part in parts], axis=0)


def to_entries(slot_vals, at_rank, owner):
    k, wide = slot_vals.shape
    tall, toks = at_rank.shape[0], owner.shape[1]
    peers = wide // PITCH
    full = jnp.concatenate([slot_vals, jnp.zeros((tall - k, wide), F32)], axis=0).T
    high = full.astype(BF)
    low = (full - high.astype(F32)).astype(BF)
    peer = lax.broadcasted_iota(jnp.int32, (wide, toks), 0) // PITCH
    out = []
    for r in range(owner.shape[0]):
        at = at_rank[:, r * toks : (r + 1) * toks]
        got = mm(high, at) + mm(low, at)
        got = jnp.where(peer == owner[r : r + 1, :], got, 0.0)
        out.append(jnp.sum(got.reshape(peers, PITCH, toks), axis=0))
    return out


def to_slots(entry_vals, at_rank, owner, peers, slots):
    toks = owner.shape[1]
    wide = peers * PITCH
    peer = lax.broadcasted_iota(jnp.int32, (wide, toks), 0) // PITCH
    total = jnp.zeros((at_rank.shape[0], wide), F32)
    for r, vals in enumerate(entry_vals):
        tiled = jnp.concatenate([vals] * peers, axis=0)
        mine = jnp.where(peer == owner[r : r + 1, :], tiled, 0.0).astype(BF)
        total = total + mm_nt(at_rank[:, r * toks : (r + 1) * toks], mine)
    return total[:slots]


def token_marks_kernel(column, row, marks, marks_t):
    marks[...] = (
        column[...] == lax.broadcasted_iota(jnp.int32, marks.shape, 1) + 1
    ).astype(BF)
    marks_t[...] = (row[...] == lax.broadcasted_iota(jnp.int32, marks_t.shape, 0) + 1).astype(BF)


def query_rows_kernel(token, query, out):
    out[...] = mm(token[...], query[...]).astype(BF).reshape(out.shape)


def rows_in_kernel(arrived, query, w_k, w_v, keys, vals, scores):
    group, k, dim = arrived.shape
    rows = arrived[...].reshape(group * k, dim)
    key = mm(rows, w_k[...])
    keys[...] = key.astype(BF).reshape(group, k, dim)
    prod = (key * query[...].reshape(group * k, dim).astype(F32)).astype(BF)
    scores[...] = to_lanes(mm(prod, head_sum(dim)), k) * 0.125
    vals[...] = mm(rows, w_v[...]).astype(BF).reshape(group, k, dim)


def attend_kernel(
    scores, vals, token_t, at_rank, owner, bias, prob_tok, prob_slot, mixed, total
):
    step, part = pl.program_id(0), pl.program_id(1)
    k, dim = vals.shape[1:]
    slots, wide = scores.shape

    @pl.when((step == 0) & (part == 0))
    def _():
        entry = to_entries(scores[...], at_rank, owner)
        top = functools.reduce(jnp.maximum, entry)
        expo = [jnp.exp(part - top) for part in entry]
        norm = functools.reduce(jnp.add, expo)
        probs = [part / norm for part in expo]
        for r, part in enumerate(probs):
            prob_tok[r * PITCH : (r + 1) * PITCH, :] = part
        prob_slot[...] = to_slots(probs, at_rank, owner, wide // PITCH, slots)
        total[...] = jnp.zeros_like(total)

    lanes = pl.ds(pl.multiple_of(step * LANES, LANES), LANES)
    here = pl.ds(pl.multiple_of(part * k, 16), k)
    prob = mm(from_lanes(prob_slot[here, lanes]), head_spread(dim))
    prod = (prob * vals[...].reshape(-1, dim).astype(F32)).astype(BF)
    total[...] += mm(token_t[...], prod)

    @pl.when((step == pl.num_programs(0) - 1) & (part == pl.num_programs(1) - 1))
    def _():
        mixed[...] = (total[...] + bias[...]).astype(BF)


def attend_back_kernel(
    vals, token, grad, prob_tok, at_rank, owner, grads, grad_slot, slot_p
):
    step, part = pl.program_id(0), pl.program_id(1)
    k, dim = vals.shape[1:]
    slots, wide = slot_p.shape
    lanes = pl.ds(pl.multiple_of(step * LANES, LANES), LANES)
    here = pl.ds(pl.multiple_of(part * k, 16), k)
    rows = mm(token[...], grad[...])
    grads[...] = rows.astype(BF).reshape(vals.shape)
    prod = (rows * vals[...].reshape(-1, dim).astype(F32)).astype(BF)
    slot_p[here, lanes] = to_lanes(mm(prod, head_sum(dim)), k)

    @pl.when((step == pl.num_programs(0) - 1) & (part == pl.num_programs(1) - 1))
    def _():
        entry = to_entries(slot_p[...], at_rank, owner)
        probs = [prob_tok[r * PITCH : (r + 1) * PITCH, :] for r in range(len(entry))]
        dots = functools.reduce(jnp.add, [p * g for p, g in zip(probs, entry)])
        scores = [(p * (g - dots)).astype(BF).astype(F32) for p, g in zip(probs, entry)]
        grad_slot[...] = to_slots(scores, at_rank, owner, wide // PITCH, slots)


def weigh(prob_slot, grad_slot, grad, query):
    dim = grad.shape[2]
    spread = head_spread(dim)
    prob = mm(from_lanes(prob_slot[...]), spread)
    mix = (prob * grad[...].reshape(-1, dim).astype(F32)).astype(BF)
    score = mm(from_lanes(grad_slot[...]), spread) * 0.125
    return mix, (score * query[...].reshape(-1, dim).astype(F32)).astype(BF)


def rows_out_kernel(prob_slot, grad_slot, grad, query, w_k, w_v, out, flag):
    mix, ask = weigh(prob_slot, grad_slot, grad, query)
    out[...] = (mm_nt(mix, w_v[...]) + mm_nt(ask, w_k[...])).astype(BF).reshape(grad.shape)
    flag[...] = jnp.zeros_like(flag)


def rows_weights_kernel(*refs):
    prob_slot, grad_slot, grad, query, rows = refs[:5]
    by_key, by_value, key_sum, value_sum = refs[-4:]
    step, part = pl.program_id(0), pl.program_id(1)

    @pl.when((step == 0) & (part == 0))
    def _():
        key_sum[...] = jnp.zeros_like(key_sum)
        value_sum[...] = jnp.zeros_like(value_sum)

    mix, ask = weigh(prob_slot, grad_slot, grad, query)
    left = rows[...].reshape(mix.shape)
    key_sum[...] += mm_tn(left, ask)
    value_sum[...] += mm_tn(left, mix)

    @pl.when((step == pl.num_programs(0) - 1) & (part == pl.num_programs(1) - 1))
    def _():
        by_key[...] = key_sum[...].astype(BF)
        by_value[...] = value_sum[...].astype(BF)


def query_back_kernel(keys, token_t, grad_slot, waited, out, total):
    del waited
    step, part = pl.program_id(0), pl.program_id(1)
    k, dim = keys.shape[1:]

    @pl.when((step == 0) & (part == 0))
    def _():
        total[...] = jnp.zeros_like(total)

    score = mm(from_lanes(grad_slot[...]), head_spread(dim)) * 0.125
    prod = (score * keys[...].reshape(-1, dim).astype(F32)).astype(BF)
    total[...] += mm(token_t[...], prod)

    @pl.when((step == pl.num_programs(0) - 1) & (part == pl.num_programs(1) - 1))
    def _():
        out[...] = total[...].astype(BF)


def vector_sums_kernel(*refs, plain, pairs):
    ops, (wide, out, out_wide) = refs[: plain + 2 * pairs], refs[plain + 2 * pairs :]
    rows = [ops[i][...].astype(F32) for i in range(plain)]
    lefts = [ops[plain + 2 * i][...].astype(F32) for i in range(pairs)]
    rows += [lefts[i] * ops[plain + 2 * i + 1][...] for i in range(pairs)]
    rows += lefts
    sums = [jnp.sum(row, axis=0, keepdims=True) for row in rows]
    sums.append(jnp.zeros((out.shape[0] - len(sums), out.shape[1]), F32))
    out[...] = jnp.concatenate(sums, axis=0)
    out_wide[...] = jnp.sum(wide[...].astype(F32), axis=0, keepdims=True)


def vector_sums(plain, pairs, wide):
    ops = list(plain) + [x for pair in pairs for x in pair] + [wide]
    dim = plain[0].shape[1]
    return pl.pallas_call(
        functools.partial(vector_sums_kernel, plain=len(plain), pairs=len(pairs)),
        out_shape=(
            jax.ShapeDtypeStruct((16, dim), F32),
            jax.ShapeDtypeStruct((1, wide.shape[1]), F32),
        ),
        compiler_params=pltpu.CompilerParams(vmem_limit_bytes=24 * 1024 * 1024),
        cost_estimate=cost(2),
        name="vector_sums",
    )(*ops)


class SlotAttention:
    split = 2

    def __init__(self, ret_rows, shard_rows, peers, slots, dim):
        self.toks, self.ret = ret_rows.shape
        self.peers, self.slots, self.dim = peers, slots, dim
        self.k = slots // self.split
        self.wanted, token, self.at_rank, self.owner = plan_slots(
            ret_rows.T, shard_rows, peers, slots
        )
        k, dim, toks = self.k, self.dim, self.toks
        groups, wide = peers // GROUP, peers * PITCH
        self.grid = (groups, self.split)
        self.rows = pl.BlockSpec((GROUP, k, dim), lambda g, c: (g, c, 0))
        self.lanes = pl.BlockSpec((k, LANES), lambda g, c: (c, g))
        self.mark = pl.BlockSpec((GROUP * k, toks), lambda g, c: (c * groups + g, 0))
        self.mark_t = pl.BlockSpec((toks, GROUP * k), lambda g, c: (0, c * groups + g))
        self.square = self.whole(dim, dim)
        self.heads = self.whole(slots, wide)
        self.slot_rows = in_hbm((peers, slots, dim), BF)
        self.slot_heads = jax.ShapeDtypeStruct((slots, wide), F32)
        token = token.reshape(peers, self.split, k).transpose(1, 0, 2)
        self.token, self.token_t = self.call(
            token_marks_kernel,
            "token_marks",
            5,
            [
                pl.BlockSpec((GROUP * k, 1), lambda g, c: (c * groups + g, 0)),
                pl.BlockSpec((1, GROUP * k), lambda g, c: (0, c * groups + g)),
            ],
            [self.mark, self.mark_t],
            (in_hbm((peers * slots, toks), BF), in_hbm((toks, peers * slots), BF)),
        )(token.reshape(-1, 1), token.reshape(1, -1))

    @staticmethod
    def whole(*shape):
        return pl.BlockSpec(shape, lambda g, c: (0,) * len(shape))

    def call(self, kernel, name, micros, in_specs, out_specs, out_shape, scratch=(), mib=28):
        return pl.pallas_call(
            kernel,
            grid=self.grid,
            in_specs=in_specs,
            out_specs=out_specs,
            out_shape=out_shape,
            scratch_shapes=list(scratch),
            compiler_params=pltpu.CompilerParams(vmem_limit_bytes=mib * 1024 * 1024),
            cost_estimate=cost(micros),
            name=name,
        )

    def prepare(self, cross_q):
        self.query = self.call(
            query_rows_kernel,
            "query_rows",
            7,
            [self.mark, self.whole(self.toks, self.dim)],
            self.rows,
            self.slot_rows,
        )(self.token, cross_q)

    def forward(self, arrived, w_k, w_v, bias):
        dim, toks = self.dim, self.toks
        self.arrived, self.w_k, self.w_v = arrived, w_k, w_v
        self.keys, self.vals, scores = self.call(
            rows_in_kernel,
            "rows_in",
            22,
            [self.rows, self.rows, self.square, self.square],
            [self.rows, self.rows, self.lanes],
            (self.slot_rows, self.slot_rows, self.slot_heads),
        )(from_hbm(arrived), from_hbm(self.query), w_k, w_v)
        entries = (self.ret * PITCH, toks)
        self.prob_tok, self.prob_slot, mixed = self.call(
            attend_kernel,
            "attend",
            11,
            [self.heads, self.rows, self.mark_t]
            + [self.whole(*self.at_rank.shape), self.whole(*self.owner.shape), self.whole(1, dim)],
            [self.whole(*entries), self.heads, self.whole(toks, dim)],
            (
                jax.ShapeDtypeStruct(entries, F32),
                self.slot_heads,
                jax.ShapeDtypeStruct((toks, dim), BF),
            ),
            [pltpu.VMEM((toks, dim), F32)],
        )(scores, from_hbm(self.vals), self.token_t, self.at_rank, self.owner, bias.reshape(1, dim))
        return mixed

    def backward(self, grad):
        dim, toks = self.dim, self.toks
        grads, self.grad_slot = self.call(
            attend_back_kernel,
            "attend_back",
            13,
            [self.rows, self.mark, self.whole(toks, dim), self.whole(self.ret * PITCH, toks)]
            + [self.whole(*self.at_rank.shape), self.whole(*self.owner.shape)],
            [self.rows, self.heads],
            (self.slot_rows, self.slot_heads),
            [pltpu.VMEM(self.slot_heads.shape, F32)],
        )(from_hbm(self.vals), self.token, grad, self.prob_tok, self.at_rank, self.owner)
        self.factors = (self.prob_slot, self.grad_slot, from_hbm(grads), from_hbm(self.query))
        self.factor_specs = [self.lanes, self.lanes, self.rows, self.rows]
        sent, self.flag = self.call(
            rows_out_kernel,
            "rows_out",
            28,
            self.factor_specs + [self.square, self.square],
            [self.rows, self.whole(8, LANES)],
            (self.slot_rows, jax.ShapeDtypeStruct((8, LANES), F32)),
        )(*self.factors, self.w_k, self.w_v)
        return sent

    def query_grad(self):
        dim, toks = self.dim, self.toks
        return self.call(
            query_back_kernel,
            "query_back",
            7,
            [self.rows, self.mark_t, self.lanes, self.whole(8, LANES)],
            self.whole(toks, dim),
            jax.ShapeDtypeStruct((toks, dim), BF),
            [pltpu.VMEM((toks, dim), F32)],
        )(from_hbm(self.keys), self.token_t, self.grad_slot, self.flag)

    def weights(self, after):
        square = (self.dim, self.dim)
        return self.call(
            rows_weights_kernel,
            "rows_weights",
            24,
            self.factor_specs + [self.rows] + [WAIT] * len(after),
            [self.square, self.square],
            (jax.ShapeDtypeStruct(square, BF), jax.ShapeDtypeStruct(square, BF)),
            [pltpu.VMEM(square, F32), pltpu.VMEM(square, F32)],
        )(*self.factors, from_hbm(self.arrived), *after)


class GatheredAttention:
    def __init__(self, ret_rows, shard_rows, peers, slots, dim):
        self.toks, self.ret = ret_rows.shape
        self.dim, self.slots = dim, slots
        self.place, self.wanted, self.entry = plan_requests(ret_rows, shard_rows, peers, slots)
        self.fwd, self.bwd, self.back_q = cross_calls(self.toks, self.ret, dim)

    def prepare(self, cross_q):
        self.cross_q = cross_q

    def forward(self, arrived, w_k, w_v, bias):
        toks, dim = self.toks, self.dim
        self.key_heads, self.val_heads = w_k.reshape(dim, H, HD), w_v.reshape(dim, H, HD)
        query = self.cross_q.reshape(toks, H, HD)
        self.query_keys = jnp.einsum(
            "the,dhe->htd", query, self.key_heads, preferred_element_type=F32
        ).astype(BF)
        self.fetched = arrived.reshape(-1, dim)[self.place]
        self.state_mix, self.cross_p = self.fwd(self.query_keys, self.fetched)
        mixed = jnp.einsum(
            "htd,dhe->the", self.state_mix, self.val_heads, preferred_element_type=F32
        )
        return (mixed.reshape(toks, dim) + bias).astype(BF)

    def backward(self, grad):
        self.grad = grad.reshape(self.toks, H, HD)
        grad_mix = jnp.einsum(
            "the,dhe->htd", self.grad, self.val_heads, preferred_element_type=F32
        ).astype(BF)
        rows, self.grad_s = self.bwd(self.query_keys, grad_mix, self.fetched, self.cross_p)
        return rows[self.entry]

    def query_grad(self):
        self.grad_qk = self.back_q(self.grad_s, self.fetched)
        grad_q = jnp.einsum(
            "htd,dhe->the", self.grad_qk, self.key_heads, preferred_element_type=F32
        )
        return grad_q.reshape(self.toks, self.dim).astype(BF)

    def weights(self, after):
        def product(left, right):
            got = jnp.einsum("htd,the->dhe", left, right, preferred_element_type=F32)
            return got.reshape(self.dim, self.dim).astype(BF)

        grad_k = product(self.grad_qk, self.cross_q.reshape(self.toks, H, HD))
        return grad_k, product(self.state_mix, self.grad)


def store_sum_kernel(asked, returned, *refs, block, added):
    first = pl.program_id(0) * block + 1
    shape = (block, asked.shape[1])
    hit = lax.broadcasted_iota(jnp.int32, shape, 0) + first == asked[...]
    total = mm(hit.astype(BF), returned[...])
    refs[-1][...] = total + refs[0][...] if added else total


def store_sum(asked, returned, shard_rows, so_far, after=()):
    count, dim = returned.shape
    block = 256
    out = pl.BlockSpec((block, dim), lambda g: (g, 0))
    before = [] if so_far is None else [so_far]
    return pl.pallas_call(
        functools.partial(store_sum_kernel, block=block, added=so_far is not None),
        grid=(shard_rows // block,),
        in_specs=[
            pl.BlockSpec((1, count), lambda g: (0, 0)),
            pl.BlockSpec((count, dim), lambda g: (0, 0)),
        ]
        + [out] * len(before)
        + [WAIT] * len(after),
        out_specs=out,
        out_shape=jax.ShapeDtypeStruct((shard_rows, dim), F32),
        input_output_aliases={2: 0} if before else {},
        compiler_params=pltpu.CompilerParams(vmem_limit_bytes=VMEM_LIMIT),
        cost_estimate=cost(25),
        name="store_sum",
    )(asked.reshape(1, count), returned, *before, *after)


def all_to_all(array):
    return lax.all_to_all(array, RANKS, split_axis=0, concat_axis=0, tiled=True)


def on_device(
    tokens,
    seg_ids,
    live_mask,
    ret_rows,
    enc_store,
    attn_in,
    attn_out,
    ff_in,
    ff_out,
    biases,
    ln_gain,
    ln_shift,
    ff_bias,
    cotangent,
):
    n_rows = lax.axis_size("row")
    n_cols = lax.axis_size("col")
    peers = n_rows * n_cols
    tok_count, dim = tokens.shape
    shard_rows = enc_store.shape[0]
    ret = ret_rows.shape[1]
    slots = 3 * ret_rows.size // (2 * peers)
    rb, cb = attn_in.shape[1], attn_in.shape[2]
    order_a, order_b = bit_orders(n_rows, n_cols)
    n_row_bits = n_rows.bit_length() - 1
    n_far = n_row_bits - 2
    by_rows = n_cols == 2 and rb % 16 == 0 and cb % 128 == 0
    orders = (order_a, order_b, order_a, order_b)
    shapes = ((rb, cb), (rb, cb), (rb, 4 * cb), (4 * rb, cb))
    counts = (4, 4, 1, 1)
    if by_rows:
        col = lax.axis_index("col").astype(jnp.int32)[None]
        place_a = jnp.concatenate([block_of_row(order_a, n_rows), col])
        place_b = jnp.concatenate([block_of_row(order_b, n_rows), col])
        places = (place_a, place_b, place_a, place_b)

    in_slots = (
        by_rows
        and slots % (16 * SlotAttention.split) == 0
        and peers % GROUP == 0
        and tok_count % LANES == 0
        and tok_count <= 256
        and shard_rows & (shard_rows - 1) == 0
        and H <= PITCH
    )
    attention = (SlotAttention if in_slots else GatheredAttention)(
        ret_rows, shard_rows, peers, slots, dim
    )

    def vector_rows(parts):
        parts = [jnp.pad(part, ((0, 0), (0, cb - part.shape[1]))) for part in parts]
        return jnp.pad(jnp.concatenate(parts, axis=0), ((0, 2), (0, 0)))

    small = vector_rows([biases, ln_gain, ln_shift, ff_bias.reshape(1, -1)])
    packs = [*join(attn_in, attn_out, small, attention.wanted), ff_in[None], ff_out[None]]
    packs = [gather_bits(p, order[:1]) for p, order in zip(packs, orders)]
    asked = all_to_all(attention.wanted)
    asked = tie(asked, packs) if by_rows else asked
    packs = [gather_bits(p, order[1:n_far]) for p, order in zip(packs, orders)]

    answer = enc_store[jnp.maximum(asked - 1, 0)]
    for i in range(2):
        packs[i] = gather_bits(packs[i], orders[i][n_far : n_far + 1])
    arrived = all_to_all(hold(answer, packs) if by_rows else answer)
    if in_slots:
        packs[0] = hold(packs[0], [attention.token, attention.token_t])
    extras = (0, small.shape[0], 0, 0)

    def whole(i, after=()):
        done = n_far + 1
        if by_rows:
            own = gather_bits(packs[i], orders[i][done:n_row_bits])
            other = swap_bit(own, "col", 1)
            other = hold(other, after) if after else other
            return unpack(own, other, places[i], counts[i], shapes[i], extras[i])
        blocks = gather_bits(packs[i], orders[i][done:])
        return unpack_any(blocks, orders[i], counts[i], shapes[i], extras[i], n_rows, n_cols)

    mats = [whole(0), whole(1)]
    w_q, w_k, w_v = (mats[0][i] for i in range(3))
    w_ck, w_cv, w_o, w_co = (mats[1][0][i] for i in range(4))
    small_all = mats[1][1]
    small_all = small_all.astype(F32)
    vectors = small_all[:, :13, :rb].transpose(1, 0, 2).reshape(13, dim)
    bias_all, gain_all, shift_all = vectors[:7], vectors[7:10], vectors[10:]
    bias_ff = small_all[:, 13, : ff_bias.size].reshape(-1)

    *qkv, mixed, first, first_norm, first_scale, cross_q = self_fwd(
        tokens, seg_ids, live_mask, mats[0], w_o, bias_all, gain_all, shift_all
    )
    first_low = first.astype(BF)

    attention.prepare(cross_q)
    if in_slots:
        for i in (2, 3):
            packs[i] = gather_bits(packs[i], orders[i][n_far : n_far + 1])
    else:
        for i in (2, 3):
            packs[i] = gather_bits(packs[i], orders[i][n_far : n_far + 1])
    cross_low = attention.forward(arrived, w_ck, w_cv, bias_all[4])
    branch_two = mm(cross_low, w_co) + bias_all[5]
    second, second_norm, second_scale = norm_fwd(first + branch_two, gain_all[1], shift_all[1])
    second_low = second.astype(BF)

    after = [attention.query] if in_slots else []
    w_ff1, w_ff2 = whole(2, after)[0], whole(3, after)[0]
    hidden_act, hidden_slope = gelu_parts(mm(second_low, w_ff1) + bias_ff)
    hidden_low = hidden_act.astype(BF)
    branch_ffn = mm(hidden_low, w_ff2) + bias_all[6]
    final, final_norm, final_scale = norm_fwd(second + branch_ffn, gain_all[2], shift_all[2])
    output = final.astype(BF)
    cot = cotangent.astype(F32)
    grad_three = norm_back(cot, final_norm, final_scale, gain_all[2])
    grad_y = grad_three.astype(BF)
    grad_pre = (mm_nt(grad_y, w_ff2) * hidden_slope).astype(BF)
    grad_second = grad_three + mm_nt(grad_pre, w_ff1)
    grad_two = norm_back(grad_second, second_norm, second_scale, gain_all[1])
    grad_o2 = grad_two.astype(BF)
    grad_cmix = mm_nt(grad_o2, w_co).astype(BF)
    send_back = attention.backward(grad_cmix)
    returned = all_to_all(send_back)

    def packed(order, place, mats, small=None, after=()):
        if by_rows:
            return pack(mats, place, small, after)
        return pack_any(mats, order[::-1], small, n_rows, n_cols)

    def on_both(pairs, start, stop):
        return [
            scatter_bits(*pair, back[start:stop]) for pair, back in zip(pairs, (back_a, back_b))
        ]

    tile = (rb, cb)
    near = len(order_a) - n_far
    back_a, back_b = order_a[::-1], order_b[::-1]
    at_a, at_b = (place_a, place_b) if by_rows else (None, None)
    grad_cq = attention.query_grad()
    ff = [
        (order_a, at_a, [((second_low, grad_pre), tile, 4)]),
        (order_b, at_b, [((hidden_low, grad_y), (4 * rb, cb), 1)]),
    ]
    ff = [packed(*part, None, [grad_cq]) for part in ff]
    if by_rows:
        grad_cq = hold(grad_cq, [x for pair in ff for x in pair])
    grad_first, grad_one, grad_o, grad_q, grad_k, grad_v = self_bwd(
        grad_cq,
        grad_two,
        first_norm,
        first_scale,
        gain_all,
        qkv,
        seg_ids,
        live_mask,
        mats[0],
        w_o,
    )
    grad_tokens = (
        grad_one + mm_nt(grad_q, w_q) + mm_nt(grad_k, w_k) + mm_nt(grad_v, w_v)
    )

    vectors, wide = vector_sums(
        [grad_q, grad_v, grad_o, grad_cq, grad_cmix, grad_o2, grad_y],
        [(grad_first, first_norm), (grad_second, second_norm), (cotangent, final_norm)],
        grad_pre,
    )
    vectors = vectors[:13].reshape(13, n_rows, rb).transpose(1, 0, 2)
    wide = wide.reshape(n_rows, 1, -1)
    grad_small = [
        jnp.pad(vectors, ((0, 0), (0, 0), (0, cb - rb))),
        jnp.pad(wide, ((0, 0), (0, 2), (0, cb - ff_bias.size))),
    ]
    grad_small = jnp.concatenate(grad_small, axis=1).astype(BF)
    attn_one = packed(
        order_a,
        at_a,
        [
            ((tokens, grad_q), tile, 1),
            ((tokens, grad_k), tile, 1),
            ((tokens, grad_v), tile, 1),
            ((first_low, grad_cq), tile, 1),
        ],
    )
    ff = on_both(ff, 0, near - 2)
    before = [*attn_one, ff[0][1], ff[1][1]] if in_slots else []
    grad_wk, grad_wv = attention.weights(before)
    attn_two = packed(
        order_b,
        at_b,
        [
            (grad_wk, tile, 1),
            (grad_wv, tile, 1),
            ((mixed, grad_o), tile, 1),
            ((cross_low, grad_o2), tile, 1),
        ],
        grad_small,
    )
    def join_pairs(pairs):
        return tuple(jnp.concatenate(both, axis=1) for both in zip(*pairs))

    ff = join_pairs(on_both(ff, near - 2, near))
    attn = join_pairs(on_both([attn_one, attn_two], 0, near))
    grad_store = store_sum(asked, returned.reshape(-1, dim), shard_rows, None)
    if by_rows:
        ff, attn = ((hold(keep, [grad_store]), send) for keep, send in (ff, attn))
    ff, attn = (scatter_bits(*pair, back_a[near:-1]) for pair in (ff, attn))
    total_a, total_b = (
        (keep + swap_bit(send, *order_a[0]))[0].astype(F32) for keep, send in (attn, ff)
    )

    sum_small = total_a[8 * rb :]
    return (
        output,
        grad_tokens,
        grad_store,
        total_a[: 6 * rb].reshape(6, rb, cb),
        total_a[6 * rb : 8 * rb].reshape(2, rb, cb),
        jnp.concatenate([total_b[k * rb : (k + 1) * rb] for k in range(4)], axis=1),
        total_b[4 * rb :],
        sum_small[:7, :rb],
        sum_small[7:10, :rb],
        sum_small[10:13, :rb],
        sum_small[13, : ff_bias.size],
    )


def solution(mesh):
    both = ("row", "col")
    return jax.shard_map(
        on_device,
        mesh=mesh,
        in_specs=(
            P(both, None),
            P(both, None),
            P(both, None),
            P(both, None),
            P(both, None),
            P(None, "row", "col"),
            P(None, "row", "col"),
            P("row", "col"),
            P("row", "col"),
            P(None, "row"),
            P(None, "row"),
            P(None, "row"),
            P("row"),
            P(both, None),
        ),
        out_specs=(
            P(both, None),
            P(both, None),
            P(both, None),
            P(None, "row", "col"),
            P(None, "row", "col"),
            P("row", "col"),
            P("row", "col"),
            P(None, "row"),
            P(None, "row"),
            P(None, "row"),
            P("row"),
        ),
        check_vma=False,
    )
```

```python
import functools

import jax
import jax.numpy as jnp
import numpy as np
from jax import lax
from jax.experimental import pallas as pl
from jax.experimental.pallas import tpu as pltpu
from jax.sharding import PartitionSpec as P

H = 12
HD = 64
RANKS = ("row", "col")
BF = jnp.bfloat16
F32 = jnp.float32
VMEM_LIMIT = 60 * 1024 * 1024


def mm(a, b):
    return jnp.dot(a, b, preferred_element_type=F32)


def mm_nt(a, b):
    return lax.dot_general(a, b, (((1,), (1,)), ((), ())), preferred_element_type=F32)


def mm_tn(a, b):
    return lax.dot_general(a, b, (((0,), (0,)), ((), ())), preferred_element_type=F32)


def norm_fwd(resid, gain, shift):
    row_mean = jnp.mean(resid, axis=-1, keepdims=True)
    centered = resid - row_mean
    inv_std = lax.rsqrt(jnp.mean(centered * centered, axis=-1, keepdims=True) + 1e-05)
    normed = centered * inv_std
    return (normed * gain + shift, normed, inv_std)


def norm_back(grad_in, normed, inv_std, gain):
    scaled = grad_in * gain
    return inv_std * (
        scaled
        - jnp.mean(scaled, axis=-1, keepdims=True)
        - normed * jnp.mean(scaled * normed, axis=-1, keepdims=True)
    )


def gelu_parts(pre_act):
    cdf_part = 0.5 * (1.0 + lax.erf(pre_act * 0.7071067811865476))
    density = jnp.exp(-0.5 * pre_act * pre_act) * 0.3989422804014327
    return (pre_act * cdf_part, cdf_part + pre_act * density)


def column_sum(array):
    return jnp.sum(array.astype(F32), axis=0)


def bit_orders(n_rows, n_cols):
    row_bits = [("row", 1 << b) for b in reversed(range(n_rows.bit_length() - 1))]
    col_bits = [("col", 1 << b) for b in reversed(range(n_cols.bit_length() - 1))]
    swapped = row_bits[:-2] + row_bits[-1:] + row_bits[-2:-1]
    return row_bits + col_bits, swapped + col_bits


def swap_bit(array, axis, bit):
    pairs = [(i, i ^ bit) for i in range(lax.axis_size(axis))]
    return lax.ppermute(array, axis, pairs)


def gather_bits(blocks, order):
    for axis, bit in order:
        blocks = jnp.concatenate([blocks, swap_bit(blocks, axis, bit)], axis=0)
    return blocks


def scatter_bits(keep, send, order):
    for axis, bit in order:
        got = swap_bit(send, axis, bit)
        half = keep.shape[0] // 2
        keep, send = keep[:half] + got[:half], keep[half:] + got[half:]
    return keep, send


def block_of_row(order, n_rows):
    apart = np.zeros(n_rows, np.int32)
    for k, (_, bit) in enumerate(order[: n_rows.bit_length() - 1]):
        apart[(np.arange(n_rows) >> k) & 1 == 1] ^= bit
    table = np.zeros(n_rows, np.int32)
    table[apart] = np.arange(n_rows)
    return jnp.asarray(table)[lax.axis_index("row") ^ jnp.arange(n_rows, dtype=jnp.int32)]


def flip_by_position(blocks, stages):
    for k, (axis, bit) in enumerate(stages):
        here = (lax.axis_index(axis) & bit) != 0
        blocks = jnp.where(here, jnp.flip(blocks, axis=k), blocks)
    return blocks


def by_device(blocks, order):
    stages = order[::-1]
    shape = blocks.shape[1:]
    blocks = flip_by_position(blocks.reshape((2,) * len(stages) + shape), stages)
    rank = sorted(range(len(stages)), key=lambda k: (stages[k][0] == "col", -stages[k][1]))
    rest = list(range(len(stages), blocks.ndim))
    return blocks.transpose(rank + rest).reshape((-1,) + shape)


def by_stage(blocks, stages):
    shape = blocks.shape[1:]
    rank = sorted(range(len(stages)), key=lambda k: (stages[k][0] == "col", -stages[k][1]))
    rest = list(range(len(stages), len(stages) + len(shape)))
    back = [rank.index(k) for k in range(len(stages))]
    blocks = blocks.reshape((2,) * len(stages) + shape).transpose(back + rest)
    return flip_by_position(blocks, stages).reshape((-1,) + shape)


def cost(micros):
    return pl.CostEstimate(flops=int(micros * 1.1e9), bytes_accessed=0, transcendentals=0)


WAIT = pl.BlockSpec(memory_space=pltpu.HBM)


def in_hbm(shape, dtype):
    return pltpu.HBM(shape=shape, dtype=dtype)


def from_hbm(array):
    return pltpu.with_memory_space_constraint(array, pltpu.HBM)


def tie_kernel(*refs):
    refs[-1][...] = refs[0][...]


def tie(array, after):
    return pl.pallas_call(
        tie_kernel,
        in_specs=[pl.BlockSpec(memory_space=pltpu.VMEM)] + [WAIT] * len(after),
        out_shape=jax.ShapeDtypeStruct(array.shape, array.dtype),
        name="tie",
    )(array, *after)


def hold_kernel(*refs):
    del refs


def hold(array, after):
    return pl.pallas_call(
        hold_kernel,
        in_specs=[WAIT] * (1 + len(after)),
        out_specs=WAIT,
        out_shape=jax.ShapeDtypeStruct(array.shape, array.dtype),
        input_output_aliases={0: 0},
        name="hold",
    )(array, *after)


def tile_of(buf, k, r, c, shape):
    rows, cols = shape
    return buf.at[
        k, pl.ds(pl.multiple_of(r * rows, rows), rows), pl.ds(pl.multiple_of(c * cols, cols), cols)
    ]


def unpack_kernel(place, own, other, *refs, count, shape, extra):
    outs, (buf, *more) = refs[: 1 + bool(extra)], refs[1 + bool(extra) :]
    sems = more[-1]
    n_rows, col, rows = own.shape[0], place[own.shape[0]], shape[0]

    def fill(r, carry):
        j = place[r]
        for src, c, sem in ((own, col, 0), (other, 1 - col, 1)):
            for k in range(count):
                part = src.at[j, pl.ds(k * rows, rows)]
                pltpu.make_async_copy(part, tile_of(buf, k, r, c, shape), sems.at[sem]).start()
        if extra:
            tail = own.at[j, pl.ds(count * rows, extra)]
            pltpu.make_async_copy(tail, more[0].at[r], sems.at[2]).start()
        return carry

    lax.fori_loop(0, n_rows, fill, 0)
    body = own.at[:, pl.ds(0, count * rows)]
    for sem in range(2):
        pltpu.make_async_copy(body, body, sems.at[sem]).wait()
    out = pltpu.make_async_copy(buf, outs[0], sems.at[3])
    out.start()
    if extra:
        pltpu.make_async_copy(more[0], more[0], sems.at[2]).wait()
        tails = pltpu.make_async_copy(more[0], outs[1], sems.at[4])
        tails.start()
        tails.wait()
    out.wait()


def unpack(own, other, place, count, shape, extra=0):
    n_rows = own.shape[0]
    rows, cols = shape
    whole = jax.ShapeDtypeStruct((count, n_rows * rows, 2 * cols), BF)
    tails = jax.ShapeDtypeStruct((n_rows, extra, cols), BF)
    shapes = [whole] + [tails] * bool(extra)
    got = pl.pallas_call(
        functools.partial(unpack_kernel, count=count, shape=shape, extra=extra),
        in_specs=[pl.BlockSpec(memory_space=pltpu.SMEM)] + [pl.BlockSpec(memory_space=pl.ANY)] * 2,
        out_specs=[pl.BlockSpec(memory_space=pl.ANY)] * len(shapes),
        out_shape=shapes,
        scratch_shapes=[pltpu.VMEM(x.shape, BF) for x in shapes] + [pltpu.SemaphoreType.DMA((5,))],
        compiler_params=pltpu.CompilerParams(vmem_limit_bytes=32 * 1024 * 1024),
        cost_estimate=pl.CostEstimate(
            flops=0, bytes_accessed=4 * whole.size * 2, transcendentals=0
        ),
        name="unpack",
    )(place, own, other)
    return got if extra else got[0]


def join_kernel(attn_in, attn_out, small, waited, one, two, *, rb):
    del waited
    for k in range(4):
        one[0, k * rb : (k + 1) * rb] = attn_in[k]
    for k in range(2):
        two[0, k * rb : (k + 1) * rb] = attn_in[4 + k]
        two[0, (2 + k) * rb : (3 + k) * rb] = attn_out[k]
    two[0, 4 * rb :] = small[...]


def join(attn_in, attn_out, small, after):
    rb, cb = attn_in.shape[1:]
    if rb % 16 or cb % 128:
        two = [attn_in[4:].reshape(-1, cb), attn_out.reshape(-1, cb), small]
        return attn_in[:4].reshape(1, -1, cb), jnp.concatenate(two, axis=0)[None]
    return pl.pallas_call(
        functools.partial(join_kernel, rb=rb),
        in_specs=[pl.BlockSpec(memory_space=pltpu.VMEM)] * 3 + [WAIT],
        out_shape=(
            jax.ShapeDtypeStruct((1, 4 * rb, cb), BF),
            jax.ShapeDtypeStruct((1, 4 * rb + small.shape[0], cb), BF),
        ),
        name="join",
    )(attn_in, attn_out, small, after)


def pack_kernel(place, *refs, mats, rows, extra, waits):
    n_ops = 1 + max(max(mat[0]) for mat in mats)
    ops, refs = refs[:n_ops], refs[n_ops:]
    small, refs = refs[: bool(extra)], refs[bool(extra) + waits :]
    keep, send, *bufs, sems = refs
    n_rows, col = keep.shape[0], place[keep.shape[0]]
    loads = {}
    for k, (at, _, _) in enumerate(mats):
        if len(at) == 1:
            loads[k] = pltpu.make_async_copy(ops[at[0]], bufs[k].at[0], sems.at[2 + k])
            loads[k].start()
    for k, (at, _, _) in enumerate(mats):
        if len(at) == 2:
            left, right = ops[at[0]], ops[at[1]]
            _, tall, wide = bufs[k].shape
            tile = min(tall, wide)
            for i in range(0, tall, tile):
                for j in range(0, wide, tile):
                    got = mm_tn(left[:, i : i + tile], right[:, j : j + tile])
                    bufs[k][0, i : i + tile, j : j + tile] = got.astype(BF)
    for load in loads.values():
        load.wait()

    def spread(r, carry):
        j = place[r]
        for dst, c, sem in ((keep, col, 0), (send, 1 - col, 1)):
            first = 0
            for buf, (_, shape, beside) in zip(bufs, mats):
                for k in range(beside):
                    part = dst.at[j, pl.ds(first, shape[0])]
                    tile = tile_of(buf, 0, r, c * beside + k, shape)
                    pltpu.make_async_copy(tile, part, sems.at[sem]).start()
                    first += shape[0]
            if extra:
                tail = dst.at[j, pl.ds(first, extra)]
                pltpu.make_async_copy(small[0].at[r], tail, sems.at[sem]).start()
        return carry

    lax.fori_loop(0, n_rows, spread, 0)
    for dst, sem in ((keep, 0), (send, 1)):
        pltpu.make_async_copy(dst, dst, sems.at[sem]).wait()


def pack(mats, place, small=None, after=()):
    ops, parts, specs, bufs, flops, total = [], [], [], [], 0, 0
    for mat, shape, beside in mats:
        mat = mat if isinstance(mat, tuple) else (mat,)
        parts.append((tuple(range(len(ops), len(ops) + len(mat))), shape, beside))
        ops += mat
        specs += [pl.BlockSpec(memory_space=pltpu.VMEM if len(mat) == 2 else pl.ANY)] * len(mat)
        whole = (mat[0].shape[1], mat[1].shape[1]) if len(mat) == 2 else mat[0].shape
        bufs.append(pltpu.VMEM((1,) + tuple(whole), BF))
        flops += 2 * mat[0].shape[0] * whole[0] * whole[1] if len(mat) == 2 else 0
        total += beside * shape[0]
        n_rows = whole[0] // shape[0]
    extra = 0 if small is None else small.shape[1]
    block = in_hbm((n_rows, total + extra, shape[1]), BF)
    if extra:
        ops.append(small)
        specs.append(pl.BlockSpec(memory_space=pltpu.VMEM))
    return pl.pallas_call(
        functools.partial(
            pack_kernel, mats=tuple(parts), rows=total, extra=extra, waits=len(after)
        ),
        in_specs=[pl.BlockSpec(memory_space=pltpu.SMEM)] + specs + [WAIT] * len(after),
        out_specs=[pl.BlockSpec(memory_space=pl.ANY)] * 2,
        out_shape=[block, block],
        scratch_shapes=bufs + [pltpu.SemaphoreType.DMA((2 + len(mats),))],
        compiler_params=pltpu.CompilerParams(vmem_limit_bytes=48 * 1024 * 1024),
        cost_estimate=pl.CostEstimate(
            flops=flops, bytes_accessed=8 * n_rows * total * shape[1], transcendentals=0
        ),
        name="pack",
    )(place, *ops, *after)


def unpack_any(blocks, order, count, shape, extra, n_rows, n_cols):
    rows, cols = shape
    got = by_device(blocks, order).reshape(n_rows, n_cols, -1, cols)
    mats = got[:, :, : count * rows].reshape(n_rows, n_cols, count, rows, cols)
    mats = mats.transpose(2, 0, 3, 1, 4).reshape(count, n_rows * rows, n_cols * cols)
    return (mats, got[:, 0, count * rows :]) if extra else mats


def pack_any(mats, order, small, n_rows, n_cols):
    got = []
    for mat, (rows, cols), beside in mats:
        mat = mm_tn(*mat).astype(BF) if isinstance(mat, tuple) else mat
        mat = mat.reshape(n_rows, rows, n_cols, beside, cols).transpose(0, 2, 3, 1, 4)
        got.append(mat.reshape(n_rows, n_cols, beside * rows, cols))
    if small is not None:
        got.append(jnp.broadcast_to(small[:, None], (n_rows, n_cols) + small.shape[1:]))
    got = jnp.concatenate(got, axis=2)
    got = by_stage(got.reshape((-1,) + got.shape[2:]), order)
    half = got.shape[0] // 2
    return got[:half], got[half:]


def plan_requests(ret_rows, shard_rows, peers, slots):
    flat = ret_rows.reshape(-1)
    count = flat.shape[0]
    owner = flat // shard_rows
    local_row = flat - owner * shard_rows
    mine = owner[:, None] == jnp.arange(peers, dtype=jnp.int32)[None, :]
    run = 256
    runs = count // run
    ones = mine.astype(BF).reshape(runs, run, peers)
    lower = jnp.tril(jnp.ones((run, run), BF))
    within = jnp.einsum("ij,bjo->bio", lower, ones, preferred_element_type=F32)
    totals = within[:, -1, :]
    before = jnp.cumsum(totals, axis=0) - totals
    upto = (within + before[:, None, :]).reshape(count, peers)
    rank = jnp.sum(jnp.where(mine, upto, 0.0), axis=1).astype(jnp.int32) - 1
    place = owner * slots + rank
    row_code = local_row + 1
    entry_code = jnp.arange(count, dtype=jnp.int32)
    digits = jnp.stack([row_code // 64, row_code % 64, entry_code // 64, entry_code % 64])
    left = jnp.where(mine.T[None], digits[:, None, :], 0).astype(BF)
    at_rank = (rank[:, None] == jnp.arange(slots, dtype=jnp.int32)[None, :]).astype(BF)
    codes = mm(left.reshape(4 * peers, count), at_rank).astype(jnp.int32).reshape(4, peers, slots)
    return place, codes[0] * 64 + codes[1], codes[2] * 64 + codes[3]


def row_norm(resid):
    centered = resid - jnp.mean(resid, axis=-1, keepdims=True)
    scale = lax.rsqrt(jnp.mean(centered * centered, axis=-1, keepdims=True) + 1e-05)
    return centered * scale, scale


def head_masks():
    lane = lax.broadcasted_iota(jnp.int32, (1, 2 * HD), 1)
    return [(lane // HD == i).astype(F32).astype(BF) for i in range(2)]


def self_probs(query, key, visible):
    scores = jnp.where(visible, mm_nt(query, key) * (HD**-0.5), -1e30)
    expo = jnp.exp(scores - jnp.max(scores, axis=-1, keepdims=True))
    return expo / jnp.sum(expo, axis=-1, keepdims=True)


def visible_pairs(seg_col, seg_row, live_row):
    shape = (seg_col.shape[0], seg_row.shape[1])
    at_query = lax.broadcasted_iota(jnp.int32, shape, 0)
    at_key = lax.broadcasted_iota(jnp.int32, shape, 1)
    return (
        (at_key <= at_query)
        & (seg_col[...] == seg_row[...])
        & ((live_row[...] == 1) | (at_key == at_query))
    )


def self_fwd_kernel(*refs):
    tokens, seg_col, seg_row, live_row, w_qkvc, w_o, bias, gain, shift = refs[:9]
    queries, keys, values, mixed, first, normed, scale, cross_q = refs[9:]
    x = tokens[...]
    queries[...] = (mm(x, w_qkvc[0]) + bias[0:1]).astype(BF)
    keys[...] = mm(x, w_qkvc[1]).astype(BF)
    values[...] = (mm(x, w_qkvc[2]) + bias[1:2]).astype(BF)
    visible = visible_pairs(seg_col, seg_row, live_row)
    for pair in range(H // 2):
        lanes = slice(2 * HD * pair, 2 * HD * (pair + 1))
        total = 0.0
        for mask in head_masks():
            prob = self_probs(queries[:, lanes], keys[:, lanes] * mask, visible)
            total = total + mm(prob.astype(BF), values[:, lanes] * mask)
        mixed[:, lanes] = total.astype(BF)
    resid = x.astype(F32) + mm(mixed[...], w_o[...]) + bias[2:3]
    norm, inv = row_norm(resid)
    normed[...] = norm
    scale[...] = jnp.broadcast_to(inv, scale.shape)
    out = norm * gain[0:1] + shift[0:1]
    first[...] = out
    cross_q[...] = (mm(out.astype(BF), w_qkvc[3]) + bias[3:4]).astype(BF)


def one_step(ops, picks):
    specs = []
    for i, op in enumerate(ops):
        block, at = op.shape, (0,) * op.ndim
        if i in picks:
            block, at = (None,) + op.shape[1:], (picks[i],) + at[1:]
        specs.append(pl.BlockSpec(block, lambda g, at=at: at))
    return specs


def self_fwd(tokens, seg, live, w_qkvc, mats, bias, gain, shift):
    toks, dim = tokens.shape
    ops = (tokens, seg.reshape(toks, 1), seg, live, w_qkvc, mats, bias, gain, shift)
    low = jax.ShapeDtypeStruct((toks, dim), BF)
    full = jax.ShapeDtypeStruct((toks, dim), F32)
    column = jax.ShapeDtypeStruct((toks, 128), F32)
    return pl.pallas_call(
        self_fwd_kernel,
        grid=(1,),
        in_specs=one_step(ops, {5: 2}),
        out_specs=one_step((low, low, low, low, full, full, column, low), {}),
        out_shape=(low, low, low, low, full, full, column, low),
        compiler_params=pltpu.CompilerParams(vmem_limit_bytes=28 * 1024 * 1024),
        cost_estimate=cost(5),
        name="self_fwd",
    )(*ops)


def self_bwd_kernel(*refs):
    grad_cq, grad_two, normed, scale, gain, queries, keys, values = refs[:8]
    seg_col, seg_row, live_row, w_qkvc, w_o = refs[8:13]
    grad_first, grad_one, grad_o, grad_q, grad_k, grad_v, grad_mix = refs[13:]
    incoming = grad_two[...] + mm_nt(grad_cq[...], w_qkvc[3])
    grad_first[...] = incoming
    one = norm_back(incoming, normed[...], scale[:, 0:1], gain[0:1])
    grad_one[...] = one
    low = one.astype(BF)
    grad_o[...] = low
    grad_mix[...] = mm_nt(low, w_o[...]).astype(BF)
    visible = visible_pairs(seg_col, seg_row, live_row)
    for pair in range(H // 2):
        lanes = slice(2 * HD * pair, 2 * HD * (pair + 1))
        by_query, by_key, by_value = 0.0, 0.0, 0.0
        for mask in head_masks():
            query, key = queries[:, lanes] * mask, keys[:, lanes] * mask
            grad = grad_mix[:, lanes] * mask
            prob = self_probs(query, key, visible)
            grad_p = mm_nt(grad, values[:, lanes])
            dot = jnp.sum(prob * grad_p, axis=-1, keepdims=True)
            grad_s = (prob * (grad_p - dot)).astype(BF)
            by_query = by_query + mm(grad_s, key)
            by_key = by_key + mm_tn(grad_s, query)
            by_value = by_value + mm_tn(prob.astype(BF), grad)
        grad_q[:, lanes] = (by_query * (HD**-0.5)).astype(BF)
        grad_k[:, lanes] = (by_key * (HD**-0.5)).astype(BF)
        grad_v[:, lanes] = by_value.astype(BF)


def self_bwd(grad_cq, grad_two, normed, scale, gain, qkv, seg, live, w_qkvc, mats):
    toks, dim = grad_two.shape
    ops = (grad_cq, grad_two, normed, scale, gain, *qkv)
    ops += (seg.reshape(toks, 1), seg, live, w_qkvc, mats)
    low = jax.ShapeDtypeStruct((toks, dim), BF)
    full = jax.ShapeDtypeStruct((toks, dim), F32)
    return pl.pallas_call(
        self_bwd_kernel,
        grid=(1,),
        in_specs=one_step(ops, {12: 2}),
        out_specs=one_step((full, full, low, low, low, low), {}),
        out_shape=(full, full, low, low, low, low),
        scratch_shapes=[pltpu.VMEM((toks, dim), BF)],
        compiler_params=pltpu.CompilerParams(vmem_limit_bytes=28 * 1024 * 1024),
        cost_estimate=cost(6),
        name="self_bwd",
    )(*ops)


def own_rows(tokens, ret, heads):
    shape = (heads * tokens, tokens * ret)
    row_tok = lax.broadcasted_iota(jnp.int32, shape, 0) % tokens
    col_tok = lax.broadcasted_iota(jnp.int32, shape, 1) // ret
    return row_tok == col_tok


def cross_fwd_kernel(qk, fetched, mix, probs, *, ret):
    heads, tokens, dim = qk.shape
    own = own_rows(tokens, ret, heads)
    query = qk[...].reshape(heads * tokens, dim)
    rows = fetched[...]
    scores = jnp.where(own, mm_nt(query, rows) * 0.125, -1e30)
    expo = jnp.exp(scores - jnp.max(scores, axis=-1, keepdims=True))
    prob = expo / jnp.sum(expo, axis=-1, keepdims=True)
    probs[0] = prob
    mix[...] = mm(prob.astype(BF), rows).astype(BF).reshape(heads, tokens, dim)


def cross_bwd_kernel(qk, gmix, fetched, probs, grad_rows, grad_s, *, ret):
    heads, tokens, dim = qk.shape
    query = qk[...].reshape(heads * tokens, dim)
    grad_mix = gmix[...].reshape(heads * tokens, dim)
    prob = probs[0]
    grad_p = mm_nt(grad_mix, fetched[...])
    g_s = (prob * (grad_p - jnp.sum(prob * grad_p, axis=-1, keepdims=True))).astype(BF)
    grad_s[0] = g_s
    grad_rows[...] = (
        mm_tn(prob.astype(BF), grad_mix) + mm_tn(g_s, query) * 0.125
    ).astype(BF)


def cross_back_q_kernel(grad_s, fetched, grad_qk):
    heads, tokens, dim = grad_qk.shape
    got = mm(grad_s[0], fetched[...]) * 0.125
    grad_qk[...] = got.astype(BF).reshape(heads, tokens, dim)


def cross_calls(tok_count, ret, dim):
    tb = 16
    blocks = tok_count // tb
    by_head = pl.BlockSpec((H, tb, dim), lambda g: (0, g, 0))
    rows = pl.BlockSpec((tb * ret, dim), lambda g: (g, 0))
    square = pl.BlockSpec((1, H * tb, tb * ret), lambda g: (g, 0, 0))
    heads_shape = jax.ShapeDtypeStruct((H, tok_count, dim), BF)
    square_f32 = jax.ShapeDtypeStruct((blocks, H * tb, tb * ret), F32)
    square_bf = jax.ShapeDtypeStruct((blocks, H * tb, tb * ret), BF)
    params = pltpu.CompilerParams(vmem_limit_bytes=VMEM_LIMIT)
    fwd = pl.pallas_call(
        functools.partial(cross_fwd_kernel, ret=ret),
        grid=(blocks,),
        in_specs=[by_head, rows],
        out_specs=[by_head, square],
        out_shape=(heads_shape, square_f32),
        compiler_params=params,
        name="cross_fwd",
    )
    bwd = pl.pallas_call(
        functools.partial(cross_bwd_kernel, ret=ret),
        grid=(blocks,),
        in_specs=[by_head, by_head, rows, square],
        out_specs=[rows, square],
        out_shape=(jax.ShapeDtypeStruct((tok_count * ret, dim), BF), square_bf),
        compiler_params=params,
        name="cross_bwd",
    )
    back_q = pl.pallas_call(
        cross_back_q_kernel,
        grid=(blocks,),
        in_specs=[square, rows],
        out_specs=by_head,
        out_shape=heads_shape,
        compiler_params=params,
        name="cross_back_q",
    )
    return fwd, bwd, back_q


GROUP = 8
LANES = 128
PITCH = LANES // GROUP
TILE = 256


def plan_kernel(rows, wanted, token, at_rank, owner, *, shard_rows):
    peers, slots = wanted.shape
    ret, toks = rows.shape
    shape = (toks, toks)
    upper = (
        lax.broadcasted_iota(jnp.int32, shape, 0) <= lax.broadcasted_iota(jnp.int32, shape, 1)
    ).astype(BF)
    peer = lax.broadcasted_iota(jnp.int32, (peers, toks), 0)
    tok_code = (lax.broadcasted_iota(jnp.int32, (peers, toks), 1) + 1).astype(F32)
    k_rows = lax.broadcasted_iota(jnp.int32, (at_rank.shape[0], toks), 0)
    shift = shard_rows.bit_length() - 1
    before = jnp.zeros((peers, 1), F32)
    codes = jnp.zeros((3 * peers, at_rank.shape[0]), F32)
    for r in range(ret):
        row = rows[r : r + 1, :]
        own = lax.shift_right_logical(row, shift)
        code = lax.bitwise_and(row, shard_rows - 1) + 1
        mine = own == peer
        upto = mm(mine.astype(BF), upper) + before
        before = upto[:, toks - 1 :]
        rank = jnp.sum(jnp.where(mine, upto, 0.0), axis=0, keepdims=True).astype(jnp.int32) - 1
        at = (k_rows == rank).astype(BF)
        at_rank[:, r * toks : (r + 1) * toks] = at
        owner[r : r + 1, :] = own
        high = lax.shift_right_logical(code, 6).astype(F32)
        low = lax.bitwise_and(code, 63).astype(F32)
        left = jnp.concatenate(
            [
                jnp.where(mine, high, 0.0).astype(BF),
                jnp.where(mine, low, 0.0).astype(BF),
                jnp.where(mine, tok_code, 0.0).astype(BF),
            ],
            axis=0,
        )
        codes = codes + mm_nt(left, at)
    codes = codes[:, :slots].astype(jnp.int32)
    wanted[...] = codes[:peers] * 64 + codes[peers : 2 * peers]
    token[...] = codes[2 * peers :]


def plan_slots(rows, shard_rows, peers, slots):
    ret, toks = rows.shape
    tall = -(-slots // LANES) * LANES
    return pl.pallas_call(
        functools.partial(plan_kernel, shard_rows=shard_rows),
        out_shape=(
            jax.ShapeDtypeStruct((peers, slots), jnp.int32),
            jax.ShapeDtypeStruct((peers, slots), jnp.int32),
            jax.ShapeDtypeStruct((tall, ret * toks), BF),
            jax.ShapeDtypeStruct((ret, toks), jnp.int32),
        ),
        cost_estimate=cost(4),
        name="plan",
    )(rows)


def head_sum(dim):
    shape = (dim, LANES)
    head = lax.broadcasted_iota(jnp.int32, shape, 0) // HD
    return (head == lax.broadcasted_iota(jnp.int32, shape, 1)).astype(BF)


def head_spread(dim):
    shape = (LANES, dim)
    head = lax.broadcasted_iota(jnp.int32, shape, 1) // HD
    return (head == lax.broadcasted_iota(jnp.int32, shape, 0)).astype(BF)


def to_lanes(by_peer, k):
    total = by_peer[:k]
    for q in range(1, GROUP):
        total = total + pltpu.roll(by_peer[q * k : (q + 1) * k], PITCH * q, 1)
    return total


def from_lanes(lanes):
    parts = [lanes] + [pltpu.roll(lanes, LANES - PITCH * q, 1) for q in range(1, GROUP)]
    return jnp.concatenate([part.astype(BF) for part in parts], axis=0)


def to_entries(slot_vals, at_rank, owner):
    k, wide = slot_vals.shape
    tall, toks = at_rank.shape[0], owner.shape[1]
    peers = wide // PITCH
    full = jnp.concatenate([slot_vals, jnp.zeros((tall - k, wide), F32)], axis=0).T
    high = full.astype(BF)
    low = (full - high.astype(F32)).astype(BF)
    peer = lax.broadcasted_iota(jnp.int32, (wide, toks), 0) // PITCH
    out = []
    for r in range(owner.shape[0]):
        at = at_rank[:, r * toks : (r + 1) * toks]
        got = mm(high, at) + mm(low, at)
        got = jnp.where(peer == owner[r : r + 1, :], got, 0.0)
        out.append(jnp.sum(got.reshape(peers, PITCH, toks), axis=0))
    return out


def to_slots(entry_vals, at_rank, owner, peers, slots):
    toks = owner.shape[1]
    wide = peers * PITCH
    peer = lax.broadcasted_iota(jnp.int32, (wide, toks), 0) // PITCH
    total = jnp.zeros((at_rank.shape[0], wide), F32)
    for r, vals in enumerate(entry_vals):
        tiled = jnp.concatenate([vals] * peers, axis=0)
        mine = jnp.where(peer == owner[r : r + 1, :], tiled, 0.0).astype(BF)
        total = total + mm_nt(at_rank[:, r * toks : (r + 1) * toks], mine)
    return total[:slots]


def token_marks_kernel(column, row, marks, marks_t):
    marks[...] = (
        column[...] == lax.broadcasted_iota(jnp.int32, marks.shape, 1) + 1
    ).astype(BF)
    marks_t[...] = (row[...] == lax.broadcasted_iota(jnp.int32, marks_t.shape, 0) + 1).astype(BF)


def query_rows_kernel(token, query, out):
    out[...] = mm(token[...], query[...]).astype(BF).reshape(out.shape)


def rows_in_kernel(arrived, query, w_k, w_v, keys, vals, scores):
    group, k, dim = arrived.shape
    rows = arrived[...].reshape(group * k, dim)
    total = jnp.zeros((group * k, LANES), F32)
    for at in range(0, dim, TILE):
        tile = slice(at, at + TILE)
        key = mm(rows, w_k[:, tile])
        keys[:, :, tile] = key.astype(BF).reshape(group, k, TILE)
        prod = (key * query[:, :, tile].reshape(group * k, TILE).astype(F32)).astype(BF)
        total = total + mm(prod, head_sum(dim)[tile])
        vals[:, :, tile] = mm(rows, w_v[:, tile]).astype(BF).reshape(group, k, TILE)
    scores[...] = to_lanes(total, k) * 0.125


def attend_kernel(
    scores, vals, token_t, at_rank, owner, bias, prob_tok, prob_slot, mixed, total
):
    step, part = pl.program_id(0), pl.program_id(1)
    k, dim = vals.shape[1:]
    slots, wide = scores.shape

    @pl.when((step == 0) & (part == 0))
    def _():
        entry = to_entries(scores[...], at_rank, owner)
        top = functools.reduce(jnp.maximum, entry)
        expo = [jnp.exp(part - top) for part in entry]
        norm = functools.reduce(jnp.add, expo)
        probs = [part / norm for part in expo]
        for r, part in enumerate(probs):
            prob_tok[r * PITCH : (r + 1) * PITCH, :] = part
        prob_slot[...] = to_slots(probs, at_rank, owner, wide // PITCH, slots)
        total[...] = jnp.zeros_like(total)

    lanes = pl.ds(pl.multiple_of(step * LANES, LANES), LANES)
    here = pl.ds(pl.multiple_of(part * k, 16), k)
    prob = mm(from_lanes(prob_slot[here, lanes]), head_spread(dim))
    prod = (prob * vals[...].reshape(-1, dim).astype(F32)).astype(BF)
    total[...] += mm(token_t[...], prod)

    @pl.when((step == pl.num_programs(0) - 1) & (part == pl.num_programs(1) - 1))
    def _():
        mixed[...] = (total[...] + bias[...]).astype(BF)


def attend_back_kernel(
    vals, token, grad, prob_tok, at_rank, owner, grads, grad_slot, slot_p
):
    step, part = pl.program_id(0), pl.program_id(1)
    k, dim = vals.shape[1:]
    slots, wide = slot_p.shape
    lanes = pl.ds(pl.multiple_of(step * LANES, LANES), LANES)
    here = pl.ds(pl.multiple_of(part * k, 16), k)
    rows = mm(token[...], grad[...])
    grads[...] = rows.astype(BF).reshape(vals.shape)
    prod = (rows * vals[...].reshape(-1, dim).astype(F32)).astype(BF)
    slot_p[here, lanes] = to_lanes(mm(prod, head_sum(dim)), k)

    @pl.when((step == pl.num_programs(0) - 1) & (part == pl.num_programs(1) - 1))
    def _():
        entry = to_entries(slot_p[...], at_rank, owner)
        probs = [prob_tok[r * PITCH : (r + 1) * PITCH, :] for r in range(len(entry))]
        dots = functools.reduce(jnp.add, [p * g for p, g in zip(probs, entry)])
        scores = [(p * (g - dots)).astype(BF).astype(F32) for p, g in zip(probs, entry)]
        grad_slot[...] = to_slots(scores, at_rank, owner, wide // PITCH, slots)


def weigh(prob_slot, grad_slot, grad, query):
    dim = grad.shape[2]
    spread = head_spread(dim)
    prob = mm(from_lanes(prob_slot[...]), spread)
    mix = (prob * grad[...].reshape(-1, dim).astype(F32)).astype(BF)
    score = mm(from_lanes(grad_slot[...]), spread) * 0.125
    return mix, (score * query[...].reshape(-1, dim).astype(F32)).astype(BF)


def rows_out_kernel(prob_slot, grad_slot, grad, query, w_k, w_v, out, flag):
    group, k, dim = grad.shape
    mix, ask = weigh(prob_slot, grad_slot, grad, query)
    for at in range(0, dim, TILE):
        tile = slice(at, at + TILE)
        got = mm_nt(mix, w_v[tile]) + mm_nt(ask, w_k[tile])
        out[:, :, tile] = got.astype(BF).reshape(group, k, TILE)
    flag[...] = jnp.zeros_like(flag)


def rows_weights_kernel(*refs):
    prob_slot, grad_slot, grad, query, rows = refs[:5]
    by_key, by_value, key_sum, value_sum = refs[-4:]
    step, part = pl.program_id(0), pl.program_id(1)

    @pl.when((step == 0) & (part == 0))
    def _():
        key_sum[...] = jnp.zeros_like(key_sum)
        value_sum[...] = jnp.zeros_like(value_sum)

    mix, ask = weigh(prob_slot, grad_slot, grad, query)
    left = rows[...].reshape(mix.shape)
    key_sum[...] += mm_tn(left, ask)
    value_sum[...] += mm_tn(left, mix)

    @pl.when((step == pl.num_programs(0) - 1) & (part == pl.num_programs(1) - 1))
    def _():
        by_key[...] = key_sum[...].astype(BF)
        by_value[...] = value_sum[...].astype(BF)


def query_back_kernel(keys, token_t, grad_slot, waited, out, total):
    del waited
    step, part = pl.program_id(0), pl.program_id(1)
    k, dim = keys.shape[1:]

    @pl.when((step == 0) & (part == 0))
    def _():
        total[...] = jnp.zeros_like(total)

    score = mm(from_lanes(grad_slot[...]), head_spread(dim)) * 0.125
    prod = (score * keys[...].reshape(-1, dim).astype(F32)).astype(BF)
    total[...] += mm(token_t[...], prod)

    @pl.when((step == pl.num_programs(0) - 1) & (part == pl.num_programs(1) - 1))
    def _():
        out[...] = total[...].astype(BF)


def vector_sums_kernel(*refs, plain, pairs):
    ops, (wide, out, out_wide) = refs[: plain + 2 * pairs], refs[plain + 2 * pairs :]
    rows = [ops[i][...].astype(F32) for i in range(plain)]
    lefts = [ops[plain + 2 * i][...].astype(F32) for i in range(pairs)]
    rows += [lefts[i] * ops[plain + 2 * i + 1][...] for i in range(pairs)]
    rows += lefts
    sums = [jnp.sum(row, axis=0, keepdims=True) for row in rows]
    sums.append(jnp.zeros((out.shape[0] - len(sums), out.shape[1]), F32))
    out[...] = jnp.concatenate(sums, axis=0)
    out_wide[...] = jnp.sum(wide[...].astype(F32), axis=0, keepdims=True)


def vector_sums(plain, pairs, wide):
    ops = list(plain) + [x for pair in pairs for x in pair] + [wide]
    dim = plain[0].shape[1]
    return pl.pallas_call(
        functools.partial(vector_sums_kernel, plain=len(plain), pairs=len(pairs)),
        out_shape=(
            jax.ShapeDtypeStruct((16, dim), F32),
            jax.ShapeDtypeStruct((1, wide.shape[1]), F32),
        ),
        compiler_params=pltpu.CompilerParams(vmem_limit_bytes=24 * 1024 * 1024),
        cost_estimate=cost(2),
        name="vector_sums",
    )(*ops)


class SlotAttention:
    split = 1

    def __init__(self, ret_rows, shard_rows, peers, slots, dim):
        self.toks, self.ret = ret_rows.shape
        self.peers, self.slots, self.dim = peers, slots, dim
        self.k = slots // self.split
        self.wanted, token, self.at_rank, self.owner = plan_slots(
            ret_rows.T, shard_rows, peers, slots
        )
        k, dim, toks = self.k, self.dim, self.toks
        groups, wide = peers // GROUP, peers * PITCH
        self.grid = (groups, self.split)
        self.rows = pl.BlockSpec((GROUP, k, dim), lambda g, c: (g, c, 0))
        self.lanes = pl.BlockSpec((k, LANES), lambda g, c: (c, g))
        self.mark = pl.BlockSpec((GROUP * k, toks), lambda g, c: (c * groups + g, 0))
        self.mark_t = pl.BlockSpec((toks, GROUP * k), lambda g, c: (0, c * groups + g))
        self.square = self.whole(dim, dim)
        self.w_specs = [pl.BlockSpec((None, dim, dim), lambda g, c, i=i: (i, 0, 0)) for i in range(2)]
        self.heads = self.whole(slots, wide)
        self.slot_rows = in_hbm((peers, slots, dim), BF)
        self.slot_heads = jax.ShapeDtypeStruct((slots, wide), F32)
        token = token.reshape(peers, self.split, k).transpose(1, 0, 2)
        self.token, self.token_t = self.call(
            token_marks_kernel,
            "token_marks",
            5,
            [
                pl.BlockSpec((GROUP * k, 1), lambda g, c: (c * groups + g, 0)),
                pl.BlockSpec((1, GROUP * k), lambda g, c: (0, c * groups + g)),
            ],
            [self.mark, self.mark_t],
            (in_hbm((peers * slots, toks), BF), in_hbm((toks, peers * slots), BF)),
        )(token.reshape(-1, 1), token.reshape(1, -1))

    @staticmethod
    def whole(*shape):
        return pl.BlockSpec(shape, lambda g, c: (0,) * len(shape))

    def call(self, kernel, name, micros, in_specs, out_specs, out_shape, scratch=(), mib=44):
        return pl.pallas_call(
            kernel,
            grid=self.grid,
            in_specs=in_specs,
            out_specs=out_specs,
            out_shape=out_shape,
            scratch_shapes=list(scratch),
            compiler_params=pltpu.CompilerParams(vmem_limit_bytes=mib * 1024 * 1024),
            cost_estimate=cost(micros),
            name=name,
        )

    def prepare(self, cross_q):
        self.query = self.call(
            query_rows_kernel,
            "query_rows",
            7,
            [self.mark, self.whole(self.toks, self.dim)],
            self.rows,
            self.slot_rows,
        )(self.token, cross_q)

    def forward(self, arrived, mats, bias):
        dim, toks = self.dim, self.toks
        self.arrived, self.mats = arrived, mats
        self.keys, self.vals, scores = self.call(
            rows_in_kernel,
            "rows_in",
            22,
            [self.rows, self.rows, *self.w_specs],
            [self.rows, self.rows, self.lanes],
            (self.slot_rows, self.slot_rows, self.slot_heads),
        )(from_hbm(arrived), from_hbm(self.query), mats, mats)
        entries = (self.ret * PITCH, toks)
        self.prob_tok, self.prob_slot, mixed = self.call(
            attend_kernel,
            "attend",
            11,
            [self.heads, self.rows, self.mark_t]
            + [self.whole(*self.at_rank.shape), self.whole(*self.owner.shape), self.whole(1, dim)],
            [self.whole(*entries), self.heads, self.whole(toks, dim)],
            (
                jax.ShapeDtypeStruct(entries, F32),
                self.slot_heads,
                jax.ShapeDtypeStruct((toks, dim), BF),
            ),
            [pltpu.VMEM((toks, dim), F32)],
        )(scores, from_hbm(self.vals), self.token_t, self.at_rank, self.owner, bias.reshape(1, dim))
        return mixed

    def backward(self, grad):
        dim, toks = self.dim, self.toks
        grads, self.grad_slot = self.call(
            attend_back_kernel,
            "attend_back",
            13,
            [self.rows, self.mark, self.whole(toks, dim), self.whole(self.ret * PITCH, toks)]
            + [self.whole(*self.at_rank.shape), self.whole(*self.owner.shape)],
            [self.rows, self.heads],
            (self.slot_rows, self.slot_heads),
            [pltpu.VMEM(self.slot_heads.shape, F32)],
        )(from_hbm(self.vals), self.token, grad, self.prob_tok, self.at_rank, self.owner)
        self.factors = (self.prob_slot, self.grad_slot, from_hbm(grads), from_hbm(self.query))
        self.factor_specs = [self.lanes, self.lanes, self.rows, self.rows]
        sent, self.flag = self.call(
            rows_out_kernel,
            "rows_out",
            28,
            self.factor_specs + self.w_specs,
            [self.rows, self.whole(8, LANES)],
            (self.slot_rows, jax.ShapeDtypeStruct((8, LANES), F32)),
        )(*self.factors, self.mats, self.mats)
        return sent

    def query_grad(self):
        dim, toks = self.dim, self.toks
        return self.call(
            query_back_kernel,
            "query_back",
            7,
            [self.rows, self.mark_t, self.lanes, self.whole(8, LANES)],
            self.whole(toks, dim),
            jax.ShapeDtypeStruct((toks, dim), BF),
            [pltpu.VMEM((toks, dim), F32)],
        )(from_hbm(self.keys), self.token_t, self.grad_slot, self.flag)

    def weights(self, after):
        square = (self.dim, self.dim)
        return self.call(
            rows_weights_kernel,
            "rows_weights",
            24,
            self.factor_specs + [self.rows] + [WAIT] * len(after),
            [self.square, self.square],
            (jax.ShapeDtypeStruct(square, BF), jax.ShapeDtypeStruct(square, BF)),
            [pltpu.VMEM(square, F32), pltpu.VMEM(square, F32)],
        )(*self.factors, from_hbm(self.arrived), *after)


class GatheredAttention:
    def __init__(self, ret_rows, shard_rows, peers, slots, dim):
        self.toks, self.ret = ret_rows.shape
        self.dim, self.slots = dim, slots
        self.place, self.wanted, self.entry = plan_requests(ret_rows, shard_rows, peers, slots)
        self.fwd, self.bwd, self.back_q = cross_calls(self.toks, self.ret, dim)

    def prepare(self, cross_q):
        self.cross_q = cross_q

    def forward(self, arrived, mats, bias):
        toks, dim = self.toks, self.dim
        w_k, w_v = mats[0], mats[1]
        self.key_heads, self.val_heads = w_k.reshape(dim, H, HD), w_v.reshape(dim, H, HD)
        query = self.cross_q.reshape(toks, H, HD)
        self.query_keys = jnp.einsum(
            "the,dhe->htd", query, self.key_heads, preferred_element_type=F32
        ).astype(BF)
        self.fetched = arrived.reshape(-1, dim)[self.place]
        self.state_mix, self.cross_p = self.fwd(self.query_keys, self.fetched)
        mixed = jnp.einsum(
            "htd,dhe->the", self.state_mix, self.val_heads, preferred_element_type=F32
        )
        return (mixed.reshape(toks, dim) + bias).astype(BF)

    def backward(self, grad):
        self.grad = grad.reshape(self.toks, H, HD)
        grad_mix = jnp.einsum(
            "the,dhe->htd", self.grad, self.val_heads, preferred_element_type=F32
        ).astype(BF)
        rows, self.grad_s = self.bwd(self.query_keys, grad_mix, self.fetched, self.cross_p)
        return rows[self.entry]

    def query_grad(self):
        self.grad_qk = self.back_q(self.grad_s, self.fetched)
        grad_q = jnp.einsum(
            "htd,dhe->the", self.grad_qk, self.key_heads, preferred_element_type=F32
        )
        return grad_q.reshape(self.toks, self.dim).astype(BF)

    def weights(self, after):
        def product(left, right):
            got = jnp.einsum("htd,the->dhe", left, right, preferred_element_type=F32)
            return got.reshape(self.dim, self.dim).astype(BF)

        grad_k = product(self.grad_qk, self.cross_q.reshape(self.toks, H, HD))
        return grad_k, product(self.state_mix, self.grad)


def store_sum_kernel(asked, returned, *refs, block, skip):
    first = (pl.program_id(0) + skip) * block + 1
    shape = (block, asked.shape[1])
    hit = lax.broadcasted_iota(jnp.int32, shape, 0) + first == asked[...]
    refs[-1][...] = mm(hit.astype(BF), returned[...])


def store_sum(asked, returned, shard_rows, part, so_far=(), after=()):
    count, dim = returned.shape
    block = 256
    steps = shard_rows // block // 2
    skip = part * steps
    return pl.pallas_call(
        functools.partial(store_sum_kernel, block=block, skip=skip),
        grid=(steps,),
        in_specs=[
            pl.BlockSpec((1, count), lambda g: (0, 0)),
            pl.BlockSpec((count, dim), lambda g: (0, 0)),
        ]
        + [WAIT] * (len(so_far) + len(after)),
        out_specs=pl.BlockSpec((block, dim), lambda g: (g + skip, 0)),
        out_shape=in_hbm((shard_rows, dim), F32),
        input_output_aliases={2: 0} if so_far else {},
        compiler_params=pltpu.CompilerParams(vmem_limit_bytes=VMEM_LIMIT),
        cost_estimate=cost(13),
        name="store_sum",
    )(asked.reshape(1, count), returned, *so_far, *after)


def all_to_all(array):
    return lax.all_to_all(array, RANKS, split_axis=0, concat_axis=0, tiled=True)


def on_device(
    tokens,
    seg_ids,
    live_mask,
    ret_rows,
    enc_store,
    attn_in,
    attn_out,
    ff_in,
    ff_out,
    biases,
    ln_gain,
    ln_shift,
    ff_bias,
    cotangent,
):
    n_rows = lax.axis_size("row")
    n_cols = lax.axis_size("col")
    peers = n_rows * n_cols
    tok_count, dim = tokens.shape
    shard_rows = enc_store.shape[0]
    ret = ret_rows.shape[1]
    slots = 3 * ret_rows.size // (2 * peers)
    rb, cb = attn_in.shape[1], attn_in.shape[2]
    order_a, order_b = bit_orders(n_rows, n_cols)
    n_row_bits = n_rows.bit_length() - 1
    n_far = n_row_bits - 2
    by_rows = n_cols == 2 and rb % 16 == 0 and cb % 128 == 0
    orders = (order_a, order_b, order_a, order_b)
    shapes = ((rb, cb), (rb, cb), (rb, 4 * cb), (4 * rb, cb))
    counts = (4, 4, 1, 1)
    if by_rows:
        col = lax.axis_index("col").astype(jnp.int32)[None]
        place_a = jnp.concatenate([block_of_row(order_a, n_rows), col])
        place_b = jnp.concatenate([block_of_row(order_b, n_rows), col])
        places = (place_a, place_b, place_a, place_b)

    in_slots = (
        by_rows
        and slots % (16 * SlotAttention.split) == 0
        and peers % GROUP == 0
        and tok_count % LANES == 0
        and tok_count <= 256
        and shard_rows & (shard_rows - 1) == 0
        and H <= PITCH
    )
    attention = (SlotAttention if in_slots else GatheredAttention)(
        ret_rows, shard_rows, peers, slots, dim
    )

    def vector_rows(parts):
        parts = [jnp.pad(part, ((0, 0), (0, cb - part.shape[1]))) for part in parts]
        return jnp.pad(jnp.concatenate(parts, axis=0), ((0, 2), (0, 0)))

    small = vector_rows([biases, ln_gain, ln_shift, ff_bias.reshape(1, -1)])
    packs = [*join(attn_in, attn_out, small, attention.wanted), ff_in[None], ff_out[None]]
    packs = [gather_bits(p, order[:1]) for p, order in zip(packs, orders)]
    asked = all_to_all(attention.wanted)
    asked = tie(asked, packs[:2]) if by_rows else asked
    packs = [gather_bits(p, order[1:n_far]) for p, order in zip(packs, orders)]

    answer = enc_store[jnp.maximum(asked - 1, 0)]
    for i in range(2):
        packs[i] = gather_bits(packs[i], orders[i][n_far : n_far + 1])
    arrived = all_to_all(hold(answer, packs) if by_rows else answer)
    if in_slots:
        packs[0] = hold(packs[0], [attention.token, attention.token_t])
    extras = (0, small.shape[0], 0, 0)

    def whole(i, after=()):
        done = n_far + 1
        if by_rows:
            got = swap_bit(packs[i], *orders[i][done])
            own = hold(packs[i], after) if after else packs[i]
            own = jnp.concatenate([own, got], axis=0)
            other = swap_bit(own, "col", 1)
            return unpack(own, other, places[i], counts[i], shapes[i], extras[i])
        blocks = gather_bits(packs[i], orders[i][done:])
        return unpack_any(blocks, orders[i], counts[i], shapes[i], extras[i], n_rows, n_cols)

    mats = [whole(0), whole(1)]
    w_q, w_k, w_v = (mats[0][i] for i in range(3))
    w_co = mats[1][0][3]
    small_all = mats[1][1]
    small_all = small_all.astype(F32)
    vectors = small_all[:, :13, :rb].transpose(1, 0, 2).reshape(13, dim)
    bias_all, gain_all, shift_all = vectors[:7], vectors[7:10], vectors[10:]
    bias_ff = small_all[:, 13, : ff_bias.size].reshape(-1)

    *qkv, mixed, first, first_norm, first_scale, cross_q = self_fwd(
        tokens, seg_ids, live_mask, mats[0], mats[1][0], bias_all, gain_all, shift_all
    )
    first_low = first.astype(BF)

    attention.prepare(cross_q)
    if in_slots:
        for i in (2, 3):
            packs[i] = gather_bits(packs[i], orders[i][n_far : n_far + 1])
    else:
        for i in (2, 3):
            packs[i] = gather_bits(packs[i], orders[i][n_far : n_far + 1])
    cross_low = attention.forward(arrived, mats[1][0], bias_all[4])
    branch_two = mm(cross_low, w_co) + bias_all[5]
    second, second_norm, second_scale = norm_fwd(first + branch_two, gain_all[1], shift_all[1])
    second_low = second.astype(BF)

    after = [attention.query] if in_slots else []
    w_ff1, w_ff2 = whole(2, after)[0], whole(3, after)[0]
    hidden_act, hidden_slope = gelu_parts(mm(second_low, w_ff1) + bias_ff)
    hidden_low = hidden_act.astype(BF)
    branch_ffn = mm(hidden_low, w_ff2) + bias_all[6]
    final, final_norm, final_scale = norm_fwd(second + branch_ffn, gain_all[2], shift_all[2])
    output = final.astype(BF)
    cot = cotangent.astype(F32)
    grad_three = norm_back(cot, final_norm, final_scale, gain_all[2])
    grad_y = grad_three.astype(BF)
    grad_pre = (mm_nt(grad_y, w_ff2) * hidden_slope).astype(BF)
    grad_second = grad_three + mm_nt(grad_pre, w_ff1)
    grad_two = norm_back(grad_second, second_norm, second_scale, gain_all[1])
    grad_o2 = grad_two.astype(BF)
    grad_cmix = mm_nt(grad_o2, w_co).astype(BF)
    send_back = attention.backward(grad_cmix)
    returned = all_to_all(send_back)

    def packed(order, place, mats, small=None, after=()):
        if by_rows:
            return pack(mats, place, small, after)
        return pack_any(mats, order[::-1], small, n_rows, n_cols)

    def on_both(pairs, start, stop):
        return [
            scatter_bits(*pair, back[start:stop]) for pair, back in zip(pairs, (back_a, back_b))
        ]

    tile = (rb, cb)
    near = len(order_a) - n_far
    back_a, back_b = order_a[::-1], order_b[::-1]
    at_a, at_b = (place_a, place_b) if by_rows else (None, None)
    grad_cq = attention.query_grad()
    ff = [
        (order_a, at_a, [((second_low, grad_pre), tile, 4)]),
        (order_b, at_b, [((hidden_low, grad_y), (4 * rb, cb), 1)]),
    ]
    ff = [packed(*part, None, [grad_cq]) for part in ff]
    if by_rows:
        grad_cq = hold(grad_cq, [x for pair in ff for x in pair])
    grad_first, grad_one, grad_o, grad_q, grad_k, grad_v = self_bwd(
        grad_cq,
        grad_two,
        first_norm,
        first_scale,
        gain_all,
        qkv,
        seg_ids,
        live_mask,
        mats[0],
        mats[1][0],
    )
    grad_tokens = (
        grad_one + mm_nt(grad_q, w_q) + mm_nt(grad_k, w_k) + mm_nt(grad_v, w_v)
    )

    vectors, wide = vector_sums(
        [grad_q, grad_v, grad_o, grad_cq, grad_cmix, grad_o2, grad_y],
        [(grad_first, first_norm), (grad_second, second_norm), (cotangent, final_norm)],
        grad_pre,
    )
    vectors = vectors[:13].reshape(13, n_rows, rb).transpose(1, 0, 2)
    wide = wide.reshape(n_rows, 1, -1)
    grad_small = [
        jnp.pad(vectors, ((0, 0), (0, 0), (0, cb - rb))),
        jnp.pad(wide, ((0, 0), (0, 2), (0, cb - ff_bias.size))),
    ]
    grad_small = jnp.concatenate(grad_small, axis=1).astype(BF)
    attn_one = packed(
        order_a,
        at_a,
        [
            ((tokens, grad_q), tile, 1),
            ((tokens, grad_k), tile, 1),
            ((tokens, grad_v), tile, 1),
            ((first_low, grad_cq), tile, 1),
        ],
    )
    ff = on_both(ff, 0, near - 2)
    before = [*attn_one, ff[0][1], ff[1][1]] if in_slots else []
    grad_wk, grad_wv = attention.weights(before)
    attn_two = packed(
        order_b,
        at_b,
        [
            (grad_wk, tile, 1),
            (grad_wv, tile, 1),
            ((mixed, grad_o), tile, 1),
            ((cross_low, grad_o2), tile, 1),
        ],
        grad_small,
    )
    def join_pairs(pairs):
        return tuple(jnp.concatenate(both, axis=1) for both in zip(*pairs))

    ff = join_pairs(on_both(ff, near - 2, near))
    attn = join_pairs(on_both([attn_one, attn_two], 0, near))
    def behind(pair, array):
        return (hold(pair[0], [array]), pair[1]) if by_rows else pair

    rows = returned.reshape(-1, dim)
    grad_store = store_sum(asked, rows, shard_rows, 0)
    ff, attn = (scatter_bits(*behind(x, grad_store), back_a[near:-1]) for x in (ff, attn))
    last = join_pairs([attn, ff])
    grad_store = store_sum(asked, rows, shard_rows, 1, (grad_store,), (last[1],))
    keep, send = behind(last, grad_store)
    total = (keep + swap_bit(send, *order_a[0]))[0].astype(F32)
    total_a, total_b = total[: attn[0].shape[1]], total[attn[0].shape[1] :]

    sum_small = total_a[8 * rb :]
    return (
        output,
        grad_tokens,
        grad_store,
        total_a[: 6 * rb].reshape(6, rb, cb),
        total_a[6 * rb : 8 * rb].reshape(2, rb, cb),
        jnp.concatenate([total_b[k * rb : (k + 1) * rb] for k in range(4)], axis=1),
        total_b[4 * rb :],
        sum_small[:7, :rb],
        sum_small[7:10, :rb],
        sum_small[10:13, :rb],
        sum_small[13, : ff_bias.size],
    )


def solution(mesh):
    both = ("row", "col")
    return jax.shard_map(
        on_device,
        mesh=mesh,
        in_specs=(
            P(both, None),
            P(both, None),
            P(both, None),
            P(both, None),
            P(both, None),
            P(None, "row", "col"),
            P(None, "row", "col"),
            P("row", "col"),
            P("row", "col"),
            P(None, "row"),
            P(None, "row"),
            P(None, "row"),
            P("row"),
            P(both, None),
        ),
        out_specs=(
            P(both, None),
            P(both, None),
            P(both, None),
            P(None, "row", "col"),
            P(None, "row", "col"),
            P("row", "col"),
            P("row", "col"),
            P(None, "row"),
            P(None, "row"),
            P(None, "row"),
            P("row"),
        ),
        check_vma=False,
    )
```

```python
import functools

import jax
import jax.numpy as jnp
import numpy as np
from jax import lax
from jax.experimental import pallas as pl
from jax.experimental.pallas import tpu as pltpu
from jax.sharding import PartitionSpec as P

H = 12
HD = 64
RANKS = ("row", "col")
BF = jnp.bfloat16
F32 = jnp.float32
VMEM_LIMIT = 60 * 1024 * 1024


def mm(a, b):
    return jnp.dot(a, b, preferred_element_type=F32)


def mm_nt(a, b):
    return lax.dot_general(a, b, (((1,), (1,)), ((), ())), preferred_element_type=F32)


def mm_tn(a, b):
    return lax.dot_general(a, b, (((0,), (0,)), ((), ())), preferred_element_type=F32)


def norm_fwd(resid, gain, shift):
    row_mean = jnp.mean(resid, axis=-1, keepdims=True)
    centered = resid - row_mean
    inv_std = lax.rsqrt(jnp.mean(centered * centered, axis=-1, keepdims=True) + 1e-05)
    normed = centered * inv_std
    return (normed * gain + shift, normed, inv_std)


def norm_back(grad_in, normed, inv_std, gain):
    scaled = grad_in * gain
    return inv_std * (
        scaled
        - jnp.mean(scaled, axis=-1, keepdims=True)
        - normed * jnp.mean(scaled * normed, axis=-1, keepdims=True)
    )


def gelu_parts(pre_act):
    cdf_part = 0.5 * (1.0 + lax.erf(pre_act * 0.7071067811865476))
    density = jnp.exp(-0.5 * pre_act * pre_act) * 0.3989422804014327
    return (pre_act * cdf_part, cdf_part + pre_act * density)


def column_sum(array):
    return jnp.sum(array.astype(F32), axis=0)


def bit_orders(n_rows, n_cols):
    row_bits = [("row", 1 << b) for b in reversed(range(n_rows.bit_length() - 1))]
    col_bits = [("col", 1 << b) for b in reversed(range(n_cols.bit_length() - 1))]
    swapped = row_bits[:-2] + row_bits[-1:] + row_bits[-2:-1]
    return row_bits + col_bits, swapped + col_bits


def swap_bit(array, axis, bit):
    pairs = [(i, i ^ bit) for i in range(lax.axis_size(axis))]
    return lax.ppermute(array, axis, pairs)


def gather_bits(blocks, order):
    for axis, bit in order:
        blocks = jnp.concatenate([blocks, swap_bit(blocks, axis, bit)], axis=0)
    return blocks


def scatter_bits(keep, send, order):
    for axis, bit in order:
        got = swap_bit(send, axis, bit)
        half = keep.shape[0] // 2
        keep, send = keep[:half] + got[:half], keep[half:] + got[half:]
    return keep, send


def block_of_row(order, n_rows):
    apart = np.zeros(n_rows, np.int32)
    for k, (_, bit) in enumerate(order[: n_rows.bit_length() - 1]):
        apart[(np.arange(n_rows) >> k) & 1 == 1] ^= bit
    table = np.zeros(n_rows, np.int32)
    table[apart] = np.arange(n_rows)
    return jnp.asarray(table)[lax.axis_index("row") ^ jnp.arange(n_rows, dtype=jnp.int32)]


def flip_by_position(blocks, stages):
    for k, (axis, bit) in enumerate(stages):
        here = (lax.axis_index(axis) & bit) != 0
        blocks = jnp.where(here, jnp.flip(blocks, axis=k), blocks)
    return blocks


def by_device(blocks, order):
    stages = order[::-1]
    shape = blocks.shape[1:]
    blocks = flip_by_position(blocks.reshape((2,) * len(stages) + shape), stages)
    rank = sorted(range(len(stages)), key=lambda k: (stages[k][0] == "col", -stages[k][1]))
    rest = list(range(len(stages), blocks.ndim))
    return blocks.transpose(rank + rest).reshape((-1,) + shape)


def by_stage(blocks, stages):
    shape = blocks.shape[1:]
    rank = sorted(range(len(stages)), key=lambda k: (stages[k][0] == "col", -stages[k][1]))
    rest = list(range(len(stages), len(stages) + len(shape)))
    back = [rank.index(k) for k in range(len(stages))]
    blocks = blocks.reshape((2,) * len(stages) + shape).transpose(back + rest)
    return flip_by_position(blocks, stages).reshape((-1,) + shape)


def cost(micros):
    return pl.CostEstimate(flops=int(micros * 1.1e9), bytes_accessed=0, transcendentals=0)


WAIT = pl.BlockSpec(memory_space=pltpu.HBM)


def in_hbm(shape, dtype):
    return pltpu.HBM(shape=shape, dtype=dtype)


def from_hbm(array):
    return pltpu.with_memory_space_constraint(array, pltpu.HBM)


def tie_kernel(*refs):
    refs[-1][...] = refs[0][...]


def tie(array, after):
    return pl.pallas_call(
        tie_kernel,
        in_specs=[pl.BlockSpec(memory_space=pltpu.VMEM)] + [WAIT] * len(after),
        out_shape=jax.ShapeDtypeStruct(array.shape, array.dtype),
        name="tie",
    )(array, *after)


def hold_kernel(*refs):
    del refs


def hold(array, after):
    return pl.pallas_call(
        hold_kernel,
        in_specs=[WAIT] * (1 + len(after)),
        out_specs=WAIT,
        out_shape=jax.ShapeDtypeStruct(array.shape, array.dtype),
        input_output_aliases={0: 0},
        name="hold",
    )(array, *after)


def tile_of(buf, k, r, c, shape):
    rows, cols = shape
    return buf.at[
        k, pl.ds(pl.multiple_of(r * rows, rows), rows), pl.ds(pl.multiple_of(c * cols, cols), cols)
    ]


def unpack_kernel(place, own, other, *refs, count, shape, extra):
    outs, (buf, *more) = refs[: 1 + bool(extra)], refs[1 + bool(extra) :]
    sems = more[-1]
    n_rows, col, rows = own.shape[0], place[own.shape[0]], shape[0]

    def fill(r, carry):
        j = place[r]
        for src, c, sem in ((own, col, 0), (other, 1 - col, 1)):
            for k in range(count):
                part = src.at[j, pl.ds(k * rows, rows)]
                pltpu.make_async_copy(part, tile_of(buf, k, r, c, shape), sems.at[sem]).start()
        if extra:
            tail = own.at[j, pl.ds(count * rows, extra)]
            pltpu.make_async_copy(tail, more[0].at[r], sems.at[2]).start()
        return carry

    lax.fori_loop(0, n_rows, fill, 0)
    body = own.at[:, pl.ds(0, count * rows)]
    for sem in range(2):
        pltpu.make_async_copy(body, body, sems.at[sem]).wait()
    out = pltpu.make_async_copy(buf, outs[0], sems.at[3])
    out.start()
    if extra:
        pltpu.make_async_copy(more[0], more[0], sems.at[2]).wait()
        tails = pltpu.make_async_copy(more[0], outs[1], sems.at[4])
        tails.start()
        tails.wait()
    out.wait()


def unpack(own, other, place, count, shape, extra=0):
    n_rows = own.shape[0]
    rows, cols = shape
    whole = jax.ShapeDtypeStruct((count, n_rows * rows, 2 * cols), BF)
    tails = jax.ShapeDtypeStruct((n_rows, extra, cols), BF)
    shapes = [whole] + [tails] * bool(extra)
    got = pl.pallas_call(
        functools.partial(unpack_kernel, count=count, shape=shape, extra=extra),
        in_specs=[pl.BlockSpec(memory_space=pltpu.SMEM)] + [pl.BlockSpec(memory_space=pl.ANY)] * 2,
        out_specs=[pl.BlockSpec(memory_space=pl.ANY)] * len(shapes),
        out_shape=shapes,
        scratch_shapes=[pltpu.VMEM(x.shape, BF) for x in shapes] + [pltpu.SemaphoreType.DMA((5,))],
        compiler_params=pltpu.CompilerParams(vmem_limit_bytes=32 * 1024 * 1024),
        cost_estimate=pl.CostEstimate(
            flops=0, bytes_accessed=4 * whole.size * 2, transcendentals=0
        ),
        name="unpack",
    )(place, own, other)
    return got if extra else got[0]


def join_kernel(attn_in, attn_out, small, waited, one, two, *, rb):
    del waited
    for k in range(4):
        one[0, k * rb : (k + 1) * rb] = attn_in[k]
    for k in range(2):
        two[0, k * rb : (k + 1) * rb] = attn_in[4 + k]
        two[0, (2 + k) * rb : (3 + k) * rb] = attn_out[k]
    two[0, 4 * rb :] = small[...]


def join(attn_in, attn_out, small, after):
    rb, cb = attn_in.shape[1:]
    if rb % 16 or cb % 128:
        two = [attn_in[4:].reshape(-1, cb), attn_out.reshape(-1, cb), small]
        return attn_in[:4].reshape(1, -1, cb), jnp.concatenate(two, axis=0)[None]
    return pl.pallas_call(
        functools.partial(join_kernel, rb=rb),
        in_specs=[pl.BlockSpec(memory_space=pltpu.VMEM)] * 3 + [WAIT],
        out_shape=(
            jax.ShapeDtypeStruct((1, 4 * rb, cb), BF),
            jax.ShapeDtypeStruct((1, 4 * rb + small.shape[0], cb), BF),
        ),
        name="join",
    )(attn_in, attn_out, small, after)


def pack_kernel(place, *refs, mats, rows, extra, waits):
    n_ops = 1 + max(max(mat[0]) for mat in mats)
    ops, refs = refs[:n_ops], refs[n_ops:]
    small, refs = refs[: bool(extra)], refs[bool(extra) + waits :]
    keep, send, *bufs, sems = refs
    n_rows, col = keep.shape[0], place[keep.shape[0]]
    loads = {}
    for k, (at, _, _) in enumerate(mats):
        if len(at) == 1:
            loads[k] = pltpu.make_async_copy(ops[at[0]], bufs[k].at[0], sems.at[2 + k])
            loads[k].start()
    for k, (at, _, _) in enumerate(mats):
        if len(at) == 2:
            left, right = ops[at[0]], ops[at[1]]
            _, tall, wide = bufs[k].shape
            tile = min(tall, wide)
            for i in range(0, tall, tile):
                for j in range(0, wide, tile):
                    got = mm_tn(left[:, i : i + tile], right[:, j : j + tile])
                    bufs[k][0, i : i + tile, j : j + tile] = got.astype(BF)
    for load in loads.values():
        load.wait()

    def spread(r, carry):
        j = place[r]
        for dst, c, sem in ((keep, col, 0), (send, 1 - col, 1)):
            first = 0
            for buf, (_, shape, beside) in zip(bufs, mats):
                for k in range(beside):
                    part = dst.at[j, pl.ds(first, shape[0])]
                    tile = tile_of(buf, 0, r, c * beside + k, shape)
                    pltpu.make_async_copy(tile, part, sems.at[sem]).start()
                    first += shape[0]
            if extra:
                tail = dst.at[j, pl.ds(first, extra)]
                pltpu.make_async_copy(small[0].at[r], tail, sems.at[sem]).start()
        return carry

    lax.fori_loop(0, n_rows, spread, 0)
    for dst, sem in ((keep, 0), (send, 1)):
        pltpu.make_async_copy(dst, dst, sems.at[sem]).wait()


def pack(mats, place, small=None, after=()):
    ops, parts, specs, bufs, flops, total = [], [], [], [], 0, 0
    for mat, shape, beside in mats:
        mat = mat if isinstance(mat, tuple) else (mat,)
        parts.append((tuple(range(len(ops), len(ops) + len(mat))), shape, beside))
        ops += mat
        specs += [pl.BlockSpec(memory_space=pltpu.VMEM if len(mat) == 2 else pl.ANY)] * len(mat)
        whole = (mat[0].shape[1], mat[1].shape[1]) if len(mat) == 2 else mat[0].shape
        bufs.append(pltpu.VMEM((1,) + tuple(whole), BF))
        flops += 2 * mat[0].shape[0] * whole[0] * whole[1] if len(mat) == 2 else 0
        total += beside * shape[0]
        n_rows = whole[0] // shape[0]
    extra = 0 if small is None else small.shape[1]
    block = in_hbm((n_rows, total + extra, shape[1]), BF)
    if extra:
        ops.append(small)
        specs.append(pl.BlockSpec(memory_space=pltpu.VMEM))
    return pl.pallas_call(
        functools.partial(
            pack_kernel, mats=tuple(parts), rows=total, extra=extra, waits=len(after)
        ),
        in_specs=[pl.BlockSpec(memory_space=pltpu.SMEM)] + specs + [WAIT] * len(after),
        out_specs=[pl.BlockSpec(memory_space=pl.ANY)] * 2,
        out_shape=[block, block],
        scratch_shapes=bufs + [pltpu.SemaphoreType.DMA((2 + len(mats),))],
        compiler_params=pltpu.CompilerParams(vmem_limit_bytes=48 * 1024 * 1024),
        cost_estimate=pl.CostEstimate(
            flops=flops, bytes_accessed=8 * n_rows * total * shape[1], transcendentals=0
        ),
        name="pack",
    )(place, *ops, *after)


def unpack_any(blocks, order, count, shape, extra, n_rows, n_cols):
    rows, cols = shape
    got = by_device(blocks, order).reshape(n_rows, n_cols, -1, cols)
    mats = got[:, :, : count * rows].reshape(n_rows, n_cols, count, rows, cols)
    mats = mats.transpose(2, 0, 3, 1, 4).reshape(count, n_rows * rows, n_cols * cols)
    return (mats, got[:, 0, count * rows :]) if extra else mats


def pack_any(mats, order, small, n_rows, n_cols):
    got = []
    for mat, (rows, cols), beside in mats:
        mat = mm_tn(*mat).astype(BF) if isinstance(mat, tuple) else mat
        mat = mat.reshape(n_rows, rows, n_cols, beside, cols).transpose(0, 2, 3, 1, 4)
        got.append(mat.reshape(n_rows, n_cols, beside * rows, cols))
    if small is not None:
        got.append(jnp.broadcast_to(small[:, None], (n_rows, n_cols) + small.shape[1:]))
    got = jnp.concatenate(got, axis=2)
    got = by_stage(got.reshape((-1,) + got.shape[2:]), order)
    half = got.shape[0] // 2
    return got[:half], got[half:]


def plan_requests(ret_rows, shard_rows, peers, slots):
    flat = ret_rows.reshape(-1)
    count = flat.shape[0]
    owner = flat // shard_rows
    local_row = flat - owner * shard_rows
    mine = owner[:, None] == jnp.arange(peers, dtype=jnp.int32)[None, :]
    run = 256
    runs = count // run
    ones = mine.astype(BF).reshape(runs, run, peers)
    lower = jnp.tril(jnp.ones((run, run), BF))
    within = jnp.einsum("ij,bjo->bio", lower, ones, preferred_element_type=F32)
    totals = within[:, -1, :]
    before = jnp.cumsum(totals, axis=0) - totals
    upto = (within + before[:, None, :]).reshape(count, peers)
    rank = jnp.sum(jnp.where(mine, upto, 0.0), axis=1).astype(jnp.int32) - 1
    place = owner * slots + rank
    row_code = local_row + 1
    entry_code = jnp.arange(count, dtype=jnp.int32)
    digits = jnp.stack([row_code // 64, row_code % 64, entry_code // 64, entry_code % 64])
    left = jnp.where(mine.T[None], digits[:, None, :], 0).astype(BF)
    at_rank = (rank[:, None] == jnp.arange(slots, dtype=jnp.int32)[None, :]).astype(BF)
    codes = mm(left.reshape(4 * peers, count), at_rank).astype(jnp.int32).reshape(4, peers, slots)
    return place, codes[0] * 64 + codes[1], codes[2] * 64 + codes[3]


def row_norm(resid):
    centered = resid - jnp.mean(resid, axis=-1, keepdims=True)
    scale = lax.rsqrt(jnp.mean(centered * centered, axis=-1, keepdims=True) + 1e-05)
    return centered * scale, scale


def head_masks():
    lane = lax.broadcasted_iota(jnp.int32, (1, 2 * HD), 1)
    return [(lane // HD == i).astype(F32).astype(BF) for i in range(2)]


def self_probs(query, key, visible):
    scores = jnp.where(visible, mm_nt(query, key) * (HD**-0.5), -1e30)
    expo = jnp.exp(scores - jnp.max(scores, axis=-1, keepdims=True))
    return expo / jnp.sum(expo, axis=-1, keepdims=True)


def visible_pairs(seg_col, seg_row, live_row):
    shape = (seg_col.shape[0], seg_row.shape[1])
    at_query = lax.broadcasted_iota(jnp.int32, shape, 0)
    at_key = lax.broadcasted_iota(jnp.int32, shape, 1)
    return (
        (at_key <= at_query)
        & (seg_col[...] == seg_row[...])
        & ((live_row[...] == 1) | (at_key == at_query))
    )


def self_fwd_kernel(*refs):
    tokens, seg_col, seg_row, live_row, w_qkvc, w_o, bias, gain, shift = refs[:9]
    queries, keys, values, mixed, first, normed, scale, cross_q = refs[9:]
    x = tokens[...]
    queries[...] = (mm(x, w_qkvc[0]) + bias[0:1]).astype(BF)
    keys[...] = mm(x, w_qkvc[1]).astype(BF)
    values[...] = (mm(x, w_qkvc[2]) + bias[1:2]).astype(BF)
    visible = visible_pairs(seg_col, seg_row, live_row)
    for pair in range(H // 2):
        lanes = slice(2 * HD * pair, 2 * HD * (pair + 1))
        total = 0.0
        for mask in head_masks():
            prob = self_probs(queries[:, lanes], keys[:, lanes] * mask, visible)
            total = total + mm(prob.astype(BF), values[:, lanes] * mask)
        mixed[:, lanes] = total.astype(BF)
    resid = x.astype(F32) + mm(mixed[...], w_o[...]) + bias[2:3]
    norm, inv = row_norm(resid)
    normed[...] = norm
    scale[...] = jnp.broadcast_to(inv, scale.shape)
    out = norm * gain[0:1] + shift[0:1]
    first[...] = out
    cross_q[...] = (mm(out.astype(BF), w_qkvc[3]) + bias[3:4]).astype(BF)


def one_step(ops, picks):
    specs = []
    for i, op in enumerate(ops):
        block, at = op.shape, (0,) * op.ndim
        if i in picks:
            block, at = (None,) + op.shape[1:], (picks[i],) + at[1:]
        specs.append(pl.BlockSpec(block, lambda g, at=at: at))
    return specs


def self_fwd(tokens, seg, live, w_qkvc, mats, bias, gain, shift):
    toks, dim = tokens.shape
    ops = (tokens, seg.reshape(toks, 1), seg, live, w_qkvc, mats, bias, gain, shift)
    low = jax.ShapeDtypeStruct((toks, dim), BF)
    full = jax.ShapeDtypeStruct((toks, dim), F32)
    column = jax.ShapeDtypeStruct((toks, 128), F32)
    return pl.pallas_call(
        self_fwd_kernel,
        grid=(1,),
        in_specs=one_step(ops, {5: 2}),
        out_specs=one_step((low, low, low, low, full, full, column, low), {}),
        out_shape=(low, low, low, low, full, full, column, low),
        compiler_params=pltpu.CompilerParams(vmem_limit_bytes=28 * 1024 * 1024),
        cost_estimate=cost(5),
        name="self_fwd",
    )(*ops)


def self_bwd_kernel(*refs):
    grad_cq, grad_two, normed, scale, gain, queries, keys, values = refs[:8]
    seg_col, seg_row, live_row, w_qkvc, w_o = refs[8:13]
    grad_first, grad_one, grad_o, grad_q, grad_k, grad_v, grad_mix = refs[13:]
    incoming = grad_two[...] + mm_nt(grad_cq[...], w_qkvc[3])
    grad_first[...] = incoming
    one = norm_back(incoming, normed[...], scale[:, 0:1], gain[0:1])
    grad_one[...] = one
    low = one.astype(BF)
    grad_o[...] = low
    grad_mix[...] = mm_nt(low, w_o[...]).astype(BF)
    visible = visible_pairs(seg_col, seg_row, live_row)
    for pair in range(H // 2):
        lanes = slice(2 * HD * pair, 2 * HD * (pair + 1))
        by_query, by_key, by_value = 0.0, 0.0, 0.0
        for mask in head_masks():
            query, key = queries[:, lanes] * mask, keys[:, lanes] * mask
            grad = grad_mix[:, lanes] * mask
            prob = self_probs(query, key, visible)
            grad_p = mm_nt(grad, values[:, lanes])
            dot = jnp.sum(prob * grad_p, axis=-1, keepdims=True)
            grad_s = (prob * (grad_p - dot)).astype(BF)
            by_query = by_query + mm(grad_s, key)
            by_key = by_key + mm_tn(grad_s, query)
            by_value = by_value + mm_tn(prob.astype(BF), grad)
        grad_q[:, lanes] = (by_query * (HD**-0.5)).astype(BF)
        grad_k[:, lanes] = (by_key * (HD**-0.5)).astype(BF)
        grad_v[:, lanes] = by_value.astype(BF)


def self_bwd(grad_cq, grad_two, normed, scale, gain, qkv, seg, live, w_qkvc, mats):
    toks, dim = grad_two.shape
    ops = (grad_cq, grad_two, normed, scale, gain, *qkv)
    ops += (seg.reshape(toks, 1), seg, live, w_qkvc, mats)
    low = jax.ShapeDtypeStruct((toks, dim), BF)
    full = jax.ShapeDtypeStruct((toks, dim), F32)
    return pl.pallas_call(
        self_bwd_kernel,
        grid=(1,),
        in_specs=one_step(ops, {12: 2}),
        out_specs=one_step((full, full, low, low, low, low), {}),
        out_shape=(full, full, low, low, low, low),
        scratch_shapes=[pltpu.VMEM((toks, dim), BF)],
        compiler_params=pltpu.CompilerParams(vmem_limit_bytes=28 * 1024 * 1024),
        cost_estimate=cost(6),
        name="self_bwd",
    )(*ops)


def own_rows(tokens, ret, heads):
    shape = (heads * tokens, tokens * ret)
    row_tok = lax.broadcasted_iota(jnp.int32, shape, 0) % tokens
    col_tok = lax.broadcasted_iota(jnp.int32, shape, 1) // ret
    return row_tok == col_tok


def cross_fwd_kernel(qk, fetched, mix, probs, *, ret):
    heads, tokens, dim = qk.shape
    own = own_rows(tokens, ret, heads)
    query = qk[...].reshape(heads * tokens, dim)
    rows = fetched[...]
    scores = jnp.where(own, mm_nt(query, rows) * 0.125, -1e30)
    expo = jnp.exp(scores - jnp.max(scores, axis=-1, keepdims=True))
    prob = expo / jnp.sum(expo, axis=-1, keepdims=True)
    probs[0] = prob
    mix[...] = mm(prob.astype(BF), rows).astype(BF).reshape(heads, tokens, dim)


def cross_bwd_kernel(qk, gmix, fetched, probs, grad_rows, grad_s, *, ret):
    heads, tokens, dim = qk.shape
    query = qk[...].reshape(heads * tokens, dim)
    grad_mix = gmix[...].reshape(heads * tokens, dim)
    prob = probs[0]
    grad_p = mm_nt(grad_mix, fetched[...])
    g_s = (prob * (grad_p - jnp.sum(prob * grad_p, axis=-1, keepdims=True))).astype(BF)
    grad_s[0] = g_s
    grad_rows[...] = (
        mm_tn(prob.astype(BF), grad_mix) + mm_tn(g_s, query) * 0.125
    ).astype(BF)


def cross_back_q_kernel(grad_s, fetched, grad_qk):
    heads, tokens, dim = grad_qk.shape
    got = mm(grad_s[0], fetched[...]) * 0.125
    grad_qk[...] = got.astype(BF).reshape(heads, tokens, dim)


def cross_calls(tok_count, ret, dim):
    tb = 16
    blocks = tok_count // tb
    by_head = pl.BlockSpec((H, tb, dim), lambda g: (0, g, 0))
    rows = pl.BlockSpec((tb * ret, dim), lambda g: (g, 0))
    square = pl.BlockSpec((1, H * tb, tb * ret), lambda g: (g, 0, 0))
    heads_shape = jax.ShapeDtypeStruct((H, tok_count, dim), BF)
    square_f32 = jax.ShapeDtypeStruct((blocks, H * tb, tb * ret), F32)
    square_bf = jax.ShapeDtypeStruct((blocks, H * tb, tb * ret), BF)
    params = pltpu.CompilerParams(vmem_limit_bytes=VMEM_LIMIT)
    fwd = pl.pallas_call(
        functools.partial(cross_fwd_kernel, ret=ret),
        grid=(blocks,),
        in_specs=[by_head, rows],
        out_specs=[by_head, square],
        out_shape=(heads_shape, square_f32),
        compiler_params=params,
        name="cross_fwd",
    )
    bwd = pl.pallas_call(
        functools.partial(cross_bwd_kernel, ret=ret),
        grid=(blocks,),
        in_specs=[by_head, by_head, rows, square],
        out_specs=[rows, square],
        out_shape=(jax.ShapeDtypeStruct((tok_count * ret, dim), BF), square_bf),
        compiler_params=params,
        name="cross_bwd",
    )
    back_q = pl.pallas_call(
        cross_back_q_kernel,
        grid=(blocks,),
        in_specs=[square, rows],
        out_specs=by_head,
        out_shape=heads_shape,
        compiler_params=params,
        name="cross_back_q",
    )
    return fwd, bwd, back_q


GROUP = 8
LANES = 128
PITCH = LANES // GROUP
TILE = 256


def plan_kernel(rows, wanted, token, at_rank, owner, *, shard_rows):
    peers, slots = wanted.shape
    ret, toks = rows.shape
    shape = (toks, toks)
    upper = (
        lax.broadcasted_iota(jnp.int32, shape, 0) <= lax.broadcasted_iota(jnp.int32, shape, 1)
    ).astype(BF)
    peer = lax.broadcasted_iota(jnp.int32, (peers, toks), 0)
    tok_code = (lax.broadcasted_iota(jnp.int32, (peers, toks), 1) + 1).astype(F32)
    k_rows = lax.broadcasted_iota(jnp.int32, (at_rank.shape[0], toks), 0)
    shift = shard_rows.bit_length() - 1
    before = jnp.zeros((peers, 1), F32)
    codes = jnp.zeros((3 * peers, at_rank.shape[0]), F32)
    for r in range(ret):
        row = rows[r : r + 1, :]
        own = lax.shift_right_logical(row, shift)
        code = lax.bitwise_and(row, shard_rows - 1) + 1
        mine = own == peer
        upto = mm(mine.astype(BF), upper) + before
        before = upto[:, toks - 1 :]
        rank = jnp.sum(jnp.where(mine, upto, 0.0), axis=0, keepdims=True).astype(jnp.int32) - 1
        at = (k_rows == rank).astype(BF)
        at_rank[:, r * toks : (r + 1) * toks] = at
        owner[r : r + 1, :] = own
        high = lax.shift_right_logical(code, 6).astype(F32)
        low = lax.bitwise_and(code, 63).astype(F32)
        left = jnp.concatenate(
            [
                jnp.where(mine, high, 0.0).astype(BF),
                jnp.where(mine, low, 0.0).astype(BF),
                jnp.where(mine, tok_code, 0.0).astype(BF),
            ],
            axis=0,
        )
        codes = codes + mm_nt(left, at)
    codes = codes[:, :slots].astype(jnp.int32)
    wanted[...] = codes[:peers] * 64 + codes[peers : 2 * peers]
    token[...] = codes[2 * peers :]


def plan_slots(rows, shard_rows, peers, slots):
    ret, toks = rows.shape
    tall = -(-slots // LANES) * LANES
    return pl.pallas_call(
        functools.partial(plan_kernel, shard_rows=shard_rows),
        out_shape=(
            jax.ShapeDtypeStruct((peers, slots), jnp.int32),
            jax.ShapeDtypeStruct((peers, slots), jnp.int32),
            jax.ShapeDtypeStruct((tall, ret * toks), BF),
            jax.ShapeDtypeStruct((ret, toks), jnp.int32),
        ),
        cost_estimate=cost(4),
        name="plan",
    )(rows)


def head_sum(dim):
    shape = (dim, LANES)
    head = lax.broadcasted_iota(jnp.int32, shape, 0) // HD
    return (head == lax.broadcasted_iota(jnp.int32, shape, 1)).astype(BF)


def head_spread(dim):
    shape = (LANES, dim)
    head = lax.broadcasted_iota(jnp.int32, shape, 1) // HD
    return (head == lax.broadcasted_iota(jnp.int32, shape, 0)).astype(BF)


def to_lanes(by_peer, k):
    total = by_peer[:k]
    for q in range(1, GROUP):
        total = total + pltpu.roll(by_peer[q * k : (q + 1) * k], PITCH * q, 1)
    return total


def from_lanes(lanes):
    parts = [lanes] + [pltpu.roll(lanes, LANES - PITCH * q, 1) for q in range(1, GROUP)]
    return jnp.concatenate([part.astype(BF) for part in parts], axis=0)


def to_entries(slot_vals, at_rank, owner):
    k, wide = slot_vals.shape
    tall, toks = at_rank.shape[0], owner.shape[1]
    peers = wide // PITCH
    full = jnp.concatenate([slot_vals, jnp.zeros((tall - k, wide), F32)], axis=0).T
    high = full.astype(BF)
    low = (full - high.astype(F32)).astype(BF)
    peer = lax.broadcasted_iota(jnp.int32, (wide, toks), 0) // PITCH
    out = []
    for r in range(owner.shape[0]):
        at = at_rank[:, r * toks : (r + 1) * toks]
        got = mm(high, at) + mm(low, at)
        got = jnp.where(peer == owner[r : r + 1, :], got, 0.0)
        out.append(jnp.sum(got.reshape(peers, PITCH, toks), axis=0))
    return out


def to_slots(entry_vals, at_rank, owner, peers, slots):
    toks = owner.shape[1]
    wide = peers * PITCH
    peer = lax.broadcasted_iota(jnp.int32, (wide, toks), 0) // PITCH
    total = jnp.zeros((at_rank.shape[0], wide), F32)
    for r, vals in enumerate(entry_vals):
        tiled = jnp.concatenate([vals] * peers, axis=0)
        mine = jnp.where(peer == owner[r : r + 1, :], tiled, 0.0).astype(BF)
        total = total + mm_nt(at_rank[:, r * toks : (r + 1) * toks], mine)
    return total[:slots]


def token_marks_kernel(column, row, marks, marks_t):
    marks[...] = (
        column[...] == lax.broadcasted_iota(jnp.int32, marks.shape, 1) + 1
    ).astype(BF)
    marks_t[...] = (row[...] == lax.broadcasted_iota(jnp.int32, marks_t.shape, 0) + 1).astype(BF)


def query_rows_kernel(token, query, out):
    out[...] = mm(token[...], query[...]).astype(BF).reshape(out.shape)


def rows_in_kernel(arrived, query, w_k, w_v, keys, vals, scores):
    group, k, dim = arrived.shape
    rows = arrived[...].reshape(group * k, dim)
    total = jnp.zeros((group * k, LANES), F32)
    for at in range(0, dim, TILE):
        tile = slice(at, at + TILE)
        key = mm(rows, w_k[:, tile])
        keys[:, :, tile] = key.astype(BF).reshape(group, k, TILE)
        prod = (key * query[:, :, tile].reshape(group * k, TILE).astype(F32)).astype(BF)
        total = total + mm(prod, head_sum(dim)[tile])
        vals[:, :, tile] = mm(rows, w_v[:, tile]).astype(BF).reshape(group, k, TILE)
    scores[...] = to_lanes(total, k) * 0.125


def attend_kernel(
    scores, vals, token_t, at_rank, owner, bias, prob_tok, prob_slot, mixed, total
):
    step, part = pl.program_id(0), pl.program_id(1)
    k, dim = vals.shape[1:]
    slots, wide = scores.shape

    @pl.when((step == 0) & (part == 0))
    def _():
        entry = to_entries(scores[...], at_rank, owner)
        top = functools.reduce(jnp.maximum, entry)
        expo = [jnp.exp(part - top) for part in entry]
        norm = functools.reduce(jnp.add, expo)
        probs = [part / norm for part in expo]
        for r, part in enumerate(probs):
            prob_tok[r * PITCH : (r + 1) * PITCH, :] = part
        prob_slot[...] = to_slots(probs, at_rank, owner, wide // PITCH, slots)
        total[...] = jnp.zeros_like(total)

    lanes = pl.ds(pl.multiple_of(step * LANES, LANES), LANES)
    here = pl.ds(pl.multiple_of(part * k, 16), k)
    prob = mm(from_lanes(prob_slot[here, lanes]), head_spread(dim))
    prod = (prob * vals[...].reshape(-1, dim).astype(F32)).astype(BF)
    total[...] += mm(token_t[...], prod)

    @pl.when((step == pl.num_programs(0) - 1) & (part == pl.num_programs(1) - 1))
    def _():
        mixed[...] = (total[...] + bias[...]).astype(BF)


def attend_back_kernel(
    vals, token, grad, prob_tok, at_rank, owner, grads, grad_slot, slot_p
):
    step, part = pl.program_id(0), pl.program_id(1)
    k, dim = vals.shape[1:]
    slots, wide = slot_p.shape
    lanes = pl.ds(pl.multiple_of(step * LANES, LANES), LANES)
    here = pl.ds(pl.multiple_of(part * k, 16), k)
    rows = mm(token[...], grad[...])
    grads[...] = rows.astype(BF).reshape(vals.shape)
    prod = (rows * vals[...].reshape(-1, dim).astype(F32)).astype(BF)
    slot_p[here, lanes] = to_lanes(mm(prod, head_sum(dim)), k)

    @pl.when((step == pl.num_programs(0) - 1) & (part == pl.num_programs(1) - 1))
    def _():
        entry = to_entries(slot_p[...], at_rank, owner)
        probs = [prob_tok[r * PITCH : (r + 1) * PITCH, :] for r in range(len(entry))]
        dots = functools.reduce(jnp.add, [p * g for p, g in zip(probs, entry)])
        scores = [(p * (g - dots)).astype(BF).astype(F32) for p, g in zip(probs, entry)]
        grad_slot[...] = to_slots(scores, at_rank, owner, wide // PITCH, slots)


def weigh(prob_slot, grad_slot, grad, query):
    dim = grad.shape[2]
    spread = head_spread(dim)
    prob = mm(from_lanes(prob_slot[...]), spread)
    mix = (prob * grad[...].reshape(-1, dim).astype(F32)).astype(BF)
    score = mm(from_lanes(grad_slot[...]), spread) * 0.125
    return mix, (score * query[...].reshape(-1, dim).astype(F32)).astype(BF)


def rows_out_kernel(prob_slot, grad_slot, grad, query, w_k, w_v, *refs):
    out, flag = refs[-2:]
    mix, ask = weigh(prob_slot, grad_slot, grad, query)
    out[...] = (mm_nt(mix, w_v[...]) + mm_nt(ask, w_k[...])).astype(BF).reshape(grad.shape)
    flag[...] = jnp.zeros_like(flag)


def rows_weights_kernel(*refs):
    prob_slot, grad_slot, grad, query, rows = refs[:5]
    by_key, by_value, key_sum, value_sum = refs[-4:]
    step, part = pl.program_id(0), pl.program_id(1)

    @pl.when((step == 0) & (part == 0))
    def _():
        key_sum[...] = jnp.zeros_like(key_sum)
        value_sum[...] = jnp.zeros_like(value_sum)

    mix, ask = weigh(prob_slot, grad_slot, grad, query)
    left = rows[...].reshape(mix.shape)
    key_sum[...] += mm_tn(left, ask)
    value_sum[...] += mm_tn(left, mix)

    @pl.when((step == pl.num_programs(0) - 1) & (part == pl.num_programs(1) - 1))
    def _():
        by_key[...] = key_sum[...].astype(BF)
        by_value[...] = value_sum[...].astype(BF)


def query_back_kernel(keys, token_t, grad_slot, waited, out, total):
    del waited
    step, part = pl.program_id(0), pl.program_id(1)
    k, dim = keys.shape[1:]

    @pl.when((step == 0) & (part == 0))
    def _():
        total[...] = jnp.zeros_like(total)

    score = mm(from_lanes(grad_slot[...]), head_spread(dim)) * 0.125
    prod = (score * keys[...].reshape(-1, dim).astype(F32)).astype(BF)
    total[...] += mm(token_t[...], prod)

    @pl.when((step == pl.num_programs(0) - 1) & (part == pl.num_programs(1) - 1))
    def _():
        out[...] = total[...].astype(BF)


def vector_sums_kernel(*refs, plain, pairs):
    ops, (wide, out, out_wide) = refs[: plain + 2 * pairs], refs[plain + 2 * pairs :]
    rows = [ops[i][...].astype(F32) for i in range(plain)]
    lefts = [ops[plain + 2 * i][...].astype(F32) for i in range(pairs)]
    rows += [lefts[i] * ops[plain + 2 * i + 1][...] for i in range(pairs)]
    rows += lefts
    sums = [jnp.sum(row, axis=0, keepdims=True) for row in rows]
    sums.append(jnp.zeros((out.shape[0] - len(sums), out.shape[1]), F32))
    out[...] = jnp.concatenate(sums, axis=0)
    out_wide[...] = jnp.sum(wide[...].astype(F32), axis=0, keepdims=True)


def vector_sums(plain, pairs, wide):
    ops = list(plain) + [x for pair in pairs for x in pair] + [wide]
    dim = plain[0].shape[1]
    return pl.pallas_call(
        functools.partial(vector_sums_kernel, plain=len(plain), pairs=len(pairs)),
        out_shape=(
            jax.ShapeDtypeStruct((16, dim), F32),
            jax.ShapeDtypeStruct((1, wide.shape[1]), F32),
        ),
        compiler_params=pltpu.CompilerParams(vmem_limit_bytes=24 * 1024 * 1024),
        cost_estimate=cost(2),
        name="vector_sums",
    )(*ops)


class SlotAttention:
    split = 1

    def __init__(self, ret_rows, shard_rows, peers, slots, dim):
        self.toks, self.ret = ret_rows.shape
        self.peers, self.slots, self.dim = peers, slots, dim
        self.k = slots // self.split
        self.wanted, token, self.at_rank, self.owner = plan_slots(
            ret_rows.T, shard_rows, peers, slots
        )
        k, dim, toks = self.k, self.dim, self.toks
        groups, wide = peers // GROUP, peers * PITCH
        self.grid = (groups, self.split)
        self.rows = pl.BlockSpec((GROUP, k, dim), lambda g, c: (g, c, 0))
        self.lanes = pl.BlockSpec((k, LANES), lambda g, c: (c, g))
        self.mark = pl.BlockSpec((GROUP * k, toks), lambda g, c: (c * groups + g, 0))
        self.mark_t = pl.BlockSpec((toks, GROUP * k), lambda g, c: (0, c * groups + g))
        self.square = self.whole(dim, dim)
        self.w_specs = [pl.BlockSpec((None, dim, dim), lambda g, c, i=i: (i, 0, 0)) for i in range(2)]
        self.heads = self.whole(slots, wide)
        self.slot_rows = in_hbm((peers, slots, dim), BF)
        self.slot_heads = jax.ShapeDtypeStruct((slots, wide), F32)
        token = token.reshape(peers, self.split, k).transpose(1, 0, 2)
        self.token, self.token_t = self.call(
            token_marks_kernel,
            "token_marks",
            5,
            [
                pl.BlockSpec((GROUP * k, 1), lambda g, c: (c * groups + g, 0)),
                pl.BlockSpec((1, GROUP * k), lambda g, c: (0, c * groups + g)),
            ],
            [self.mark, self.mark_t],
            (in_hbm((peers * slots, toks), BF), in_hbm((toks, peers * slots), BF)),
        )(token.reshape(-1, 1), token.reshape(1, -1))

    @staticmethod
    def whole(*shape):
        return pl.BlockSpec(shape, lambda g, c: (0,) * len(shape))

    def call(self, kernel, name, micros, in_specs, out_specs, out_shape, scratch=(), mib=44):
        return pl.pallas_call(
            kernel,
            grid=self.grid,
            in_specs=in_specs,
            out_specs=out_specs,
            out_shape=out_shape,
            scratch_shapes=list(scratch),
            compiler_params=pltpu.CompilerParams(vmem_limit_bytes=mib * 1024 * 1024),
            cost_estimate=cost(micros),
            name=name,
        )

    def prepare(self, cross_q):
        self.query = self.call(
            query_rows_kernel,
            "query_rows",
            7,
            [self.mark, self.whole(self.toks, self.dim)],
            self.rows,
            self.slot_rows,
        )(self.token, cross_q)

    def forward(self, arrived, mats, bias):
        dim, toks = self.dim, self.toks
        self.arrived, self.mats = arrived, mats
        self.keys, self.vals, scores = self.call(
            rows_in_kernel,
            "rows_in",
            22,
            [self.rows, self.rows, *self.w_specs],
            [self.rows, self.rows, self.lanes],
            (self.slot_rows, self.slot_rows, self.slot_heads),
        )(from_hbm(arrived), from_hbm(self.query), mats, mats)
        entries = (self.ret * PITCH, toks)
        self.prob_tok, self.prob_slot, mixed = self.call(
            attend_kernel,
            "attend",
            11,
            [self.heads, self.rows, self.mark_t]
            + [self.whole(*self.at_rank.shape), self.whole(*self.owner.shape), self.whole(1, dim)],
            [self.whole(*entries), self.heads, self.whole(toks, dim)],
            (
                jax.ShapeDtypeStruct(entries, F32),
                self.slot_heads,
                jax.ShapeDtypeStruct((toks, dim), BF),
            ),
            [pltpu.VMEM((toks, dim), F32)],
        )(scores, from_hbm(self.vals), self.token_t, self.at_rank, self.owner, bias.reshape(1, dim))
        return mixed

    def backward(self, grad):
        dim, toks = self.dim, self.toks
        grads, self.grad_slot = self.call(
            attend_back_kernel,
            "attend_back",
            13,
            [self.rows, self.mark, self.whole(toks, dim), self.whole(self.ret * PITCH, toks)]
            + [self.whole(*self.at_rank.shape), self.whole(*self.owner.shape)],
            [self.rows, self.heads],
            (self.slot_rows, self.slot_heads),
            [pltpu.VMEM(self.slot_heads.shape, F32)],
        )(from_hbm(self.vals), self.token, grad, self.prob_tok, self.at_rank, self.owner)
        self.factors = (self.prob_slot, self.grad_slot, from_hbm(grads), from_hbm(self.query))
        self.factor_specs = [self.lanes, self.lanes, self.rows, self.rows]
        return [self.send(0), self.send(1)]

    def send(self, part):
        k = self.slots // 2
        some = pl.BlockSpec((GROUP, k, self.dim), lambda g, c: (g, part, 0))
        lanes = pl.BlockSpec((k, LANES), lambda g, c: (part, g))
        before = [self.flag] if part else []
        sent, self.flag = self.call(
            rows_out_kernel,
            "rows_out",
            14,
            [lanes, lanes, some, some] + self.w_specs + [self.whole(8, LANES)] * part,
            [pl.BlockSpec((GROUP, k, self.dim), lambda g, c: (g, 0, 0)), self.whole(8, LANES)],
            (
                in_hbm((self.peers, k, self.dim), BF),
                jax.ShapeDtypeStruct((8, LANES), F32),
            ),
        )(*self.factors, self.mats, self.mats, *before)
        return sent

    def query_grad(self):
        dim, toks = self.dim, self.toks
        return self.call(
            query_back_kernel,
            "query_back",
            7,
            [self.rows, self.mark_t, self.lanes, self.whole(8, LANES)],
            self.whole(toks, dim),
            jax.ShapeDtypeStruct((toks, dim), BF),
            [pltpu.VMEM((toks, dim), F32)],
        )(from_hbm(self.keys), self.token_t, self.grad_slot, self.flag)

    def weights(self, after):
        square = (self.dim, self.dim)
        return self.call(
            rows_weights_kernel,
            "rows_weights",
            24,
            self.factor_specs + [self.rows] + [WAIT] * len(after),
            [self.square, self.square],
            (jax.ShapeDtypeStruct(square, BF), jax.ShapeDtypeStruct(square, BF)),
            [pltpu.VMEM(square, F32), pltpu.VMEM(square, F32)],
        )(*self.factors, from_hbm(self.arrived), *after)


class GatheredAttention:
    def __init__(self, ret_rows, shard_rows, peers, slots, dim):
        self.toks, self.ret = ret_rows.shape
        self.dim, self.slots = dim, slots
        self.place, self.wanted, self.entry = plan_requests(ret_rows, shard_rows, peers, slots)
        self.fwd, self.bwd, self.back_q = cross_calls(self.toks, self.ret, dim)

    def prepare(self, cross_q):
        self.cross_q = cross_q

    def forward(self, arrived, mats, bias):
        toks, dim = self.toks, self.dim
        w_k, w_v = mats[0], mats[1]
        self.key_heads, self.val_heads = w_k.reshape(dim, H, HD), w_v.reshape(dim, H, HD)
        query = self.cross_q.reshape(toks, H, HD)
        self.query_keys = jnp.einsum(
            "the,dhe->htd", query, self.key_heads, preferred_element_type=F32
        ).astype(BF)
        self.fetched = arrived.reshape(-1, dim)[self.place]
        self.state_mix, self.cross_p = self.fwd(self.query_keys, self.fetched)
        mixed = jnp.einsum(
            "htd,dhe->the", self.state_mix, self.val_heads, preferred_element_type=F32
        )
        return (mixed.reshape(toks, dim) + bias).astype(BF)

    def backward(self, grad):
        self.grad = grad.reshape(self.toks, H, HD)
        grad_mix = jnp.einsum(
            "the,dhe->htd", self.grad, self.val_heads, preferred_element_type=F32
        ).astype(BF)
        rows, self.grad_s = self.bwd(self.query_keys, grad_mix, self.fetched, self.cross_p)
        return [rows[self.entry]]

    def query_grad(self):
        self.grad_qk = self.back_q(self.grad_s, self.fetched)
        grad_q = jnp.einsum(
            "htd,dhe->the", self.grad_qk, self.key_heads, preferred_element_type=F32
        )
        return grad_q.reshape(self.toks, self.dim).astype(BF)

    def weights(self, after):
        def product(left, right):
            got = jnp.einsum("htd,the->dhe", left, right, preferred_element_type=F32)
            return got.reshape(self.dim, self.dim).astype(BF)

        grad_k = product(self.grad_qk, self.cross_q.reshape(self.toks, H, HD))
        return grad_k, product(self.state_mix, self.grad)


def store_sum_kernel(asked, returned, *refs, block, skip, added):
    first = (pl.program_id(0) + skip) * block + 1
    shape = (block, asked.shape[1])
    hit = lax.broadcasted_iota(jnp.int32, shape, 0) + first == asked[...]
    total = mm(hit.astype(BF), returned[...])
    refs[-1][...] = total + refs[0][...] if added else total


def store_sum(asked, returned, shard_rows, so_far=(), rows=(0, 1), after=()):
    count, dim = returned.shape
    block = 256
    part, parts = rows
    steps = shard_rows // block // parts
    skip = part * steps
    here = pl.BlockSpec((block, dim), lambda g: (g + skip, 0))
    return pl.pallas_call(
        functools.partial(store_sum_kernel, block=block, skip=skip, added=bool(so_far)),
        grid=(steps,),
        in_specs=[
            pl.BlockSpec((1, count), lambda g: (0, 0)),
            pl.BlockSpec((count, dim), lambda g: (0, 0)),
        ]
        + [here] * len(so_far)
        + [WAIT] * len(after),
        out_specs=here,
        out_shape=in_hbm((shard_rows, dim), F32),
        input_output_aliases={2: 0} if so_far else {},
        compiler_params=pltpu.CompilerParams(vmem_limit_bytes=VMEM_LIMIT),
        cost_estimate=cost(13 if parts == 1 else 8),
        name="store_sum",
    )(asked.reshape(1, count), returned, *so_far, *after)


def all_to_all(array):
    return lax.all_to_all(array, RANKS, split_axis=0, concat_axis=0, tiled=True)


def on_device(
    tokens,
    seg_ids,
    live_mask,
    ret_rows,
    enc_store,
    attn_in,
    attn_out,
    ff_in,
    ff_out,
    biases,
    ln_gain,
    ln_shift,
    ff_bias,
    cotangent,
):
    n_rows = lax.axis_size("row")
    n_cols = lax.axis_size("col")
    peers = n_rows * n_cols
    tok_count, dim = tokens.shape
    shard_rows = enc_store.shape[0]
    ret = ret_rows.shape[1]
    slots = 3 * ret_rows.size // (2 * peers)
    rb, cb = attn_in.shape[1], attn_in.shape[2]
    order_a, order_b = bit_orders(n_rows, n_cols)
    n_row_bits = n_rows.bit_length() - 1
    n_far = n_row_bits - 2
    by_rows = n_cols == 2 and rb % 16 == 0 and cb % 128 == 0
    orders = (order_a, order_b, order_a, order_b)
    shapes = ((rb, cb), (rb, cb), (rb, 4 * cb), (4 * rb, cb))
    counts = (4, 4, 1, 1)
    if by_rows:
        col = lax.axis_index("col").astype(jnp.int32)[None]
        place_a = jnp.concatenate([block_of_row(order_a, n_rows), col])
        place_b = jnp.concatenate([block_of_row(order_b, n_rows), col])
        places = (place_a, place_b, place_a, place_b)

    in_slots = (
        by_rows
        and slots % (16 * SlotAttention.split) == 0
        and peers % GROUP == 0
        and tok_count % LANES == 0
        and tok_count <= 256
        and shard_rows & (shard_rows - 1) == 0
        and H <= PITCH
    )
    attention = (SlotAttention if in_slots else GatheredAttention)(
        ret_rows, shard_rows, peers, slots, dim
    )

    def vector_rows(parts):
        parts = [jnp.pad(part, ((0, 0), (0, cb - part.shape[1]))) for part in parts]
        return jnp.pad(jnp.concatenate(parts, axis=0), ((0, 2), (0, 0)))

    small = vector_rows([biases, ln_gain, ln_shift, ff_bias.reshape(1, -1)])
    packs = [*join(attn_in, attn_out, small, attention.wanted), ff_in[None], ff_out[None]]
    packs = [gather_bits(p, order[:1]) for p, order in zip(packs, orders)]
    asked = all_to_all(attention.wanted)
    asked = tie(asked, packs[:2]) if by_rows else asked
    packs = [gather_bits(p, order[1:n_far]) for p, order in zip(packs, orders)]

    answer = enc_store[jnp.maximum(asked - 1, 0)]
    for i in range(2):
        packs[i] = gather_bits(packs[i], orders[i][n_far : n_far + 1])
    arrived = all_to_all(hold(answer, packs) if by_rows else answer)
    if in_slots:
        packs[0] = hold(packs[0], [attention.token, attention.token_t])
    extras = (0, small.shape[0], 0, 0)

    def whole(i, after=()):
        done = n_far + 1
        if by_rows:
            got = swap_bit(packs[i], *orders[i][done])
            own = hold(packs[i], after) if after else packs[i]
            own = jnp.concatenate([own, got], axis=0)
            other = swap_bit(own, "col", 1)
            return unpack(own, other, places[i], counts[i], shapes[i], extras[i])
        blocks = gather_bits(packs[i], orders[i][done:])
        return unpack_any(blocks, orders[i], counts[i], shapes[i], extras[i], n_rows, n_cols)

    mats = [whole(0), whole(1)]
    w_q, w_k, w_v = (mats[0][i] for i in range(3))
    w_co = mats[1][0][3]
    small_all = mats[1][1]
    small_all = small_all.astype(F32)
    vectors = small_all[:, :13, :rb].transpose(1, 0, 2).reshape(13, dim)
    bias_all, gain_all, shift_all = vectors[:7], vectors[7:10], vectors[10:]
    bias_ff = small_all[:, 13, : ff_bias.size].reshape(-1)

    *qkv, mixed, first, first_norm, first_scale, cross_q = self_fwd(
        tokens, seg_ids, live_mask, mats[0], mats[1][0], bias_all, gain_all, shift_all
    )
    first_low = first.astype(BF)

    attention.prepare(cross_q)
    if in_slots:
        for i in (2, 3):
            packs[i] = gather_bits(packs[i], orders[i][n_far : n_far + 1])
    else:
        for i in (2, 3):
            packs[i] = gather_bits(packs[i], orders[i][n_far : n_far + 1])
    cross_low = attention.forward(arrived, mats[1][0], bias_all[4])
    branch_two = mm(cross_low, w_co) + bias_all[5]
    second, second_norm, second_scale = norm_fwd(first + branch_two, gain_all[1], shift_all[1])
    second_low = second.astype(BF)

    after = [attention.query] if in_slots else []
    w_ff1, w_ff2 = whole(2, after)[0], whole(3, after)[0]
    hidden_act, hidden_slope = gelu_parts(mm(second_low, w_ff1) + bias_ff)
    hidden_low = hidden_act.astype(BF)
    branch_ffn = mm(hidden_low, w_ff2) + bias_all[6]
    final, final_norm, final_scale = norm_fwd(second + branch_ffn, gain_all[2], shift_all[2])
    output = final.astype(BF)
    cot = cotangent.astype(F32)
    grad_three = norm_back(cot, final_norm, final_scale, gain_all[2])
    grad_y = grad_three.astype(BF)
    grad_pre = (mm_nt(grad_y, w_ff2) * hidden_slope).astype(BF)
    grad_second = grad_three + mm_nt(grad_pre, w_ff1)
    grad_two = norm_back(grad_second, second_norm, second_scale, gain_all[1])
    grad_o2 = grad_two.astype(BF)
    grad_cmix = mm_nt(grad_o2, w_co).astype(BF)
    send_back = attention.backward(grad_cmix)
    returned = [all_to_all(send_back[0])]

    def packed(order, place, mats, small=None, after=()):
        if by_rows:
            return pack(mats, place, small, after)
        return pack_any(mats, order[::-1], small, n_rows, n_cols)

    def on_both(pairs, start, stop):
        return [
            scatter_bits(*pair, back[start:stop]) for pair, back in zip(pairs, (back_a, back_b))
        ]

    tile = (rb, cb)
    near = len(order_a) - n_far
    back_a, back_b = order_a[::-1], order_b[::-1]
    at_a, at_b = (place_a, place_b) if by_rows else (None, None)
    grad_cq = attention.query_grad()
    ff = [
        (order_a, at_a, [((second_low, grad_pre), tile, 4)]),
        (order_b, at_b, [((hidden_low, grad_y), (4 * rb, cb), 1)]),
    ]
    ff = [packed(*part, None, [grad_cq]) for part in ff]
    if by_rows:
        grad_cq = hold(grad_cq, [x for pair in ff for x in pair])
    grad_first, grad_one, grad_o, grad_q, grad_k, grad_v = self_bwd(
        grad_cq,
        grad_two,
        first_norm,
        first_scale,
        gain_all,
        qkv,
        seg_ids,
        live_mask,
        mats[0],
        mats[1][0],
    )
    grad_tokens = (
        grad_one + mm_nt(grad_q, w_q) + mm_nt(grad_k, w_k) + mm_nt(grad_v, w_v)
    )

    vectors, wide = vector_sums(
        [grad_q, grad_v, grad_o, grad_cq, grad_cmix, grad_o2, grad_y],
        [(grad_first, first_norm), (grad_second, second_norm), (cotangent, final_norm)],
        grad_pre,
    )
    vectors = vectors[:13].reshape(13, n_rows, rb).transpose(1, 0, 2)
    wide = wide.reshape(n_rows, 1, -1)
    grad_small = [
        jnp.pad(vectors, ((0, 0), (0, 0), (0, cb - rb))),
        jnp.pad(wide, ((0, 0), (0, 2), (0, cb - ff_bias.size))),
    ]
    grad_small = jnp.concatenate(grad_small, axis=1).astype(BF)
    attn_one = packed(
        order_a,
        at_a,
        [
            ((tokens, grad_q), tile, 1),
            ((tokens, grad_k), tile, 1),
            ((tokens, grad_v), tile, 1),
            ((first_low, grad_cq), tile, 1),
        ],
    )
    ff = on_both(ff, 0, near - 2)
    before = [*attn_one, ff[0][1], ff[1][1]] if in_slots else []
    grad_wk, grad_wv = attention.weights(before)
    attn_two = packed(
        order_b,
        at_b,
        [
            (grad_wk, tile, 1),
            (grad_wv, tile, 1),
            ((mixed, grad_o), tile, 1),
            ((cross_low, grad_o2), tile, 1),
        ],
        grad_small,
    )
    ff = on_both(ff, near - 2, near - 1)
    if len(send_back) > 1:
        attn_one = scatter_bits(*attn_one, back_a[: near - 2])
    for part in send_back[1:]:
        before = [*returned, *attn_two, *attn_one, *ff[0], *ff[1]]
        returned.append(all_to_all(hold(part, before)))

    def join_pairs(pairs):
        return tuple(jnp.concatenate(both, axis=1) for both in zip(*pairs))

    if len(send_back) > 1:
        attn_two = scatter_bits(*attn_two, back_b[: near - 2])
        attn = join_pairs(on_both([attn_one, attn_two], near - 2, near))
    else:
        attn = join_pairs(on_both([attn_one, attn_two], 0, near))
    def behind(pair, array):
        return (hold(pair[0], [array]), pair[1]) if by_rows else pair

    size = asked.shape[1] // len(returned)
    lists = [
        (asked[:, i * size : (i + 1) * size], rows.reshape(-1, dim), shard_rows)
        for i, rows in enumerate(returned)
    ]
    so_far = ()
    for args in lists[:-1]:
        so_far = (store_sum(*args),)
        ff = [behind(pair, so_far[0]) for pair in ff]
    ff = join_pairs(on_both(ff, near - 1, near))
    grad_store = store_sum(*lists[-1], so_far, (0, 2)) if so_far else None
    if so_far:
        ff, attn = behind(ff, grad_store), behind(attn, grad_store)
    ff, attn = (scatter_bits(*x, back_a[near:-1]) for x in (ff, attn))
    last = join_pairs([attn, ff])
    if so_far:
        grad_store = store_sum(*lists[-1], (grad_store,), (1, 2), (last[1],))
        keep, send = behind(last, grad_store)
    else:
        grad_store = store_sum(*lists[-1])
        keep, send = last
    total = (keep + swap_bit(send, *order_a[0]))[0].astype(F32)
    total_a, total_b = total[: attn[0].shape[1]], total[attn[0].shape[1] :]

    sum_small = total_a[8 * rb :]
    return (
        output,
        grad_tokens,
        grad_store,
        total_a[: 6 * rb].reshape(6, rb, cb),
        total_a[6 * rb : 8 * rb].reshape(2, rb, cb),
        jnp.concatenate([total_b[k * rb : (k + 1) * rb] for k in range(4)], axis=1),
        total_b[4 * rb :],
        sum_small[:7, :rb],
        sum_small[7:10, :rb],
        sum_small[10:13, :rb],
        sum_small[13, : ff_bias.size],
    )


def solution(mesh):
    both = ("row", "col")
    return jax.shard_map(
        on_device,
        mesh=mesh,
        in_specs=(
            P(both, None),
            P(both, None),
            P(both, None),
            P(both, None),
            P(both, None),
            P(None, "row", "col"),
            P(None, "row", "col"),
            P("row", "col"),
            P("row", "col"),
            P(None, "row"),
            P(None, "row"),
            P(None, "row"),
            P("row"),
            P(both, None),
        ),
        out_specs=(
            P(both, None),
            P(both, None),
            P(both, None),
            P(None, "row", "col"),
            P(None, "row", "col"),
            P("row", "col"),
            P("row", "col"),
            P(None, "row"),
            P(None, "row"),
            P(None, "row"),
            P("row"),
        ),
        check_vma=False,
    )
```

```python
import functools

import jax
import jax.numpy as jnp
import numpy as np
from jax import lax
from jax.experimental import pallas as pl
from jax.experimental.pallas import tpu as pltpu
from jax.sharding import PartitionSpec as P

H = 12
HD = 64
RANKS = ("row", "col")
BF = jnp.bfloat16
F32 = jnp.float32
VMEM_LIMIT = 60 * 1024 * 1024


def mm(a, b):
    return jnp.dot(a, b, preferred_element_type=F32)


def mm_nt(a, b):
    return lax.dot_general(a, b, (((1,), (1,)), ((), ())), preferred_element_type=F32)


def mm_tn(a, b):
    return lax.dot_general(a, b, (((0,), (0,)), ((), ())), preferred_element_type=F32)


def norm_fwd(resid, gain, shift):
    row_mean = jnp.mean(resid, axis=-1, keepdims=True)
    centered = resid - row_mean
    inv_std = lax.rsqrt(jnp.mean(centered * centered, axis=-1, keepdims=True) + 1e-05)
    normed = centered * inv_std
    return (normed * gain + shift, normed, inv_std)


def norm_back(grad_in, normed, inv_std, gain):
    scaled = grad_in * gain
    return inv_std * (
        scaled
        - jnp.mean(scaled, axis=-1, keepdims=True)
        - normed * jnp.mean(scaled * normed, axis=-1, keepdims=True)
    )


def gelu_parts(pre_act):
    cdf_part = 0.5 * (1.0 + lax.erf(pre_act * 0.7071067811865476))
    density = jnp.exp(-0.5 * pre_act * pre_act) * 0.3989422804014327
    return (pre_act * cdf_part, cdf_part + pre_act * density)


def column_sum(array):
    return jnp.sum(array.astype(F32), axis=0)


def bit_orders(n_rows, n_cols):
    row_bits = [("row", 1 << b) for b in reversed(range(n_rows.bit_length() - 1))]
    col_bits = [("col", 1 << b) for b in reversed(range(n_cols.bit_length() - 1))]
    swapped = row_bits[:-2] + row_bits[-1:] + row_bits[-2:-1]
    return row_bits + col_bits, swapped + col_bits


def swap_bit(array, axis, bit):
    pairs = [(i, i ^ bit) for i in range(lax.axis_size(axis))]
    return lax.ppermute(array, axis, pairs)


def gather_bits(blocks, order):
    for axis, bit in order:
        blocks = jnp.concatenate([blocks, swap_bit(blocks, axis, bit)], axis=0)
    return blocks


def scatter_bits(keep, send, order):
    for axis, bit in order:
        got = swap_bit(send, axis, bit)
        half = keep.shape[0] // 2
        keep, send = keep[:half] + got[:half], keep[half:] + got[half:]
    return keep, send


def block_of_row(order, n_rows):
    apart = np.zeros(n_rows, np.int32)
    for k, (_, bit) in enumerate(order[: n_rows.bit_length() - 1]):
        apart[(np.arange(n_rows) >> k) & 1 == 1] ^= bit
    table = np.zeros(n_rows, np.int32)
    table[apart] = np.arange(n_rows)
    return jnp.asarray(table)[lax.axis_index("row") ^ jnp.arange(n_rows, dtype=jnp.int32)]


def flip_by_position(blocks, stages):
    for k, (axis, bit) in enumerate(stages):
        here = (lax.axis_index(axis) & bit) != 0
        blocks = jnp.where(here, jnp.flip(blocks, axis=k), blocks)
    return blocks


def by_device(blocks, order):
    stages = order[::-1]
    shape = blocks.shape[1:]
    blocks = flip_by_position(blocks.reshape((2,) * len(stages) + shape), stages)
    rank = sorted(range(len(stages)), key=lambda k: (stages[k][0] == "col", -stages[k][1]))
    rest = list(range(len(stages), blocks.ndim))
    return blocks.transpose(rank + rest).reshape((-1,) + shape)


def by_stage(blocks, stages):
    shape = blocks.shape[1:]
    rank = sorted(range(len(stages)), key=lambda k: (stages[k][0] == "col", -stages[k][1]))
    rest = list(range(len(stages), len(stages) + len(shape)))
    back = [rank.index(k) for k in range(len(stages))]
    blocks = blocks.reshape((2,) * len(stages) + shape).transpose(back + rest)
    return flip_by_position(blocks, stages).reshape((-1,) + shape)


def cost(micros):
    return pl.CostEstimate(flops=int(micros * 1.1e9), bytes_accessed=0, transcendentals=0)


WAIT = pl.BlockSpec(memory_space=pltpu.HBM)


def in_hbm(shape, dtype):
    return pltpu.HBM(shape=shape, dtype=dtype)


def from_hbm(array):
    return pltpu.with_memory_space_constraint(array, pltpu.HBM)


def tie_kernel(*refs):
    refs[-1][...] = refs[0][...]


def tie(array, after):
    return pl.pallas_call(
        tie_kernel,
        in_specs=[pl.BlockSpec(memory_space=pltpu.VMEM)] + [WAIT] * len(after),
        out_shape=jax.ShapeDtypeStruct(array.shape, array.dtype),
        name="tie",
    )(array, *after)


def hold_kernel(*refs):
    del refs


def hold(array, after):
    return pl.pallas_call(
        hold_kernel,
        in_specs=[WAIT] * (1 + len(after)),
        out_specs=WAIT,
        out_shape=jax.ShapeDtypeStruct(array.shape, array.dtype),
        input_output_aliases={0: 0},
        name="hold",
    )(array, *after)


def tile_of(buf, k, r, c, shape):
    rows, cols = shape
    return buf.at[
        k, pl.ds(pl.multiple_of(r * rows, rows), rows), pl.ds(pl.multiple_of(c * cols, cols), cols)
    ]


def unpack_kernel(place, own, other, *refs, count, shape, extra):
    outs, (buf, *more) = refs[: 1 + bool(extra)], refs[1 + bool(extra) :]
    sems = more[-1]
    n_rows, col, rows = own.shape[0], place[own.shape[0]], shape[0]

    def fill(r, carry):
        j = place[r]
        for src, c, sem in ((own, col, 0), (other, 1 - col, 1)):
            for k in range(count):
                part = src.at[j, pl.ds(k * rows, rows)]
                pltpu.make_async_copy(part, tile_of(buf, k, r, c, shape), sems.at[sem]).start()
        if extra:
            tail = own.at[j, pl.ds(count * rows, extra)]
            pltpu.make_async_copy(tail, more[0].at[r], sems.at[2]).start()
        return carry

    lax.fori_loop(0, n_rows, fill, 0)
    body = own.at[:, pl.ds(0, count * rows)]
    for sem in range(2):
        pltpu.make_async_copy(body, body, sems.at[sem]).wait()
    out = pltpu.make_async_copy(buf, outs[0], sems.at[3])
    out.start()
    if extra:
        pltpu.make_async_copy(more[0], more[0], sems.at[2]).wait()
        tails = pltpu.make_async_copy(more[0], outs[1], sems.at[4])
        tails.start()
        tails.wait()
    out.wait()


def unpack(own, other, place, count, shape, extra=0):
    n_rows = own.shape[0]
    rows, cols = shape
    whole = jax.ShapeDtypeStruct((count, n_rows * rows, 2 * cols), BF)
    tails = jax.ShapeDtypeStruct((n_rows, extra, cols), BF)
    shapes = [whole] + [tails] * bool(extra)
    got = pl.pallas_call(
        functools.partial(unpack_kernel, count=count, shape=shape, extra=extra),
        in_specs=[pl.BlockSpec(memory_space=pltpu.SMEM)] + [pl.BlockSpec(memory_space=pl.ANY)] * 2,
        out_specs=[pl.BlockSpec(memory_space=pl.ANY)] * len(shapes),
        out_shape=shapes,
        scratch_shapes=[pltpu.VMEM(x.shape, BF) for x in shapes] + [pltpu.SemaphoreType.DMA((5,))],
        compiler_params=pltpu.CompilerParams(vmem_limit_bytes=32 * 1024 * 1024),
        cost_estimate=pl.CostEstimate(
            flops=0, bytes_accessed=4 * whole.size * 2, transcendentals=0
        ),
        name="unpack",
    )(place, own, other)
    return got if extra else got[0]


def join_kernel(attn_in, attn_out, small, waited, one, two, *, rb):
    del waited
    for k in range(4):
        one[0, k * rb : (k + 1) * rb] = attn_in[k]
    for k in range(2):
        two[0, k * rb : (k + 1) * rb] = attn_in[4 + k]
        two[0, (2 + k) * rb : (3 + k) * rb] = attn_out[k]
    two[0, 4 * rb :] = small[...]


def join(attn_in, attn_out, small, after):
    rb, cb = attn_in.shape[1:]
    if rb % 16 or cb % 128:
        two = [attn_in[4:].reshape(-1, cb), attn_out.reshape(-1, cb), small]
        return attn_in[:4].reshape(1, -1, cb), jnp.concatenate(two, axis=0)[None]
    return pl.pallas_call(
        functools.partial(join_kernel, rb=rb),
        in_specs=[pl.BlockSpec(memory_space=pltpu.VMEM)] * 3 + [WAIT],
        out_shape=(
            jax.ShapeDtypeStruct((1, 4 * rb, cb), BF),
            jax.ShapeDtypeStruct((1, 4 * rb + small.shape[0], cb), BF),
        ),
        name="join",
    )(attn_in, attn_out, small, after)


def pack_kernel(place, *refs, mats, rows, extra, waits):
    n_ops = 1 + max(max(mat[0]) for mat in mats)
    ops, refs = refs[:n_ops], refs[n_ops:]
    small, refs = refs[: bool(extra)], refs[bool(extra) + waits :]
    keep, send, *bufs, sems = refs
    n_rows, col = keep.shape[0], place[keep.shape[0]]
    loads = {}
    for k, (at, _, _) in enumerate(mats):
        if len(at) == 1:
            loads[k] = pltpu.make_async_copy(ops[at[0]], bufs[k].at[0], sems.at[2 + k])
            loads[k].start()
    for k, (at, _, _) in enumerate(mats):
        if len(at) == 2:
            left, right = ops[at[0]], ops[at[1]]
            _, tall, wide = bufs[k].shape
            tile = min(tall, wide)
            for i in range(0, tall, tile):
                for j in range(0, wide, tile):
                    got = mm_tn(left[:, i : i + tile], right[:, j : j + tile])
                    bufs[k][0, i : i + tile, j : j + tile] = got.astype(BF)
    for load in loads.values():
        load.wait()

    def spread(r, carry):
        j = place[r]
        for dst, c, sem in ((keep, col, 0), (send, 1 - col, 1)):
            first = 0
            for buf, (_, shape, beside) in zip(bufs, mats):
                for k in range(beside):
                    part = dst.at[j, pl.ds(first, shape[0])]
                    tile = tile_of(buf, 0, r, c * beside + k, shape)
                    pltpu.make_async_copy(tile, part, sems.at[sem]).start()
                    first += shape[0]
            if extra:
                tail = dst.at[j, pl.ds(first, extra)]
                pltpu.make_async_copy(small[0].at[r], tail, sems.at[sem]).start()
        return carry

    lax.fori_loop(0, n_rows, spread, 0)
    for dst, sem in ((keep, 0), (send, 1)):
        pltpu.make_async_copy(dst, dst, sems.at[sem]).wait()


def pack(mats, place, small=None, after=()):
    ops, parts, specs, bufs, flops, total = [], [], [], [], 0, 0
    for mat, shape, beside in mats:
        mat = mat if isinstance(mat, tuple) else (mat,)
        parts.append((tuple(range(len(ops), len(ops) + len(mat))), shape, beside))
        ops += mat
        specs += [pl.BlockSpec(memory_space=pltpu.VMEM if len(mat) == 2 else pl.ANY)] * len(mat)
        whole = (mat[0].shape[1], mat[1].shape[1]) if len(mat) == 2 else mat[0].shape
        bufs.append(pltpu.VMEM((1,) + tuple(whole), BF))
        flops += 2 * mat[0].shape[0] * whole[0] * whole[1] if len(mat) == 2 else 0
        total += beside * shape[0]
        n_rows = whole[0] // shape[0]
    extra = 0 if small is None else small.shape[1]
    block = in_hbm((n_rows, total + extra, shape[1]), BF)
    if extra:
        ops.append(small)
        specs.append(pl.BlockSpec(memory_space=pltpu.VMEM))
    return pl.pallas_call(
        functools.partial(
            pack_kernel, mats=tuple(parts), rows=total, extra=extra, waits=len(after)
        ),
        in_specs=[pl.BlockSpec(memory_space=pltpu.SMEM)] + specs + [WAIT] * len(after),
        out_specs=[pl.BlockSpec(memory_space=pl.ANY)] * 2,
        out_shape=[block, block],
        scratch_shapes=bufs + [pltpu.SemaphoreType.DMA((2 + len(mats),))],
        compiler_params=pltpu.CompilerParams(vmem_limit_bytes=48 * 1024 * 1024),
        cost_estimate=pl.CostEstimate(
            flops=flops, bytes_accessed=8 * n_rows * total * shape[1], transcendentals=0
        ),
        name="pack",
    )(place, *ops, *after)


def unpack_any(blocks, order, count, shape, extra, n_rows, n_cols):
    rows, cols = shape
    got = by_device(blocks, order).reshape(n_rows, n_cols, -1, cols)
    mats = got[:, :, : count * rows].reshape(n_rows, n_cols, count, rows, cols)
    mats = mats.transpose(2, 0, 3, 1, 4).reshape(count, n_rows * rows, n_cols * cols)
    return (mats, got[:, 0, count * rows :]) if extra else mats


def pack_any(mats, order, small, n_rows, n_cols):
    got = []
    for mat, (rows, cols), beside in mats:
        mat = mm_tn(*mat).astype(BF) if isinstance(mat, tuple) else mat
        mat = mat.reshape(n_rows, rows, n_cols, beside, cols).transpose(0, 2, 3, 1, 4)
        got.append(mat.reshape(n_rows, n_cols, beside * rows, cols))
    if small is not None:
        got.append(jnp.broadcast_to(small[:, None], (n_rows, n_cols) + small.shape[1:]))
    got = jnp.concatenate(got, axis=2)
    got = by_stage(got.reshape((-1,) + got.shape[2:]), order)
    half = got.shape[0] // 2
    return got[:half], got[half:]


def plan_requests(ret_rows, shard_rows, peers, slots):
    flat = ret_rows.reshape(-1)
    count = flat.shape[0]
    owner = flat // shard_rows
    local_row = flat - owner * shard_rows
    mine = owner[:, None] == jnp.arange(peers, dtype=jnp.int32)[None, :]
    run = 256
    runs = count // run
    ones = mine.astype(BF).reshape(runs, run, peers)
    lower = jnp.tril(jnp.ones((run, run), BF))
    within = jnp.einsum("ij,bjo->bio", lower, ones, preferred_element_type=F32)
    totals = within[:, -1, :]
    before = jnp.cumsum(totals, axis=0) - totals
    upto = (within + before[:, None, :]).reshape(count, peers)
    rank = jnp.sum(jnp.where(mine, upto, 0.0), axis=1).astype(jnp.int32) - 1
    place = owner * slots + rank
    row_code = local_row + 1
    entry_code = jnp.arange(count, dtype=jnp.int32)
    digits = jnp.stack([row_code // 64, row_code % 64, entry_code // 64, entry_code % 64])
    left = jnp.where(mine.T[None], digits[:, None, :], 0).astype(BF)
    at_rank = (rank[:, None] == jnp.arange(slots, dtype=jnp.int32)[None, :]).astype(BF)
    codes = mm(left.reshape(4 * peers, count), at_rank).astype(jnp.int32).reshape(4, peers, slots)
    return place, codes[0] * 64 + codes[1], codes[2] * 64 + codes[3]


def row_norm(resid):
    centered = resid - jnp.mean(resid, axis=-1, keepdims=True)
    scale = lax.rsqrt(jnp.mean(centered * centered, axis=-1, keepdims=True) + 1e-05)
    return centered * scale, scale


def head_masks():
    lane = lax.broadcasted_iota(jnp.int32, (1, 2 * HD), 1)
    return [(lane // HD == i).astype(F32).astype(BF) for i in range(2)]


def self_probs(query, key, visible):
    scores = jnp.where(visible, mm_nt(query, key) * (HD**-0.5), -1e30)
    expo = jnp.exp(scores - jnp.max(scores, axis=-1, keepdims=True))
    return expo / jnp.sum(expo, axis=-1, keepdims=True)


def visible_pairs(seg_col, seg_row, live_row):
    shape = (seg_col.shape[0], seg_row.shape[1])
    at_query = lax.broadcasted_iota(jnp.int32, shape, 0)
    at_key = lax.broadcasted_iota(jnp.int32, shape, 1)
    return (
        (at_key <= at_query)
        & (seg_col[...] == seg_row[...])
        & ((live_row[...] == 1) | (at_key == at_query))
    )


def self_fwd_kernel(*refs):
    tokens, seg_col, seg_row, live_row, w_qkvc, w_o, bias, gain, shift = refs[:9]
    queries, keys, values, mixed, first, normed, scale, cross_q = refs[9:]
    x = tokens[...]
    queries[...] = (mm(x, w_qkvc[0]) + bias[0:1]).astype(BF)
    keys[...] = mm(x, w_qkvc[1]).astype(BF)
    values[...] = (mm(x, w_qkvc[2]) + bias[1:2]).astype(BF)
    visible = visible_pairs(seg_col, seg_row, live_row)
    for pair in range(H // 2):
        lanes = slice(2 * HD * pair, 2 * HD * (pair + 1))
        total = 0.0
        for mask in head_masks():
            prob = self_probs(queries[:, lanes], keys[:, lanes] * mask, visible)
            total = total + mm(prob.astype(BF), values[:, lanes] * mask)
        mixed[:, lanes] = total.astype(BF)
    resid = x.astype(F32) + mm(mixed[...], w_o[...]) + bias[2:3]
    norm, inv = row_norm(resid)
    normed[...] = norm
    scale[...] = jnp.broadcast_to(inv, scale.shape)
    out = norm * gain[0:1] + shift[0:1]
    first[...] = out
    cross_q[...] = (mm(out.astype(BF), w_qkvc[3]) + bias[3:4]).astype(BF)


def one_step(ops, picks):
    specs = []
    for i, op in enumerate(ops):
        block, at = op.shape, (0,) * op.ndim
        if i in picks:
            block, at = (None,) + op.shape[1:], (picks[i],) + at[1:]
        specs.append(pl.BlockSpec(block, lambda g, at=at: at))
    return specs


def self_fwd(tokens, seg, live, w_qkvc, mats, bias, gain, shift):
    toks, dim = tokens.shape
    ops = (tokens, seg.reshape(toks, 1), seg, live, w_qkvc, mats, bias, gain, shift)
    low = jax.ShapeDtypeStruct((toks, dim), BF)
    full = jax.ShapeDtypeStruct((toks, dim), F32)
    column = jax.ShapeDtypeStruct((toks, 128), F32)
    return pl.pallas_call(
        self_fwd_kernel,
        grid=(1,),
        in_specs=one_step(ops, {5: 2}),
        out_specs=one_step((low, low, low, low, full, full, column, low), {}),
        out_shape=(low, low, low, low, full, full, column, low),
        compiler_params=pltpu.CompilerParams(vmem_limit_bytes=28 * 1024 * 1024),
        cost_estimate=cost(5),
        name="self_fwd",
    )(*ops)


def self_bwd_kernel(*refs):
    grad_cq, grad_two, normed, scale, gain, queries, keys, values = refs[:8]
    seg_col, seg_row, live_row, w_qkvc, w_o = refs[8:13]
    grad_first, grad_one, grad_o, grad_q, grad_k, grad_v, grad_mix = refs[13:]
    incoming = grad_two[...] + mm_nt(grad_cq[...], w_qkvc[3])
    grad_first[...] = incoming
    one = norm_back(incoming, normed[...], scale[:, 0:1], gain[0:1])
    grad_one[...] = one
    low = one.astype(BF)
    grad_o[...] = low
    grad_mix[...] = mm_nt(low, w_o[...]).astype(BF)
    visible = visible_pairs(seg_col, seg_row, live_row)
    for pair in range(H // 2):
        lanes = slice(2 * HD * pair, 2 * HD * (pair + 1))
        by_query, by_key, by_value = 0.0, 0.0, 0.0
        for mask in head_masks():
            query, key = queries[:, lanes] * mask, keys[:, lanes] * mask
            grad = grad_mix[:, lanes] * mask
            prob = self_probs(query, key, visible)
            grad_p = mm_nt(grad, values[:, lanes])
            dot = jnp.sum(prob * grad_p, axis=-1, keepdims=True)
            grad_s = (prob * (grad_p - dot)).astype(BF)
            by_query = by_query + mm(grad_s, key)
            by_key = by_key + mm_tn(grad_s, query)
            by_value = by_value + mm_tn(prob.astype(BF), grad)
        grad_q[:, lanes] = (by_query * (HD**-0.5)).astype(BF)
        grad_k[:, lanes] = (by_key * (HD**-0.5)).astype(BF)
        grad_v[:, lanes] = by_value.astype(BF)


def self_bwd(grad_cq, grad_two, normed, scale, gain, qkv, seg, live, w_qkvc, mats):
    toks, dim = grad_two.shape
    ops = (grad_cq, grad_two, normed, scale, gain, *qkv)
    ops += (seg.reshape(toks, 1), seg, live, w_qkvc, mats)
    low = jax.ShapeDtypeStruct((toks, dim), BF)
    full = jax.ShapeDtypeStruct((toks, dim), F32)
    return pl.pallas_call(
        self_bwd_kernel,
        grid=(1,),
        in_specs=one_step(ops, {12: 2}),
        out_specs=one_step((full, full, low, low, low, low), {}),
        out_shape=(full, full, low, low, low, low),
        scratch_shapes=[pltpu.VMEM((toks, dim), BF)],
        compiler_params=pltpu.CompilerParams(vmem_limit_bytes=28 * 1024 * 1024),
        cost_estimate=cost(6),
        name="self_bwd",
    )(*ops)


def own_rows(tokens, ret, heads):
    shape = (heads * tokens, tokens * ret)
    row_tok = lax.broadcasted_iota(jnp.int32, shape, 0) % tokens
    col_tok = lax.broadcasted_iota(jnp.int32, shape, 1) // ret
    return row_tok == col_tok


def cross_fwd_kernel(qk, fetched, mix, probs, *, ret):
    heads, tokens, dim = qk.shape
    own = own_rows(tokens, ret, heads)
    query = qk[...].reshape(heads * tokens, dim)
    rows = fetched[...]
    scores = jnp.where(own, mm_nt(query, rows) * 0.125, -1e30)
    expo = jnp.exp(scores - jnp.max(scores, axis=-1, keepdims=True))
    prob = expo / jnp.sum(expo, axis=-1, keepdims=True)
    probs[0] = prob
    mix[...] = mm(prob.astype(BF), rows).astype(BF).reshape(heads, tokens, dim)


def cross_bwd_kernel(qk, gmix, fetched, probs, grad_rows, grad_s, *, ret):
    heads, tokens, dim = qk.shape
    query = qk[...].reshape(heads * tokens, dim)
    grad_mix = gmix[...].reshape(heads * tokens, dim)
    prob = probs[0]
    grad_p = mm_nt(grad_mix, fetched[...])
    g_s = (prob * (grad_p - jnp.sum(prob * grad_p, axis=-1, keepdims=True))).astype(BF)
    grad_s[0] = g_s
    grad_rows[...] = (
        mm_tn(prob.astype(BF), grad_mix) + mm_tn(g_s, query) * 0.125
    ).astype(BF)


def cross_back_q_kernel(grad_s, fetched, grad_qk):
    heads, tokens, dim = grad_qk.shape
    got = mm(grad_s[0], fetched[...]) * 0.125
    grad_qk[...] = got.astype(BF).reshape(heads, tokens, dim)


def cross_calls(tok_count, ret, dim):
    tb = 16
    blocks = tok_count // tb
    by_head = pl.BlockSpec((H, tb, dim), lambda g: (0, g, 0))
    rows = pl.BlockSpec((tb * ret, dim), lambda g: (g, 0))
    square = pl.BlockSpec((1, H * tb, tb * ret), lambda g: (g, 0, 0))
    heads_shape = jax.ShapeDtypeStruct((H, tok_count, dim), BF)
    square_f32 = jax.ShapeDtypeStruct((blocks, H * tb, tb * ret), F32)
    square_bf = jax.ShapeDtypeStruct((blocks, H * tb, tb * ret), BF)
    params = pltpu.CompilerParams(vmem_limit_bytes=VMEM_LIMIT)
    fwd = pl.pallas_call(
        functools.partial(cross_fwd_kernel, ret=ret),
        grid=(blocks,),
        in_specs=[by_head, rows],
        out_specs=[by_head, square],
        out_shape=(heads_shape, square_f32),
        compiler_params=params,
        name="cross_fwd",
    )
    bwd = pl.pallas_call(
        functools.partial(cross_bwd_kernel, ret=ret),
        grid=(blocks,),
        in_specs=[by_head, by_head, rows, square],
        out_specs=[rows, square],
        out_shape=(jax.ShapeDtypeStruct((tok_count * ret, dim), BF), square_bf),
        compiler_params=params,
        name="cross_bwd",
    )
    back_q = pl.pallas_call(
        cross_back_q_kernel,
        grid=(blocks,),
        in_specs=[square, rows],
        out_specs=by_head,
        out_shape=heads_shape,
        compiler_params=params,
        name="cross_back_q",
    )
    return fwd, bwd, back_q


GROUP = 8
LANES = 128
PITCH = LANES // GROUP
TILE = 256


def plan_kernel(rows, wanted, token, at_rank, owner, *, shard_rows):
    peers, slots = wanted.shape
    ret, toks = rows.shape
    shape = (toks, toks)
    upper = (
        lax.broadcasted_iota(jnp.int32, shape, 0) <= lax.broadcasted_iota(jnp.int32, shape, 1)
    ).astype(BF)
    peer = lax.broadcasted_iota(jnp.int32, (peers, toks), 0)
    tok_code = (lax.broadcasted_iota(jnp.int32, (peers, toks), 1) + 1).astype(F32)
    k_rows = lax.broadcasted_iota(jnp.int32, (at_rank.shape[0], toks), 0)
    shift = shard_rows.bit_length() - 1
    before = jnp.zeros((peers, 1), F32)
    codes = jnp.zeros((3 * peers, at_rank.shape[0]), F32)
    for r in range(ret):
        row = rows[r : r + 1, :]
        own = lax.shift_right_logical(row, shift)
        code = lax.bitwise_and(row, shard_rows - 1) + 1
        mine = own == peer
        upto = mm(mine.astype(BF), upper) + before
        before = upto[:, toks - 1 :]
        rank = jnp.sum(jnp.where(mine, upto, 0.0), axis=0, keepdims=True).astype(jnp.int32) - 1
        at = (k_rows == rank).astype(BF)
        at_rank[:, r * toks : (r + 1) * toks] = at
        owner[r : r + 1, :] = own
        high = lax.shift_right_logical(code, 6).astype(F32)
        low = lax.bitwise_and(code, 63).astype(F32)
        left = jnp.concatenate(
            [
                jnp.where(mine, high, 0.0).astype(BF),
                jnp.where(mine, low, 0.0).astype(BF),
                jnp.where(mine, tok_code, 0.0).astype(BF),
            ],
            axis=0,
        )
        codes = codes + mm_nt(left, at)
    codes = codes[:, :slots].astype(jnp.int32)
    wanted[...] = codes[:peers] * 64 + codes[peers : 2 * peers]
    token[...] = codes[2 * peers :]


def plan_slots(rows, shard_rows, peers, slots):
    ret, toks = rows.shape
    tall = -(-slots // LANES) * LANES
    return pl.pallas_call(
        functools.partial(plan_kernel, shard_rows=shard_rows),
        out_shape=(
            jax.ShapeDtypeStruct((peers, slots), jnp.int32),
            jax.ShapeDtypeStruct((peers, slots), jnp.int32),
            jax.ShapeDtypeStruct((tall, ret * toks), BF),
            jax.ShapeDtypeStruct((ret, toks), jnp.int32),
        ),
        cost_estimate=cost(4),
        name="plan",
    )(rows)


def head_sum(dim):
    shape = (dim, LANES)
    head = lax.broadcasted_iota(jnp.int32, shape, 0) // HD
    return (head == lax.broadcasted_iota(jnp.int32, shape, 1)).astype(BF)


def head_spread(dim):
    shape = (LANES, dim)
    head = lax.broadcasted_iota(jnp.int32, shape, 1) // HD
    return (head == lax.broadcasted_iota(jnp.int32, shape, 0)).astype(BF)


def to_lanes(by_peer, k):
    total = by_peer[:k]
    for q in range(1, GROUP):
        total = total + pltpu.roll(by_peer[q * k : (q + 1) * k], PITCH * q, 1)
    return total


def from_lanes(lanes):
    parts = [lanes] + [pltpu.roll(lanes, LANES - PITCH * q, 1) for q in range(1, GROUP)]
    return jnp.concatenate([part.astype(BF) for part in parts], axis=0)


def to_entries(slot_vals, at_rank, owner):
    k, wide = slot_vals.shape
    tall, toks = at_rank.shape[0], owner.shape[1]
    peers = wide // PITCH
    full = jnp.concatenate([slot_vals, jnp.zeros((tall - k, wide), F32)], axis=0).T
    high = full.astype(BF)
    low = (full - high.astype(F32)).astype(BF)
    peer = lax.broadcasted_iota(jnp.int32, (wide, toks), 0) // PITCH
    out = []
    for r in range(owner.shape[0]):
        at = at_rank[:, r * toks : (r + 1) * toks]
        got = mm(high, at) + mm(low, at)
        got = jnp.where(peer == owner[r : r + 1, :], got, 0.0)
        out.append(jnp.sum(got.reshape(peers, PITCH, toks), axis=0))
    return out


def to_slots(entry_vals, at_rank, owner, peers, slots):
    toks = owner.shape[1]
    wide = peers * PITCH
    peer = lax.broadcasted_iota(jnp.int32, (wide, toks), 0) // PITCH
    total = jnp.zeros((at_rank.shape[0], wide), F32)
    for r, vals in enumerate(entry_vals):
        tiled = jnp.concatenate([vals] * peers, axis=0)
        mine = jnp.where(peer == owner[r : r + 1, :], tiled, 0.0).astype(BF)
        total = total + mm_nt(at_rank[:, r * toks : (r + 1) * toks], mine)
    return total[:slots]


def token_marks_kernel(column, row, marks, marks_t):
    marks[...] = (
        column[...] == lax.broadcasted_iota(jnp.int32, marks.shape, 1) + 1
    ).astype(BF)
    marks_t[...] = (row[...] == lax.broadcasted_iota(jnp.int32, marks_t.shape, 0) + 1).astype(BF)


def query_rows_kernel(token, query, out):
    out[...] = mm(token[...], query[...]).astype(BF).reshape(out.shape)


def rows_in_kernel(arrived, query, w_k, w_v, keys, vals, scores):
    group, k, dim = arrived.shape
    rows = arrived[...].reshape(group * k, dim)
    total = jnp.zeros((group * k, LANES), F32)
    for at in range(0, dim, TILE):
        tile = slice(at, at + TILE)
        key = mm(rows, w_k[:, tile])
        keys[:, :, tile] = key.astype(BF).reshape(group, k, TILE)
        prod = (key * query[:, :, tile].reshape(group * k, TILE).astype(F32)).astype(BF)
        total = total + mm(prod, head_sum(dim)[tile])
        vals[:, :, tile] = mm(rows, w_v[:, tile]).astype(BF).reshape(group, k, TILE)
    scores[...] = to_lanes(total, k) * 0.125


def attend_kernel(
    scores, vals, token_t, at_rank, owner, bias, prob_tok, prob_slot, mixed, total
):
    step, part = pl.program_id(0), pl.program_id(1)
    k, dim = vals.shape[1:]
    slots, wide = scores.shape

    @pl.when((step == 0) & (part == 0))
    def _():
        entry = to_entries(scores[...], at_rank, owner)
        top = functools.reduce(jnp.maximum, entry)
        expo = [jnp.exp(part - top) for part in entry]
        norm = functools.reduce(jnp.add, expo)
        probs = [part / norm for part in expo]
        for r, part in enumerate(probs):
            prob_tok[r * PITCH : (r + 1) * PITCH, :] = part
        prob_slot[...] = to_slots(probs, at_rank, owner, wide // PITCH, slots)
        total[...] = jnp.zeros_like(total)

    lanes = pl.ds(pl.multiple_of(step * LANES, LANES), LANES)
    here = pl.ds(pl.multiple_of(part * k, 16), k)
    prob = mm(from_lanes(prob_slot[here, lanes]), head_spread(dim))
    prod = (prob * vals[...].reshape(-1, dim).astype(F32)).astype(BF)
    total[...] += mm(token_t[...], prod)

    @pl.when((step == pl.num_programs(0) - 1) & (part == pl.num_programs(1) - 1))
    def _():
        mixed[...] = (total[...] + bias[...]).astype(BF)


def attend_back_kernel(
    vals, token, grad, prob_tok, at_rank, owner, grads, grad_slot, slot_p
):
    step, part = pl.program_id(0), pl.program_id(1)
    k, dim = vals.shape[1:]
    slots, wide = slot_p.shape
    lanes = pl.ds(pl.multiple_of(step * LANES, LANES), LANES)
    here = pl.ds(pl.multiple_of(part * k, 16), k)
    rows = mm(token[...], grad[...])
    grads[...] = rows.astype(BF).reshape(vals.shape)
    prod = (rows * vals[...].reshape(-1, dim).astype(F32)).astype(BF)
    slot_p[here, lanes] = to_lanes(mm(prod, head_sum(dim)), k)

    @pl.when((step == pl.num_programs(0) - 1) & (part == pl.num_programs(1) - 1))
    def _():
        entry = to_entries(slot_p[...], at_rank, owner)
        probs = [prob_tok[r * PITCH : (r + 1) * PITCH, :] for r in range(len(entry))]
        dots = functools.reduce(jnp.add, [p * g for p, g in zip(probs, entry)])
        scores = [(p * (g - dots)).astype(BF).astype(F32) for p, g in zip(probs, entry)]
        grad_slot[...] = to_slots(scores, at_rank, owner, wide // PITCH, slots)


def weigh(prob_slot, grad_slot, grad, query):
    dim = grad.shape[2]
    spread = head_spread(dim)
    prob = mm(from_lanes(prob_slot[...]), spread)
    mix = (prob * grad[...].reshape(-1, dim).astype(F32)).astype(BF)
    score = mm(from_lanes(grad_slot[...]), spread) * 0.125
    return mix, (score * query[...].reshape(-1, dim).astype(F32)).astype(BF)


def rows_out_kernel(prob_slot, grad_slot, grad, query, w_k, w_v, *refs):
    out, flag = refs[-2:]
    mix, ask = weigh(prob_slot, grad_slot, grad, query)
    out[...] = (mm_nt(mix, w_v[...]) + mm_nt(ask, w_k[...])).astype(BF).reshape(grad.shape)
    flag[...] = jnp.zeros_like(flag)


def rows_weights_kernel(*refs):
    prob_slot, grad_slot, grad, query, rows = refs[:5]
    by_key, by_value, key_sum, value_sum = refs[-4:]
    step, part = pl.program_id(0), pl.program_id(1)

    @pl.when((step == 0) & (part == 0))
    def _():
        key_sum[...] = jnp.zeros_like(key_sum)
        value_sum[...] = jnp.zeros_like(value_sum)

    mix, ask = weigh(prob_slot, grad_slot, grad, query)
    left = rows[...].reshape(mix.shape)
    key_sum[...] += mm_tn(left, ask)
    value_sum[...] += mm_tn(left, mix)

    @pl.when((step == pl.num_programs(0) - 1) & (part == pl.num_programs(1) - 1))
    def _():
        by_key[...] = key_sum[...].astype(BF)
        by_value[...] = value_sum[...].astype(BF)


def query_back_kernel(keys, token_t, grad_slot, waited, out, total):
    del waited
    step, part = pl.program_id(0), pl.program_id(1)
    k, dim = keys.shape[1:]

    @pl.when((step == 0) & (part == 0))
    def _():
        total[...] = jnp.zeros_like(total)

    score = mm(from_lanes(grad_slot[...]), head_spread(dim)) * 0.125
    prod = (score * keys[...].reshape(-1, dim).astype(F32)).astype(BF)
    total[...] += mm(token_t[...], prod)

    @pl.when((step == pl.num_programs(0) - 1) & (part == pl.num_programs(1) - 1))
    def _():
        out[...] = total[...].astype(BF)


def vector_sums_kernel(*refs, plain, pairs):
    ops, (wide, out, out_wide) = refs[: plain + 2 * pairs], refs[plain + 2 * pairs :]
    rows = [ops[i][...].astype(F32) for i in range(plain)]
    lefts = [ops[plain + 2 * i][...].astype(F32) for i in range(pairs)]
    rows += [lefts[i] * ops[plain + 2 * i + 1][...] for i in range(pairs)]
    rows += lefts
    sums = [jnp.sum(row, axis=0, keepdims=True) for row in rows]
    sums.append(jnp.zeros((out.shape[0] - len(sums), out.shape[1]), F32))
    out[...] = jnp.concatenate(sums, axis=0)
    out_wide[...] = jnp.sum(wide[...].astype(F32), axis=0, keepdims=True)


def vector_sums(plain, pairs, wide):
    ops = list(plain) + [x for pair in pairs for x in pair] + [wide]
    dim = plain[0].shape[1]
    return pl.pallas_call(
        functools.partial(vector_sums_kernel, plain=len(plain), pairs=len(pairs)),
        out_shape=(
            jax.ShapeDtypeStruct((16, dim), F32),
            jax.ShapeDtypeStruct((1, wide.shape[1]), F32),
        ),
        compiler_params=pltpu.CompilerParams(vmem_limit_bytes=24 * 1024 * 1024),
        cost_estimate=cost(2),
        name="vector_sums",
    )(*ops)


class SlotAttention:
    split = 1

    def __init__(self, ret_rows, shard_rows, peers, slots, dim):
        self.toks, self.ret = ret_rows.shape
        self.peers, self.slots, self.dim = peers, slots, dim
        self.k = slots // self.split
        self.wanted, token, self.at_rank, self.owner = plan_slots(
            ret_rows.T, shard_rows, peers, slots
        )
        k, dim, toks = self.k, self.dim, self.toks
        groups, wide = peers // GROUP, peers * PITCH
        self.grid = (groups, self.split)
        self.rows = pl.BlockSpec((GROUP, k, dim), lambda g, c: (g, c, 0))
        self.lanes = pl.BlockSpec((k, LANES), lambda g, c: (c, g))
        self.mark = pl.BlockSpec((GROUP * k, toks), lambda g, c: (c * groups + g, 0))
        self.mark_t = pl.BlockSpec((toks, GROUP * k), lambda g, c: (0, c * groups + g))
        self.square = self.whole(dim, dim)
        self.w_specs = [pl.BlockSpec((None, dim, dim), lambda g, c, i=i: (i, 0, 0)) for i in range(2)]
        self.heads = self.whole(slots, wide)
        self.slot_rows = in_hbm((peers, slots, dim), BF)
        self.slot_heads = jax.ShapeDtypeStruct((slots, wide), F32)
        token = token.reshape(peers, self.split, k).transpose(1, 0, 2)
        self.token, self.token_t = self.call(
            token_marks_kernel,
            "token_marks",
            5,
            [
                pl.BlockSpec((GROUP * k, 1), lambda g, c: (c * groups + g, 0)),
                pl.BlockSpec((1, GROUP * k), lambda g, c: (0, c * groups + g)),
            ],
            [self.mark, self.mark_t],
            (in_hbm((peers * slots, toks), BF), in_hbm((toks, peers * slots), BF)),
        )(token.reshape(-1, 1), token.reshape(1, -1))

    @staticmethod
    def whole(*shape):
        return pl.BlockSpec(shape, lambda g, c: (0,) * len(shape))

    def call(self, kernel, name, micros, in_specs, out_specs, out_shape, scratch=(), mib=44):
        return pl.pallas_call(
            kernel,
            grid=self.grid,
            in_specs=in_specs,
            out_specs=out_specs,
            out_shape=out_shape,
            scratch_shapes=list(scratch),
            compiler_params=pltpu.CompilerParams(vmem_limit_bytes=mib * 1024 * 1024),
            cost_estimate=cost(micros),
            name=name,
        )

    def prepare(self, cross_q):
        self.query = self.call(
            query_rows_kernel,
            "query_rows",
            7,
            [self.mark, self.whole(self.toks, self.dim)],
            self.rows,
            self.slot_rows,
        )(self.token, cross_q)

    def forward(self, arrived, mats, bias):
        dim, toks = self.dim, self.toks
        self.arrived, self.mats = arrived, mats
        self.keys, self.vals, scores = self.call(
            rows_in_kernel,
            "rows_in",
            22,
            [self.rows, self.rows, *self.w_specs],
            [self.rows, self.rows, self.lanes],
            (self.slot_rows, self.slot_rows, self.slot_heads),
        )(from_hbm(arrived), from_hbm(self.query), mats, mats)
        entries = (self.ret * PITCH, toks)
        self.prob_tok, self.prob_slot, mixed = self.call(
            attend_kernel,
            "attend",
            11,
            [self.heads, self.rows, self.mark_t]
            + [self.whole(*self.at_rank.shape), self.whole(*self.owner.shape), self.whole(1, dim)],
            [self.whole(*entries), self.heads, self.whole(toks, dim)],
            (
                jax.ShapeDtypeStruct(entries, F32),
                self.slot_heads,
                jax.ShapeDtypeStruct((toks, dim), BF),
            ),
            [pltpu.VMEM((toks, dim), F32)],
        )(scores, from_hbm(self.vals), self.token_t, self.at_rank, self.owner, bias.reshape(1, dim))
        return mixed

    def backward(self, grad):
        dim, toks = self.dim, self.toks
        grads, self.grad_slot = self.call(
            attend_back_kernel,
            "attend_back",
            13,
            [self.rows, self.mark, self.whole(toks, dim), self.whole(self.ret * PITCH, toks)]
            + [self.whole(*self.at_rank.shape), self.whole(*self.owner.shape)],
            [self.rows, self.heads],
            (self.slot_rows, self.slot_heads),
            [pltpu.VMEM(self.slot_heads.shape, F32)],
        )(from_hbm(self.vals), self.token, grad, self.prob_tok, self.at_rank, self.owner)
        self.factors = (self.prob_slot, self.grad_slot, from_hbm(grads), from_hbm(self.query))
        self.factor_specs = [self.lanes, self.lanes, self.rows, self.rows]
        return [self.send(0), self.send(1)]

    def send(self, part):
        k = self.slots // 2
        some = pl.BlockSpec((GROUP, k, self.dim), lambda g, c: (g, part, 0))
        lanes = pl.BlockSpec((k, LANES), lambda g, c: (part, g))
        before = [self.flag] if part else []
        sent, self.flag = self.call(
            rows_out_kernel,
            "rows_out",
            14,
            [lanes, lanes, some, some] + self.w_specs + [self.whole(8, LANES)] * part,
            [pl.BlockSpec((GROUP, k, self.dim), lambda g, c: (g, 0, 0)), self.whole(8, LANES)],
            (
                in_hbm((self.peers, k, self.dim), BF),
                jax.ShapeDtypeStruct((8, LANES), F32),
            ),
        )(*self.factors, self.mats, self.mats, *before)
        return sent

    def query_grad(self):
        dim, toks = self.dim, self.toks
        return self.call(
            query_back_kernel,
            "query_back",
            7,
            [self.rows, self.mark_t, self.lanes, self.whole(8, LANES)],
            self.whole(toks, dim),
            jax.ShapeDtypeStruct((toks, dim), BF),
            [pltpu.VMEM((toks, dim), F32)],
        )(from_hbm(self.keys), self.token_t, self.grad_slot, self.flag)

    def weights(self, after):
        square = (self.dim, self.dim)
        return self.call(
            rows_weights_kernel,
            "rows_weights",
            24,
            self.factor_specs + [self.rows] + [WAIT] * len(after),
            [self.square, self.square],
            (jax.ShapeDtypeStruct(square, BF), jax.ShapeDtypeStruct(square, BF)),
            [pltpu.VMEM(square, F32), pltpu.VMEM(square, F32)],
        )(*self.factors, from_hbm(self.arrived), *after)


class GatheredAttention:
    def __init__(self, ret_rows, shard_rows, peers, slots, dim):
        self.toks, self.ret = ret_rows.shape
        self.dim, self.slots = dim, slots
        self.place, self.wanted, self.entry = plan_requests(ret_rows, shard_rows, peers, slots)
        self.fwd, self.bwd, self.back_q = cross_calls(self.toks, self.ret, dim)

    def prepare(self, cross_q):
        self.cross_q = cross_q

    def forward(self, arrived, mats, bias):
        toks, dim = self.toks, self.dim
        w_k, w_v = mats[0], mats[1]
        self.key_heads, self.val_heads = w_k.reshape(dim, H, HD), w_v.reshape(dim, H, HD)
        query = self.cross_q.reshape(toks, H, HD)
        self.query_keys = jnp.einsum(
            "the,dhe->htd", query, self.key_heads, preferred_element_type=F32
        ).astype(BF)
        self.fetched = arrived.reshape(-1, dim)[self.place]
        self.state_mix, self.cross_p = self.fwd(self.query_keys, self.fetched)
        mixed = jnp.einsum(
            "htd,dhe->the", self.state_mix, self.val_heads, preferred_element_type=F32
        )
        return (mixed.reshape(toks, dim) + bias).astype(BF)

    def backward(self, grad):
        self.grad = grad.reshape(self.toks, H, HD)
        grad_mix = jnp.einsum(
            "the,dhe->htd", self.grad, self.val_heads, preferred_element_type=F32
        ).astype(BF)
        rows, self.grad_s = self.bwd(self.query_keys, grad_mix, self.fetched, self.cross_p)
        return [rows[self.entry]]

    def query_grad(self):
        self.grad_qk = self.back_q(self.grad_s, self.fetched)
        grad_q = jnp.einsum(
            "htd,dhe->the", self.grad_qk, self.key_heads, preferred_element_type=F32
        )
        return grad_q.reshape(self.toks, self.dim).astype(BF)

    def weights(self, after):
        def product(left, right):
            got = jnp.einsum("htd,the->dhe", left, right, preferred_element_type=F32)
            return got.reshape(self.dim, self.dim).astype(BF)

        grad_k = product(self.grad_qk, self.cross_q.reshape(self.toks, H, HD))
        return grad_k, product(self.state_mix, self.grad)


def store_sum_kernel(asked, returned, *refs, block, skip, added):
    first = (pl.program_id(0) + skip) * block + 1
    shape = (block, asked.shape[1])
    hit = lax.broadcasted_iota(jnp.int32, shape, 0) + first == asked[...]
    total = mm(hit.astype(BF), returned[...])
    refs[-1][...] = total + refs[0][...] if added else total


def store_sum(asked, returned, shard_rows, so_far=(), rows=(0, 1), after=()):
    count, dim = returned.shape
    block = 256
    part, parts = rows
    steps = shard_rows // block // parts
    skip = part * steps
    here = pl.BlockSpec((block, dim), lambda g: (g + skip, 0))
    return pl.pallas_call(
        functools.partial(store_sum_kernel, block=block, skip=skip, added=bool(so_far)),
        grid=(steps,),
        in_specs=[
            pl.BlockSpec((1, count), lambda g: (0, 0)),
            pl.BlockSpec((count, dim), lambda g: (0, 0)),
        ]
        + [here] * len(so_far)
        + [WAIT] * len(after),
        out_specs=here,
        out_shape=in_hbm((shard_rows, dim), F32),
        input_output_aliases={2: 0} if so_far else {},
        compiler_params=pltpu.CompilerParams(vmem_limit_bytes=VMEM_LIMIT),
        cost_estimate=cost(13 if parts == 1 else 8),
        name="store_sum",
    )(asked.reshape(1, count), returned, *so_far, *after)


def all_to_all(array):
    return lax.all_to_all(array, RANKS, split_axis=0, concat_axis=0, tiled=True)


def on_device(
    tokens,
    seg_ids,
    live_mask,
    ret_rows,
    enc_store,
    attn_in,
    attn_out,
    ff_in,
    ff_out,
    biases,
    ln_gain,
    ln_shift,
    ff_bias,
    cotangent,
):
    n_rows = lax.axis_size("row")
    n_cols = lax.axis_size("col")
    peers = n_rows * n_cols
    tok_count, dim = tokens.shape
    shard_rows = enc_store.shape[0]
    ret = ret_rows.shape[1]
    slots = 3 * ret_rows.size // (2 * peers)
    rb, cb = attn_in.shape[1], attn_in.shape[2]
    order_a, order_b = bit_orders(n_rows, n_cols)
    n_row_bits = n_rows.bit_length() - 1
    n_far = n_row_bits - 2
    by_rows = n_cols == 2 and rb % 16 == 0 and cb % 128 == 0
    orders = (order_a, order_b, order_a, order_b)
    shapes = ((rb, cb), (rb, cb), (rb, 4 * cb), (4 * rb, cb))
    counts = (4, 4, 1, 1)
    if by_rows:
        col = lax.axis_index("col").astype(jnp.int32)[None]
        place_a = jnp.concatenate([block_of_row(order_a, n_rows), col])
        place_b = jnp.concatenate([block_of_row(order_b, n_rows), col])
        places = (place_a, place_b, place_a, place_b)

    in_slots = (
        by_rows
        and slots % (16 * SlotAttention.split) == 0
        and peers % GROUP == 0
        and tok_count % LANES == 0
        and tok_count <= 256
        and shard_rows & (shard_rows - 1) == 0
        and H <= PITCH
    )
    attention = (SlotAttention if in_slots else GatheredAttention)(
        ret_rows, shard_rows, peers, slots, dim
    )

    def vector_rows(parts):
        parts = [jnp.pad(part, ((0, 0), (0, cb - part.shape[1]))) for part in parts]
        return jnp.pad(jnp.concatenate(parts, axis=0), ((0, 2), (0, 0)))

    small = vector_rows([biases, ln_gain, ln_shift, ff_bias.reshape(1, -1)])
    packs = [*join(attn_in, attn_out, small, attention.wanted), ff_in[None], ff_out[None]]
    packs = [gather_bits(p, order[:1]) for p, order in zip(packs, orders)]
    asked = all_to_all(attention.wanted)
    asked = tie(asked, packs[:2]) if by_rows else asked
    packs = [gather_bits(p, order[1:n_far]) for p, order in zip(packs, orders)]

    answer = enc_store[jnp.maximum(asked - 1, 0)]
    for i in range(2):
        packs[i] = gather_bits(packs[i], orders[i][n_far : n_far + 1])
    arrived = all_to_all(hold(answer, packs) if by_rows else answer)
    if in_slots:
        packs[0] = hold(packs[0], [attention.token, attention.token_t])
    extras = (0, small.shape[0], 0, 0)

    def whole(i, after=()):
        done = n_far + 1
        if by_rows:
            got = swap_bit(packs[i], *orders[i][done])
            own = hold(packs[i], after) if after else packs[i]
            own = jnp.concatenate([own, got], axis=0)
            other = swap_bit(own, "col", 1)
            return unpack(own, other, places[i], counts[i], shapes[i], extras[i])
        blocks = gather_bits(packs[i], orders[i][done:])
        return unpack_any(blocks, orders[i], counts[i], shapes[i], extras[i], n_rows, n_cols)

    mats = [whole(0), whole(1)]
    w_q, w_k, w_v = (mats[0][i] for i in range(3))
    w_co = mats[1][0][3]
    small_all = mats[1][1]
    small_all = small_all.astype(F32)
    vectors = small_all[:, :13, :rb].transpose(1, 0, 2).reshape(13, dim)
    bias_all, gain_all, shift_all = vectors[:7], vectors[7:10], vectors[10:]
    bias_ff = small_all[:, 13, : ff_bias.size].reshape(-1)

    *qkv, mixed, first, first_norm, first_scale, cross_q = self_fwd(
        tokens, seg_ids, live_mask, mats[0], mats[1][0], bias_all, gain_all, shift_all
    )
    first_low = first.astype(BF)

    attention.prepare(cross_q)
    if in_slots:
        for i in (2, 3):
            packs[i] = gather_bits(packs[i], orders[i][n_far : n_far + 1])
    else:
        for i in (2, 3):
            packs[i] = gather_bits(packs[i], orders[i][n_far : n_far + 1])
    cross_low = attention.forward(arrived, mats[1][0], bias_all[4])
    branch_two = mm(cross_low, w_co) + bias_all[5]
    second, second_norm, second_scale = norm_fwd(first + branch_two, gain_all[1], shift_all[1])
    second_low = second.astype(BF)

    after = [attention.query] if in_slots else []
    w_ff1, w_ff2 = whole(2, after)[0], whole(3, after)[0]
    hidden_act, hidden_slope = gelu_parts(mm(second_low, w_ff1) + bias_ff)
    hidden_low = hidden_act.astype(BF)
    branch_ffn = mm(hidden_low, w_ff2) + bias_all[6]
    final, final_norm, final_scale = norm_fwd(second + branch_ffn, gain_all[2], shift_all[2])
    output = final.astype(BF)
    cot = cotangent.astype(F32)
    grad_three = norm_back(cot, final_norm, final_scale, gain_all[2])
    grad_y = grad_three.astype(BF)
    grad_pre = (mm_nt(grad_y, w_ff2) * hidden_slope).astype(BF)
    grad_second = grad_three + mm_nt(grad_pre, w_ff1)
    grad_two = norm_back(grad_second, second_norm, second_scale, gain_all[1])
    grad_o2 = grad_two.astype(BF)
    grad_cmix = mm_nt(grad_o2, w_co).astype(BF)
    send_back = attention.backward(grad_cmix)
    returned = [all_to_all(send_back[0])]

    def packed(order, place, mats, small=None, after=()):
        if by_rows:
            return pack(mats, place, small, after)
        return pack_any(mats, order[::-1], small, n_rows, n_cols)

    def on_both(pairs, start, stop):
        return [
            scatter_bits(*pair, back[start:stop]) for pair, back in zip(pairs, (back_a, back_b))
        ]

    tile = (rb, cb)
    near = len(order_a) - n_far
    back_a, back_b = order_a[::-1], order_b[::-1]
    at_a, at_b = (place_a, place_b) if by_rows else (None, None)
    grad_cq = attention.query_grad()
    ff = [
        (order_a, at_a, [((second_low, grad_pre), tile, 4)]),
        (order_b, at_b, [((hidden_low, grad_y), (4 * rb, cb), 1)]),
    ]
    ff = [packed(*part, None, [grad_cq]) for part in ff]
    if by_rows:
        grad_cq = hold(grad_cq, [x for pair in ff for x in pair])
    grad_first, grad_one, grad_o, grad_q, grad_k, grad_v = self_bwd(
        grad_cq,
        grad_two,
        first_norm,
        first_scale,
        gain_all,
        qkv,
        seg_ids,
        live_mask,
        mats[0],
        mats[1][0],
    )
    grad_tokens = (
        grad_one + mm_nt(grad_q, w_q) + mm_nt(grad_k, w_k) + mm_nt(grad_v, w_v)
    )

    vectors, wide = vector_sums(
        [grad_q, grad_v, grad_o, grad_cq, grad_cmix, grad_o2, grad_y],
        [(grad_first, first_norm), (grad_second, second_norm), (cotangent, final_norm)],
        grad_pre,
    )
    vectors = vectors[:13].reshape(13, n_rows, rb).transpose(1, 0, 2)
    wide = wide.reshape(n_rows, 1, -1)
    grad_small = [
        jnp.pad(vectors, ((0, 0), (0, 0), (0, cb - rb))),
        jnp.pad(wide, ((0, 0), (0, 2), (0, cb - ff_bias.size))),
    ]
    grad_small = jnp.concatenate(grad_small, axis=1).astype(BF)
    attn_one = packed(
        order_a,
        at_a,
        [
            ((tokens, grad_q), tile, 1),
            ((tokens, grad_k), tile, 1),
            ((tokens, grad_v), tile, 1),
            ((first_low, grad_cq), tile, 1),
        ],
    )
    ff = on_both(ff, 0, near - 2)
    before = [*attn_one, ff[0][1], ff[1][1]] if in_slots else []
    grad_wk, grad_wv = attention.weights(before)
    attn_two = packed(
        order_b,
        at_b,
        [
            (grad_wk, tile, 1),
            (grad_wv, tile, 1),
            ((mixed, grad_o), tile, 1),
            ((cross_low, grad_o2), tile, 1),
        ],
        grad_small,
    )
    ff = on_both(ff, near - 2, near - 1)
    if len(send_back) > 1:
        attn_one = scatter_bits(*attn_one, back_a[: near - 2])
    for part in send_back[1:]:
        before = [*returned, *attn_two, *attn_one, *ff[0], *ff[1]]
        returned.append(all_to_all(hold(part, before)))

    def join_pairs(pairs):
        return tuple(jnp.concatenate(both, axis=1) for both in zip(*pairs))

    if len(send_back) > 1:
        attn_two = scatter_bits(*attn_two, back_b[: near - 2])
        attn = on_both([attn_one, attn_two], near - 2, near - 1)
    else:
        attn = on_both([attn_one, attn_two], 0, near - 1)

    def behind(pair, array):
        return (hold(pair[0], [array]), pair[1]) if by_rows else pair

    size = asked.shape[1] // len(returned)
    lists = [
        (asked[:, i * size : (i + 1) * size], rows.reshape(-1, dim), shard_rows)
        for i, rows in enumerate(returned)
    ]
    so_far = ()
    for args in lists[:-1]:
        so_far = (store_sum(*args),)
        ff = [behind(pair, so_far[0]) for pair in ff]
        attn = [behind(pair, so_far[0]) for pair in attn]
    ff = join_pairs(on_both(ff, near - 1, near))
    attn = join_pairs(on_both(attn, near - 1, near))
    grad_store = store_sum(*lists[-1], so_far, (0, 2)) if so_far else None
    if so_far:
        ff, attn = behind(ff, grad_store), behind(attn, grad_store)
    ff, attn = (scatter_bits(*x, back_a[near:-1]) for x in (ff, attn))
    last = join_pairs([attn, ff])
    if so_far:
        grad_store = store_sum(*lists[-1], (grad_store,), (1, 2), (last[1],))
        keep, send = behind(last, grad_store)
    else:
        grad_store = store_sum(*lists[-1])
        keep, send = last
    total = (keep + swap_bit(send, *order_a[0]))[0].astype(F32)
    total_a, total_b = total[: attn[0].shape[1]], total[attn[0].shape[1] :]

    sum_small = total_a[8 * rb :]
    return (
        output,
        grad_tokens,
        grad_store,
        total_a[: 6 * rb].reshape(6, rb, cb),
        total_a[6 * rb : 8 * rb].reshape(2, rb, cb),
        jnp.concatenate([total_b[k * rb : (k + 1) * rb] for k in range(4)], axis=1),
        total_b[4 * rb :],
        sum_small[:7, :rb],
        sum_small[7:10, :rb],
        sum_small[10:13, :rb],
        sum_small[13, : ff_bias.size],
    )


def solution(mesh):
    both = ("row", "col")
    return jax.shard_map(
        on_device,
        mesh=mesh,
        in_specs=(
            P(both, None),
            P(both, None),
            P(both, None),
            P(both, None),
            P(both, None),
            P(None, "row", "col"),
            P(None, "row", "col"),
            P("row", "col"),
            P("row", "col"),
            P(None, "row"),
            P(None, "row"),
            P(None, "row"),
            P("row"),
            P(both, None),
        ),
        out_specs=(
            P(both, None),
            P(both, None),
            P(both, None),
            P(None, "row", "col"),
            P(None, "row", "col"),
            P("row", "col"),
            P("row", "col"),
            P(None, "row"),
            P(None, "row"),
            P(None, "row"),
            P("row"),
        ),
        check_vma=False,
    )
```
